512 devices in a mesh: dp: 64 (over y, x, z_hi), shard: 8 (over z_lo, core).
Axes of the slice: x: 4, y: 8, z: 8 (z_hi: 2, z_lo: 4; z = z_hi * 4 + z_lo), core: 2. Of those that a mesh axis runs over, the one named last changes fastest.
Arguments:
- hidden: bfloat16 [8192, 14336], P('dp', 'shard'), may hold values from -6 to 6
- out_grad: bfloat16 [8192, 4096], P('dp', 'shard'), may hold values from -6 to 6
- block_weight: bfloat16 [8, 32, 128, 128], P('shard'), may hold values from -0.1875 to 0.1875
- block_row: int32 [8, 32], replicated, may hold values from 0 to 111, as said below
- block_col: int32 [8, 32], replicated, may hold values from 0 to 31
- live_count: int32 [8], replicated, may hold values from 16 to 32, as said below
- new_owner: int32 [8, 32], replicated, may hold values from -1 to 7, as said below
- new_slot: int32 [8, 32], replicated, may hold values from 0 to 31, as said below
- first_moment: float32 [8, 32, 16384], P('shard', None, 'dp'), may hold values from -3 to 3
- second_moment: float32 [8, 32, 16384], P('shard', None, 'dp'), may hold values from 0.05 to 2
Outputs:
- projected: bfloat16 [8192, 4096], P('dp', 'shard')
- hidden_grad: bfloat16 [8192, 14336], P('dp', 'shard')
- new_weight: float32 [8, 32, 16384], P('shard', None, 'dp')
- new_first: float32 [8, 32, 16384], P('shard', None, 'dp')
- new_second: float32 [8, 32, 16384], P('shard', None, 'dp')
The draws below stay inside these ranges and needn't reach their ends.
Inputs may be any that keep to these rules, and one draw needn't show every extreme that they name: `block_row`: together with block_col, each slot's block place; no two slots of all shards share a place. `live_count`: some shard has all 32 slots live. `new_owner`: -1 for slots that are not live and for dropped blocks. At most 2 blocks of one shard go to one other shard; in every draw some shard receives exactly 2 from every other shard. `new_slot`: no two blocks with new_owner >= 0 share an owner and a slot; 0 where new_owner is -1.
All inputs are finite; a program needn't handle non-finite values.
Results may differ from the reference program's by a relative error of at most 0.004.
Values may be sent and summed in bfloat16 or wider, within the bound.
No kernel may reach another device: no remote copies, remote signals or barrier semaphores. Data moves between devices by JAX's collectives and lax.ppermute only.
A program may use at most 64 MiB of HBM per device.

```python
import math
import jax
import jax.numpy as jnp
from jax import lax

D = 4096
FF = 14336
BS = 128
KB = 32
MV = 2
TOKENS = 8192
N_SHARD = 8


def migration_plan(key):
    row_blocks = FF // BS
    col_blocks = D // BS
    subkeys = jax.random.split(key, 8)
    block_ids = jax.random.permutation(subkeys[0], row_blocks * col_blocks)[:N_SHARD * KB].reshape(N_SHARD, KB).astype(jnp.int32)
    block_rows = (block_ids // col_blocks).astype(jnp.int32)
    block_cols = (block_ids % col_blocks).astype(jnp.int32)
    shard_ids = jnp.arange(N_SHARD, dtype=jnp.int32)
    slot_ids = jnp.arange(KB, dtype=jnp.int32)
    live_counts = jax.random.randint(subkeys[1], (N_SHARD,), KB // 2, KB + 1)
    fullest = jax.random.randint(subkeys[2], (), 0, N_SHARD)
    live_counts = jnp.where(shard_ids == fullest, KB, live_counts).astype(jnp.int32)
    is_live = slot_ids[None, :] < live_counts[:, None]
    scores = jax.random.randint(subkeys[3], (N_SHARD, KB), 0, 1 << 20) * KB + slot_ids[None, :]
    scores = jnp.where(is_live, scores, (1 << 29) + slot_ids[None, :])
    slot_ranks = jnp.argsort(jnp.argsort(scores, axis=1), axis=1).astype(jnp.int32)
    move_limit = jnp.minimum(live_counts // 2, (N_SHARD - 1) * MV)
    candidate = slot_ranks < move_limit[:, None]
    offsets = jax.random.randint(subkeys[4], (N_SHARD, KB), 1, N_SHARD)
    receiver = jax.random.randint(subkeys[5], (), 0, N_SHARD)
    forced = (shard_ids[:, None] != receiver) & (slot_ranks < MV)
    offsets = jnp.where(forced, (receiver - shard_ids[:, None]) % N_SHARD, offsets)
    destinations = ((shard_ids[:, None] + offsets) % N_SHARD).astype(jnp.int32)
    earlier = (destinations[:, :, None] == destinations[:, None, :]) & candidate[:, None, :] & (slot_ranks[:, None, :] < slot_ranks[:, :, None])
    positions = jnp.sum(earlier, axis=2).astype(jnp.int32)
    relocating_blocks = candidate & (positions < MV)
    to_dest = relocating_blocks[:, :, None] & (destinations[:, :, None] == shard_ids[None, None, :])
    per_source = jnp.sum(to_dest, axis=1).astype(jnp.int32)
    arrivals = jnp.sum(per_source, axis=0)
    before = jnp.cumsum(per_source, axis=0) - per_source
    survive = is_live & ~relocating_blocks & (jax.random.randint(subkeys[6], (N_SHARD, KB), 0, 8) != 0)
    stay_ranks = jnp.sum(survive[:, None, :] & (slot_ranks[:, None, :] < slot_ranks[:, :, None]), axis=2).astype(jnp.int32)
    resident_blocks = survive & (stay_ranks < (KB - arrivals)[:, None])
    kept_count = jnp.sum(resident_blocks, axis=1).astype(jnp.int32)
    arrival_index = kept_count[destinations] + before[shard_ids[:, None], destinations] + positions
    places = jnp.where(resident_blocks, stay_ranks, arrival_index)
    owner_devices = jnp.where(resident_blocks, shard_ids[:, None], destinations)
    perm_scores = jax.random.randint(subkeys[7], (N_SHARD, KB), 0, 1 << 20) * KB + slot_ids[None, :]
    slot_perm = jnp.argsort(perm_scores, axis=1).astype(jnp.int32)
    destination_slot_list = slot_perm[owner_devices, jnp.clip(places, 0, KB - 1)]
    surviving_blocks = resident_blocks | relocating_blocks
    resulting_owner = jnp.where(surviving_blocks, owner_devices, -1).astype(jnp.int32)
    resulting_slot = jnp.where(surviving_blocks, destination_slot_list, 0).astype(jnp.int32)
    return (block_rows, block_cols, live_counts, resulting_owner, resulting_slot)


def draw_block_row(key, part):
    plan = migration_plan(key)
    return plan[0]


def draw_block_col(key, part):
    plan = migration_plan(key)
    return plan[1]


def draw_live_count(key, part):
    plan = migration_plan(key)
    return plan[2]


def draw_new_owner(key, part):
    plan = migration_plan(key)
    return plan[3]


def draw_new_slot(key, part):
    plan = migration_plan(key)
    return plan[4]


def block_scale(stream_key, extent, pieces, smallest, largest):
    def one(dim, blocks):
        heights = jax.random.uniform(jax.random.fold_in(jax.random.fold_in(stream_key, 6), dim), (blocks,), jnp.float32, smallest / len(pieces), largest / len(pieces))
        return jnp.repeat(jnp.exp(heights), extent[dim] // blocks).reshape((-1,) + (1,) * (len(extent) - dim - 1))

    level = one(*pieces[0])
    for cut in pieces[1:]:
        level = level * one(*cut)
    return level


def normal_values(rng, extent, scale, limit, pieces=(), kind=jnp.bfloat16):
    drawn = scale * jax.random.normal(rng, extent, jnp.float32)
    if pieces:
        drawn = drawn * block_scale(rng, extent, pieces, -0.22, 0.18)
    return jnp.clip(drawn, -limit, limit).astype(kind)


def setup_inputs(seed: int = 0) -> dict:
    key_list = jax.random.split(jax.random.key(seed), 11)
    return {
        "hidden": normal_values(key_list[0], (TOKENS, FF), 1.0, 6.0, ((0, 64), (1, 8))),
        "out_grad": normal_values(key_list[1], (TOKENS, D), 1.0, 6.0, ((0, 64), (1, 8))),
        "block_weight": normal_values(key_list[2], (N_SHARD, KB, BS, BS), (N_SHARD * KB * BS * BS // D) ** -0.5, 0.1875, ((0, 8),)),
        "block_row": draw_block_row(jax.random.fold_in(key_list[10], 71), 0),
        "block_col": draw_block_col(jax.random.fold_in(key_list[10], 71), 0),
        "live_count": draw_live_count(jax.random.fold_in(key_list[10], 71), 0),
        "new_owner": draw_new_owner(jax.random.fold_in(key_list[10], 71), 0),
        "new_slot": draw_new_slot(jax.random.fold_in(key_list[10], 71), 0),
        "first_moment": normal_values(key_list[8], (N_SHARD, KB, BS * BS), 0.5, 3.0, ((0, 8), (2, 64)), jnp.float32),
        "second_moment": jnp.clip(jnp.exp(math.log(2.0) - 3.6888794 * jax.random.uniform(key_list[9], (N_SHARD, KB, BS * BS), jnp.float32) ** block_scale(key_list[9], (N_SHARD, KB, BS * BS), ((0, 8), (2, 64)), -0.2, 0.2)), 0.05, 2.0),
    }


LEARN_RATE = 0.01
BETA_ONE = 0.9
BETA_TWO = 0.95
EPSILON = 1e-08

def adam_update(weight, first_state, second_state, gradient):
    first_state = BETA_ONE * first_state + (1.0 - BETA_ONE) * gradient
    second_state = BETA_TWO * second_state + (1.0 - BETA_TWO) * gradient * gradient
    weight = weight - LEARN_RATE * first_state / (jnp.sqrt(second_state) + EPSILON)
    return (weight, first_state, second_state)

def reference(hidden, out_grad, block_weight, block_row, block_col, live_count, new_owner, new_slot, first_moment, second_moment):
    row_blocks = FF // BS
    col_blocks = D // BS
    slot_total = N_SHARD * KB
    is_live = jnp.arange(KB)[None, :] < live_count[:, None]
    weights = jnp.where(is_live[:, :, None, None], block_weight, jnp.zeros((), jnp.bfloat16)).astype(jnp.float32)
    hidden_blocks = hidden.reshape(TOKENS, row_blocks, BS)
    grad_blocks = out_grad.reshape(TOKENS, col_blocks, BS)

    def one_shard(totals, member):
        blocks, row_ids, col_ids = member
        hidden_part = jnp.take(hidden_blocks, row_ids, axis=1).astype(jnp.float32)
        grad_part = jnp.take(grad_blocks, col_ids, axis=1).astype(jnp.float32)
        out_total = totals[0].at[:, col_ids].add(jnp.einsum('tkr,krc->tkc', hidden_part, blocks))
        back_total = totals[1].at[:, row_ids].add(jnp.einsum('tkc,krc->tkr', grad_part, blocks))
        return ((out_total, back_total), jnp.einsum('tkr,tkc->krc', hidden_part, grad_part))
    initial = (jnp.zeros((TOKENS, col_blocks, BS), jnp.float32), jnp.zeros((TOKENS, row_blocks, BS), jnp.float32))
    totals, gradients = lax.scan(one_shard, initial, (weights, block_row, block_col))
    projected = totals[0].reshape(TOKENS, D).astype(jnp.bfloat16)
    hidden_grad = totals[1].reshape(TOKENS, FF).astype(jnp.bfloat16)
    gradients = jnp.where(is_live[:, :, None, None], gradients * (1.0 / math.sqrt(TOKENS)), 0.0)
    gradients = gradients.reshape(N_SHARD, KB, BS * BS)
    weight_flat = block_weight.reshape(N_SHARD, KB, BS * BS).astype(jnp.float32)
    updated, first_state, second_state = adam_update(weight_flat, first_moment, second_moment, gradients)
    targets = jnp.where(new_owner >= 0, new_owner * KB + new_slot, slot_total).reshape(slot_total).astype(jnp.int32)

    def relayout(values):
        placed = jnp.zeros((slot_total + 1, BS * BS), jnp.float32).at[targets].add(values.reshape(slot_total, BS * BS))
        return placed[:slot_total].reshape(N_SHARD, KB, BS * BS)
    return (projected, hidden_grad, relayout(updated), relayout(first_state), relayout(second_state))
```

```python
import functools
import math

import jax
import jax.numpy as jnp
from jax import lax
from jax.experimental import pallas as pl
from jax.experimental.pallas import tpu as pltpu
from jax.sharding import Mesh, PartitionSpec as P

DP = ("y", "x", "zh")
SHARD = ("zl", "core")
MV = 2


LEARN_RATE = 0.01
BETA_ONE = 0.9
BETA_TWO = 0.95
EPSILON = 1e-08


def adam_update(weight, first_state, second_state, gradient):
    first_state = BETA_ONE * first_state + (1.0 - BETA_ONE) * gradient
    second_state = BETA_TWO * second_state + (1.0 - BETA_TWO) * gradient * gradient
    weight = weight - LEARN_RATE * first_state / (jnp.sqrt(second_state) + EPSILON)
    return (weight, first_state, second_state)


def send_positions(owner_devices, shard_count, slot_count):
    sources = jnp.arange(shard_count, dtype=jnp.int32)[:, None]
    moving = (owner_devices >= 0) & (owner_devices != sources)
    slot_ids = jnp.arange(slot_count)
    earlier = slot_ids[None, :] < slot_ids[:, None]
    matches = (
        (owner_devices[:, :, None] == owner_devices[:, None, :])
        & moving[:, None, :]
        & earlier[None, :, :]
    )
    return (moving, jnp.sum(matches, axis=2))


def pack_moving(values, owner_row, moving_row, position_row, shard_count, capacity):
    slot_ids = jnp.arange(values.shape[0], dtype=jnp.int32)
    targets = owner_row * capacity + position_row
    entries = jnp.arange(shard_count * capacity, dtype=jnp.int32)
    matches = (targets[None, :] == entries[:, None]) & moving_row[None, :]
    source = jnp.sum(jnp.where(matches, slot_ids[None, :], 0), axis=1)
    filled = jnp.any(matches, axis=1)
    packed = jnp.where(filled[:, None], jnp.take(values, source, axis=0), 0.0)
    return packed.reshape(shard_count, capacity, values.shape[1])


def place_blocks(
    received,
    own_values,
    owner_devices,
    destination_slot_list,
    moving,
    positions,
    my_index,
    capacity,
):
    shard_count, slot_count = owner_devices.shape
    slot_ids = jnp.arange(slot_count, dtype=jnp.int32)
    entries = (jnp.arange(shard_count, dtype=jnp.int32)[:, None] * capacity + positions).reshape(-1)
    to_me = (moving & (owner_devices == my_index)).reshape(-1)
    matches = to_me[None, :] & (destination_slot_list.reshape(-1)[None, :] == slot_ids[:, None])
    arrived = jnp.any(matches, axis=1)
    from_entry = jnp.sum(jnp.where(matches, entries[None, :], 0), axis=1)
    flattened = received.reshape(shard_count * capacity, received.shape[2])
    arrival_rows = jnp.take(flattened, from_entry, axis=0)
    stay_hit = (owner_devices[my_index] == my_index)[None, :] & (
        destination_slot_list[my_index][None, :] == slot_ids[:, None]
    )
    stayed = jnp.any(stay_hit, axis=1)
    from_slot = jnp.sum(jnp.where(stay_hit, slot_ids[None, :], 0), axis=1)
    kept_rows = jnp.take(own_values, from_slot, axis=0)
    return jnp.where(arrived[:, None], arrival_rows, jnp.where(stayed[:, None], kept_rows, 0.0))


def local_place(block_ids, first_id, local_count):
    local_ids = block_ids - first_id
    inside = (local_ids >= 0) & (local_ids < local_count)
    return jnp.where(inside, local_ids, local_count)


def general(
    hidden,
    out_grad,
    block_weight,
    block_row,
    block_col,
    live_count,
    new_owner,
    new_slot,
    first_moment,
    second_moment,
):
    shard_count = lax.axis_size(SHARD)
    dp_count = lax.axis_size(DP)
    my_index = lax.axis_index(SHARD)
    dp_index = lax.axis_index(DP)
    tokens_dev = hidden.shape[0]
    slot_count = block_weight.shape[1]
    block_size = block_weight.shape[2]
    share_size = first_moment.shape[2]
    row_blocks = hidden.shape[1] * shard_count // block_size
    col_blocks = out_grad.shape[1] * shard_count // block_size
    grad_scale = 1.0 / math.sqrt(tokens_dev * dp_count)
    slot_ids = jnp.arange(slot_count)
    live_all = slot_ids[None, :] < live_count[:, None]
    my_live = live_all[my_index]
    my_rows = block_row[my_index]
    my_cols = block_col[my_index]
    zero_bf = jnp.zeros((), jnp.bfloat16)
    full_hidden, full_grad = (
        lax.all_gather(hidden, SHARD, axis=1, tiled=True),
        lax.all_gather(out_grad, SHARD, axis=1, tiled=True),
    )
    hidden_blocks = full_hidden.reshape(tokens_dev, row_blocks, block_size)
    grad_blocks = full_grad.reshape(tokens_dev, col_blocks, block_size)
    own_hidden = jnp.take(hidden_blocks, my_rows, axis=1)
    own_grad = jnp.take(grad_blocks, my_cols, axis=1)
    grad_share = None
    col_local = col_blocks // shard_count
    row_local = row_blocks // shard_count

    def one_shard(totals, member):
        blocks, shard_index = member
        row_ids = block_row[shard_index]
        col_ids = block_col[shard_index]
        weights = jnp.where(live_all[shard_index][:, None, None], blocks, zero_bf)
        hidden_part = jnp.take(hidden_blocks, row_ids, axis=1)
        grad_part = jnp.take(grad_blocks, col_ids, axis=1)
        forward = jnp.einsum(
            "tkr,krc->tkc", hidden_part, weights, preferred_element_type=jnp.float32
        )
        backward = jnp.einsum(
            "tkc,krc->tkr", grad_part, weights, preferred_element_type=jnp.float32
        )
        col_place = local_place(col_ids, my_index * col_local, col_local)
        row_place = local_place(row_ids, my_index * row_local, row_local)
        out_total = totals[0].at[:, col_place].add(forward, mode="drop")
        back_total = totals[1].at[:, row_place].add(backward, mode="drop")
        return ((out_total, back_total), None)

    initial = (
        jnp.zeros((tokens_dev, col_local, block_size), jnp.float32),
        jnp.zeros((tokens_dev, row_local, block_size), jnp.float32),
    )
    totals = initial
    blocks_in = lax.all_gather(block_weight, SHARD, axis=0, tiled=True)
    indices = jnp.arange(blocks_in.shape[0], dtype=jnp.int32)
    totals, unused = lax.scan(one_shard, totals, (blocks_in, indices))
    out_total, back_total = totals
    projected = out_total.reshape(tokens_dev, col_local * block_size).astype(jnp.bfloat16)
    hidden_grad = back_total.reshape(tokens_dev, row_local * block_size).astype(jnp.bfloat16)
    blocks = (
        jnp.einsum("tkr,tkc->krc", own_hidden, own_grad, preferred_element_type=jnp.float32)
        * grad_scale
    )
    blocks = jnp.where(my_live[:, None, None], blocks, 0.0)
    grad_share = lax.psum_scatter(
        blocks.reshape(slot_count, block_size * block_size), DP, scatter_dimension=1, tiled=True
    )
    moving, positions = send_positions(new_owner, shard_count, slot_count)
    my_owner = new_owner[my_index]
    my_moving = moving[my_index]
    my_positions = positions[my_index]
    flat_weight = block_weight[0].reshape(slot_count, block_size * block_size)
    weight_share = lax.dynamic_slice_in_dim(
        flat_weight, dp_index * share_size, share_size, 1
    ).astype(jnp.float32)
    updated, first_state, second_state = adam_update(
        weight_share, first_moment[0], second_moment[0], grad_share
    )
    stacked = jnp.concatenate([updated, first_state, second_state], axis=1)
    packed = pack_moving(stacked, my_owner, my_moving, my_positions, shard_count, MV)
    received = lax.all_to_all(packed, SHARD, split_axis=0, concat_axis=0, tiled=True)
    placed = place_blocks(received, stacked, new_owner, new_slot, moving, positions, my_index, MV)
    new_weight = placed[:, :share_size]
    new_first = placed[:, share_size : 2 * share_size]
    new_second = placed[:, 2 * share_size :]
    return (projected, hidden_grad, new_weight[None], new_first[None], new_second[None])


CAP = 48
NX, NY, NZH, NZL = 4, 8, 2, 4
PER_X = CAP // NX
BS = 128
VMEM_LIMIT = 40 * 1024 * 1024
f32 = jnp.float32
bf16 = jnp.bfloat16


def vmem():
    return pl.BlockSpec(memory_space=pltpu.VMEM)


def smem():
    return pl.BlockSpec(memory_space=pltpu.SMEM)


def call(kernel, outs, n_smem, n_vmem, scratch=(), flops=0, byts=0):
    return pl.pallas_call(
        kernel,
        out_shape=outs,
        in_specs=[smem()] * n_smem + [vmem()] * n_vmem,
        out_specs=jax.tree.map(lambda _: vmem(), outs),
        scratch_shapes=list(scratch),
        compiler_params=pltpu.CompilerParams(vmem_limit_bytes=VMEM_LIMIT),
        cost_estimate=pl.CostEstimate(flops=flops, bytes_accessed=byts, transcendentals=0),
    )


def make_plan(block_row, block_col, live_count, new_owner, new_slot, row_local):
    shard_count, slot_count = block_row.shape
    total = shard_count * slot_count
    ids = jnp.arange(total, dtype=jnp.int32)
    live = (jnp.arange(slot_count)[None, :] < live_count[:, None]).reshape(total)
    row = block_row.reshape(total)
    col = block_col.reshape(total)
    owner = jnp.where(live, new_owner.reshape(total), -1)
    slot = new_slot.reshape(total)
    row_shard = row // row_local
    key = jnp.where(owner >= 0, ids, ids + total)
    before = (row_shard[:, None] == row_shard[None, :]) & live[None, :] & (key[None, :] < key[:, None])
    rank = jnp.sum(before.astype(jnp.int32), axis=1)
    fits = jnp.max(jnp.where(live, rank, 0)) < CAP
    return live, row, col, owner, slot, row_shard, rank, fits


def select_kernel(info, code, mine, other, out):
    my_core, my_x = info[2], info[3]
    for i in range(PER_X):
        g = code[my_x * PER_X + i] & 255
        owner_shard, k = g // 32, g % 32
        zl, core = owner_shard // 2, owner_shard % 2
        part, first = k // 8, (k % 8) * 16
        first = pl.multiple_of(first, 16)
        from_mine = mine[zl, 4 + part, pl.ds(first, 16), :]
        from_other = other[zl, 4 + part, pl.ds(first, 16), :]
        value = jnp.where(core == my_core, from_mine, from_other)
        for y in range(NY):
            out[y, i] = value


def grad_kernel(info, code, hidden, mine, other, out, cols, hidden_t, total):
    my_core = info[2]
    for zl in range(NZL):
        for sub in range(4):
            cols[(2 * zl + my_core) * 4 + sub] = mine[zl, sub]
            cols[(2 * zl + 1 - my_core) * 4 + sub] = other[zl, sub]
    row_local = hidden.shape[1] // BS
    for r in range(row_local):
        hidden_t[r] = hidden[:, r * BS : (r + 1) * BS].T

    def step(c, carry):
        word = code[c]
        r, col = (word >> 8) & 15, word >> 12
        block = jnp.dot(hidden_t[r], cols[col], preferred_element_type=f32)
        total[pl.ds(c, BS, stride=CAP), :] = block
        return carry

    lax.fori_loop(0, info[1], step, 0)
    for x in range(NX):
        for y in range(NY):
            for q in range(4):
                source = 16 * y + 4 * x + q
                out[x, 2 * y + q // 2, q % 2] = total[source * CAP : (source + 1) * CAP, :].astype(bf16)


def product_kernel(info, code, hidden, cols, weights, mine, theirs, back, out_total, back_total):
    my_core = info[2]
    row_local = hidden.shape[1] // BS
    out_total[...] = jnp.zeros_like(out_total)
    back_total[...] = jnp.zeros_like(back_total)

    def step(c, carry):
        word = code[c]
        r, col = (word >> 8) & 15, word >> 12
        w = weights[c // PER_X, :, c % PER_X].reshape(BS, BS)
        h = hidden[:, pl.ds(pl.multiple_of(r * BS, BS), BS)]
        out_total[col] += jnp.dot(h, w, preferred_element_type=f32)
        back_total[r] += lax.dot_general(
            cols[col], w, (((1,), (1,)), ((), ())), preferred_element_type=f32
        )
        return carry

    lax.fori_loop(0, info[0], step, 0)
    for zl in range(NZL):
        for sub in range(4):
            mine[zl, sub] = out_total[(2 * zl + my_core) * 4 + sub]
            theirs[zl, sub] = out_total[(2 * zl + 1 - my_core) * 4 + sub]
    for r in range(row_local):
        back[:, r * BS : (r + 1) * BS] = back_total[r].astype(bf16)


def pack_kernel(source, stacked, out):
    for e in range(out.shape[0]):
        out[pl.ds(e, 1), :] = stacked[pl.ds(source[e], 1), :]


def adam_kernel(place, stacked, received, shares, new_w, new_m, new_v, state, grad):
    slots = new_w.shape[0]
    share = new_w.shape[1]
    for j in range(slots):
        word = jnp.maximum(place[j] - 1, 0)
        g, row = word & 1023, word >> 10
        own = stacked[pl.ds(jnp.minimum(row, slots - 1), 1), :]
        came = received[pl.ds(jnp.maximum(row - slots, 0), 1), :]
        filled = place[j] > 0
        state[pl.ds(j, 1), :] = jnp.where(filled, jnp.where(row < slots, own, came), 0.0)
        shard, rank = g // CAP, g % CAP
        for b in range(2):
            value = shares[shard, b, pl.ds(rank, 1), :]
            grad[pl.ds(j, 1), b * BS : (b + 1) * BS] = jnp.where(filled, value, 0.0)
    w, m, v = adam_update(state[:, :share], state[:, share : 2 * share], state[:, 2 * share :], grad[...])
    new_w[...] = w
    new_m[...] = m
    new_v[...] = v


def fast(
    plan,
    hidden,
    out_grad,
    block_weight,
    first_moment,
    second_moment,
):
    live, row, col, owner, slot, row_shard, rank = plan
    shard_count = lax.axis_size(SHARD)
    me = lax.axis_index(SHARD)
    core = lax.axis_index("core")
    dp_index = lax.axis_index(DP)
    x_index, y_index = lax.axis_index("x"), lax.axis_index("y")
    tokens = hidden.shape[0]
    slot_count = block_weight.shape[1]
    row_local = hidden.shape[1] // BS
    share = first_moment.shape[2]
    total = shard_count * slot_count
    scale = 1.0 / math.sqrt(tokens * lax.axis_size(DP))
    ids = jnp.arange(total, dtype=jnp.int32)

    here = live & (row_shard == me)
    words = ids + 256 * ((row - row_local * me) + 16 * col)
    hit = here[None, :] & (rank[None, :] == jnp.arange(CAP)[:, None])
    code = jnp.sum(jnp.where(hit, words[None, :], 0), axis=1)
    info = jnp.stack([jnp.sum(here.astype(jnp.int32)), jnp.sum((here & (owner >= 0)).astype(jnp.int32)), core, x_index])

    owner2 = owner.reshape(shard_count, slot_count)
    sources = jnp.arange(shard_count, dtype=jnp.int32)[:, None]
    moving, positions = send_positions(owner2, shard_count, slot_count)
    entry = jnp.arange(shard_count * MV, dtype=jnp.int32)
    my_target = jnp.where(moving[me], owner2[me] * MV + positions[me], -1)
    send_hit = my_target[None, :] == entry[:, None]
    send_source = jnp.sum(jnp.where(send_hit, jnp.arange(slot_count, dtype=jnp.int32)[None, :], 0), axis=1)
    state_row = jnp.where(
        sources == me, jnp.arange(slot_count, dtype=jnp.int32)[None, :], slot_count + sources * MV + positions
    ).reshape(total)
    landing = 1 + row_shard * CAP + rank + 1024 * state_row
    lands = (owner == me)[None, :] & (slot[None, :] == jnp.arange(slot_count)[:, None])
    place = jnp.sum(jnp.where(lands, landing[None, :], 0), axis=1)

    rows_y = BS // NY
    my_cols = out_grad.reshape(tokens, 4, BS).transpose(1, 0, 2)
    my_weights = lax.dynamic_slice_in_dim(block_weight[0], y_index * rows_y, rows_y, 1).reshape(4, BS, BS)
    parcel = jnp.concatenate([my_cols, my_weights], axis=0)
    mine = lax.all_to_all(
        jnp.broadcast_to(parcel[None], (NZL,) + parcel.shape), "zl", split_axis=0, concat_axis=0, tiled=True
    )
    other = lax.ppermute(mine, "core", [(0, 1), (1, 0)])

    picked = call(select_kernel, jax.ShapeDtypeStruct((NY, PER_X, rows_y, BS), bf16), 2, 2)(info, code, mine, other)
    along_y = lax.all_to_all(picked, "y", split_axis=0, concat_axis=0, tiled=True)
    weights = lax.all_to_all(
        jnp.broadcast_to(along_y[None], (NX,) + along_y.shape), "x", split_axis=0, concat_axis=0, tiled=True
    )

    partial, cols = call(
        grad_kernel,
        (
            jax.ShapeDtypeStruct((NX, NY * NZH, 2, CAP, BS), bf16),
            jax.ShapeDtypeStruct((shard_count * 4, BS, BS), bf16),
        ),
        2,
        3,
        [pltpu.VMEM((row_local, BS, BS), bf16), pltpu.VMEM((BS * CAP, BS), f32)],
        flops=2 * CAP * BS**3,
        byts=4 * 1024 * 1024,
    )(info, code, hidden, mine, other)
    along_x = lax.all_to_all(partial, "x", split_axis=0, concat_axis=0, tiled=True)
    summed = jnp.sum(along_x.astype(f32), axis=0).astype(bf16)
    along_yz = lax.all_to_all(summed, ("y", "zh"), split_axis=0, concat_axis=0, tiled=True)
    grad_share = jnp.sum(along_yz.astype(f32), axis=0) * scale

    out_mine, out_theirs, hidden_grad = call(
        product_kernel,
        (
            jax.ShapeDtypeStruct((NZL, 4, tokens, BS), f32),
            jax.ShapeDtypeStruct((NZL, 4, tokens, BS), f32),
            jax.ShapeDtypeStruct(hidden.shape, bf16),
        ),
        2,
        3,
        [pltpu.VMEM((shard_count * 4, tokens, BS), f32), pltpu.VMEM((row_local, tokens, BS), f32)],
        flops=4 * CAP * BS**3,
        byts=8 * 1024 * 1024,
    )(info, code, hidden, cols, weights)
    from_other = lax.ppermute(out_theirs, "core", [(0, 1), (1, 0)])
    chip_sum = (out_mine + from_other).astype(bf16)
    along_z = lax.all_to_all(chip_sum, "zl", split_axis=0, concat_axis=0, tiled=True)
    projected = jnp.sum(along_z.astype(f32), axis=0).astype(bf16)
    projected = projected.transpose(1, 0, 2).reshape(tokens, 4 * BS)

    weight_share = lax.dynamic_slice_in_dim(block_weight[0], dp_index * 2, 2, 1).reshape(slot_count, share)
    stacked = jnp.concatenate([weight_share.astype(f32), first_moment[0], second_moment[0]], axis=1)
    packed = call(pack_kernel, jax.ShapeDtypeStruct((shard_count * MV, 3 * share), f32), 1, 1)(send_source, stacked)
    received = lax.all_to_all(packed, SHARD, split_axis=0, concat_axis=0, tiled=True)
    shares = lax.all_gather(grad_share, SHARD, axis=0)
    shape = jax.ShapeDtypeStruct((slot_count, share), f32)
    new_weight, new_first, new_second = call(
        adam_kernel,
        (shape, shape, shape),
        1,
        3,
        [pltpu.VMEM((slot_count, 3 * share), f32), pltpu.VMEM((slot_count, share), f32)],
    )(place, stacked, received, shares)
    return (projected, hidden_grad, new_weight[None], new_first[None], new_second[None])


def shards(
    hidden,
    out_grad,
    block_weight,
    block_row,
    block_col,
    live_count,
    new_owner,
    new_slot,
    first_moment,
    second_moment,
):
    row_local = hidden.shape[1] // BS
    *plan, fits = make_plan(block_row, block_col, live_count, new_owner, new_slot, row_local)
    return lax.cond(
        fits,
        lambda: fast(plan, hidden, out_grad, block_weight, first_moment, second_moment),
        lambda: general(
            hidden,
            out_grad,
            block_weight,
            block_row,
            block_col,
            live_count,
            new_owner,
            new_slot,
            first_moment,
            second_moment,
        ),
    )


def solution(mesh):
    split = Mesh(mesh.devices.reshape(NY, NX, NZH, NZL, 2), ("y", "x", "zh", "zl", "core"))
    in_specs = (
        P(DP, SHARD),
        P(DP, SHARD),
        P(SHARD, None, None, None),
        P(),
        P(),
        P(),
        P(),
        P(),
        P(SHARD, None, DP),
        P(SHARD, None, DP),
    )
    out_specs = (
        P(DP, SHARD),
        P(DP, SHARD),
        P(SHARD, None, DP),
        P(SHARD, None, DP),
        P(SHARD, None, DP),
    )
    return jax.shard_map(shards, mesh=split, in_specs=in_specs, out_specs=out_specs, check_vma=False)
```

```python
import functools
import math

import jax
import jax.numpy as jnp
from jax import lax
from jax.experimental import pallas as pl
from jax.experimental.pallas import tpu as pltpu
from jax.sharding import Mesh, PartitionSpec as P

DP = ("y", "x", "zh")
SHARD = ("zl", "core")
MV = 2


LEARN_RATE = 0.01
BETA_ONE = 0.9
BETA_TWO = 0.95
EPSILON = 1e-08


def adam_update(weight, first_state, second_state, gradient):
    first_state = BETA_ONE * first_state + (1.0 - BETA_ONE) * gradient
    second_state = BETA_TWO * second_state + (1.0 - BETA_TWO) * gradient * gradient
    weight = weight - LEARN_RATE * first_state / (jnp.sqrt(second_state) + EPSILON)
    return (weight, first_state, second_state)


def send_positions(owner_devices, shard_count, slot_count):
    sources = jnp.arange(shard_count, dtype=jnp.int32)[:, None]
    moving = (owner_devices >= 0) & (owner_devices != sources)
    slot_ids = jnp.arange(slot_count)
    earlier = slot_ids[None, :] < slot_ids[:, None]
    matches = (
        (owner_devices[:, :, None] == owner_devices[:, None, :])
        & moving[:, None, :]
        & earlier[None, :, :]
    )
    return (moving, jnp.sum(matches, axis=2))


def pack_moving(values, owner_row, moving_row, position_row, shard_count, capacity):
    slot_ids = jnp.arange(values.shape[0], dtype=jnp.int32)
    targets = owner_row * capacity + position_row
    entries = jnp.arange(shard_count * capacity, dtype=jnp.int32)
    matches = (targets[None, :] == entries[:, None]) & moving_row[None, :]
    source = jnp.sum(jnp.where(matches, slot_ids[None, :], 0), axis=1)
    filled = jnp.any(matches, axis=1)
    packed = jnp.where(filled[:, None], jnp.take(values, source, axis=0), 0.0)
    return packed.reshape(shard_count, capacity, values.shape[1])


def place_blocks(
    received,
    own_values,
    owner_devices,
    destination_slot_list,
    moving,
    positions,
    my_index,
    capacity,
):
    shard_count, slot_count = owner_devices.shape
    slot_ids = jnp.arange(slot_count, dtype=jnp.int32)
    entries = (jnp.arange(shard_count, dtype=jnp.int32)[:, None] * capacity + positions).reshape(-1)
    to_me = (moving & (owner_devices == my_index)).reshape(-1)
    matches = to_me[None, :] & (destination_slot_list.reshape(-1)[None, :] == slot_ids[:, None])
    arrived = jnp.any(matches, axis=1)
    from_entry = jnp.sum(jnp.where(matches, entries[None, :], 0), axis=1)
    flattened = received.reshape(shard_count * capacity, received.shape[2])
    arrival_rows = jnp.take(flattened, from_entry, axis=0)
    stay_hit = (owner_devices[my_index] == my_index)[None, :] & (
        destination_slot_list[my_index][None, :] == slot_ids[:, None]
    )
    stayed = jnp.any(stay_hit, axis=1)
    from_slot = jnp.sum(jnp.where(stay_hit, slot_ids[None, :], 0), axis=1)
    kept_rows = jnp.take(own_values, from_slot, axis=0)
    return jnp.where(arrived[:, None], arrival_rows, jnp.where(stayed[:, None], kept_rows, 0.0))


def local_place(block_ids, first_id, local_count):
    local_ids = block_ids - first_id
    inside = (local_ids >= 0) & (local_ids < local_count)
    return jnp.where(inside, local_ids, local_count)


def general(
    hidden,
    out_grad,
    block_weight,
    block_row,
    block_col,
    live_count,
    new_owner,
    new_slot,
    first_moment,
    second_moment,
):
    shard_count = lax.axis_size(SHARD)
    dp_count = lax.axis_size(DP)
    my_index = lax.axis_index(SHARD)
    dp_index = lax.axis_index(DP)
    tokens_dev = hidden.shape[0]
    slot_count = block_weight.shape[1]
    block_size = block_weight.shape[2]
    share_size = first_moment.shape[2]
    row_blocks = hidden.shape[1] * shard_count // block_size
    col_blocks = out_grad.shape[1] * shard_count // block_size
    grad_scale = 1.0 / math.sqrt(tokens_dev * dp_count)
    slot_ids = jnp.arange(slot_count)
    live_all = slot_ids[None, :] < live_count[:, None]
    my_live = live_all[my_index]
    my_rows = block_row[my_index]
    my_cols = block_col[my_index]
    zero_bf = jnp.zeros((), jnp.bfloat16)
    full_hidden, full_grad = (
        lax.all_gather(hidden, SHARD, axis=1, tiled=True),
        lax.all_gather(out_grad, SHARD, axis=1, tiled=True),
    )
    hidden_blocks = full_hidden.reshape(tokens_dev, row_blocks, block_size)
    grad_blocks = full_grad.reshape(tokens_dev, col_blocks, block_size)
    own_hidden = jnp.take(hidden_blocks, my_rows, axis=1)
    own_grad = jnp.take(grad_blocks, my_cols, axis=1)
    grad_share = None
    col_local = col_blocks // shard_count
    row_local = row_blocks // shard_count

    def one_shard(totals, member):
        blocks, shard_index = member
        row_ids = block_row[shard_index]
        col_ids = block_col[shard_index]
        weights = jnp.where(live_all[shard_index][:, None, None], blocks, zero_bf)
        hidden_part = jnp.take(hidden_blocks, row_ids, axis=1)
        grad_part = jnp.take(grad_blocks, col_ids, axis=1)
        forward = jnp.einsum(
            "tkr,krc->tkc", hidden_part, weights, preferred_element_type=jnp.float32
        )
        backward = jnp.einsum(
            "tkc,krc->tkr", grad_part, weights, preferred_element_type=jnp.float32
        )
        col_place = local_place(col_ids, my_index * col_local, col_local)
        row_place = local_place(row_ids, my_index * row_local, row_local)
        out_total = totals[0].at[:, col_place].add(forward, mode="drop")
        back_total = totals[1].at[:, row_place].add(backward, mode="drop")
        return ((out_total, back_total), None)

    initial = (
        jnp.zeros((tokens_dev, col_local, block_size), jnp.float32),
        jnp.zeros((tokens_dev, row_local, block_size), jnp.float32),
    )
    totals = initial
    blocks_in = lax.all_gather(block_weight, SHARD, axis=0, tiled=True)
    indices = jnp.arange(blocks_in.shape[0], dtype=jnp.int32)
    totals, unused = lax.scan(one_shard, totals, (blocks_in, indices))
    out_total, back_total = totals
    projected = out_total.reshape(tokens_dev, col_local * block_size).astype(jnp.bfloat16)
    hidden_grad = back_total.reshape(tokens_dev, row_local * block_size).astype(jnp.bfloat16)
    blocks = (
        jnp.einsum("tkr,tkc->krc", own_hidden, own_grad, preferred_element_type=jnp.float32)
        * grad_scale
    )
    blocks = jnp.where(my_live[:, None, None], blocks, 0.0)
    grad_share = lax.psum_scatter(
        blocks.reshape(slot_count, block_size * block_size), DP, scatter_dimension=1, tiled=True
    )
    moving, positions = send_positions(new_owner, shard_count, slot_count)
    my_owner = new_owner[my_index]
    my_moving = moving[my_index]
    my_positions = positions[my_index]
    flat_weight = block_weight[0].reshape(slot_count, block_size * block_size)
    weight_share = lax.dynamic_slice_in_dim(
        flat_weight, dp_index * share_size, share_size, 1
    ).astype(jnp.float32)
    updated, first_state, second_state = adam_update(
        weight_share, first_moment[0], second_moment[0], grad_share
    )
    stacked = jnp.concatenate([updated, first_state, second_state], axis=1)
    packed = pack_moving(stacked, my_owner, my_moving, my_positions, shard_count, MV)
    received = lax.all_to_all(packed, SHARD, split_axis=0, concat_axis=0, tiled=True)
    placed = place_blocks(received, stacked, new_owner, new_slot, moving, positions, my_index, MV)
    new_weight = placed[:, :share_size]
    new_first = placed[:, share_size : 2 * share_size]
    new_second = placed[:, 2 * share_size :]
    return (projected, hidden_grad, new_weight[None], new_first[None], new_second[None])


CAP = 48
PAIR = 16
NX, NY, NZH, NZL = 4, 8, 2, 4
BS = 128
VMEM_LIMIT = 40 * 1024 * 1024
f32 = jnp.float32
bf16 = jnp.bfloat16
i32 = jnp.int32


def call(kernel, outs, n_smem, n_vmem, scratch=(), flops=0, byts=0):
    smem = pl.BlockSpec(memory_space=pltpu.SMEM)
    vmem = pl.BlockSpec(memory_space=pltpu.VMEM)
    return pl.pallas_call(
        kernel,
        out_shape=outs,
        in_specs=[smem] * n_smem + [vmem] * n_vmem,
        out_specs=jax.tree.map(lambda _: vmem, outs),
        scratch_shapes=list(scratch),
        compiler_params=pltpu.CompilerParams(vmem_limit_bytes=VMEM_LIMIT),
        cost_estimate=pl.CostEstimate(flops=flops, bytes_accessed=byts, transcendentals=0),
    )


def like(shape, dtype):
    return jax.ShapeDtypeStruct(shape, dtype)


def make_plan(block_row, block_col, live_count, new_owner, new_slot, row_local, me):
    shard_count, slot_count = block_row.shape
    total = shard_count * slot_count
    ids = jnp.arange(total, dtype=i32)
    live = (jnp.arange(slot_count)[None, :] < live_count[:, None]).reshape(total)
    row = block_row.reshape(total)
    col = block_col.reshape(total)
    owner = jnp.where(live, new_owner.reshape(total), -1)
    slot = new_slot.reshape(total)
    kept = owner >= 0
    row_shard = row // row_local
    key = jnp.where(kept, ids, ids + total)
    same = row_shard[:, None] == row_shard[None, :]
    before = same & live[None, :] & (key[None, :] < key[:, None])
    rank = jnp.sum(before.astype(i32), axis=1)
    earlier = same & (owner[:, None] == owner[None, :]) & (ids[None, :] < ids[:, None])
    pos = jnp.sum(earlier.astype(i32), axis=1)
    fits = (jnp.max(jnp.where(live, rank, 0)) < CAP) & (jnp.max(jnp.where(kept, pos, 0)) < PAIR)

    here = live & (row_shard == me)
    words = ids + 256 * ((row - row_local * me) + 16 * col)
    hit = here[None, :] & (rank[None, :] == jnp.arange(CAP)[:, None])
    code = jnp.sum(jnp.where(hit, words[None, :], 0), axis=1)
    counts = jnp.stack([jnp.sum(here.astype(i32)), jnp.sum((here & kept).astype(i32))])
    counts = jnp.minimum(counts, CAP)
    going = jnp.where(here & kept, owner * PAIR + pos, -1)
    send_hit = going[None, :] == jnp.arange(shard_count * PAIR)[:, None]
    send = jnp.minimum(jnp.sum(jnp.where(send_hit, rank[None, :], 0), axis=1), CAP - 1)
    landing = 1 + row_shard * PAIR + jnp.minimum(pos, PAIR - 1) + shard_count * PAIR * ids
    lands = (owner == me)[None, :] & (slot[None, :] == jnp.arange(slot_count)[:, None])
    place = jnp.sum(jnp.where(lands, landing[None, :], 0), axis=1)
    return fits, code, counts, send, place


def grad_kernel(info, code, hidden, mine, other, out, cols, hidden_t, total):
    my_core = info[2]
    for zl in range(NZL):
        for sub in range(4):
            lanes = slice(sub * BS, (sub + 1) * BS)
            cols[(2 * zl + my_core) * 4 + sub] = mine[zl, :, lanes]
            cols[(2 * zl + 1 - my_core) * 4 + sub] = other[zl, :, lanes]
    row_local = hidden.shape[1] // BS
    for r in range(row_local):
        hidden_t[r] = hidden[:, r * BS : (r + 1) * BS].T

    def step(c, carry):
        word = code[c]
        r, col = (word >> 8) & 15, word >> 12
        block = jnp.dot(hidden_t[r], cols[col], preferred_element_type=f32)
        total[pl.ds(c, BS, stride=CAP), :] = block
        return carry

    lax.fori_loop(0, info[1], step, 0)
    for x in range(NX):
        for y in range(NY):
            for q in range(4):
                source = 16 * y + 4 * x + q
                out[x, 4 * y + q] = total[source * CAP : (source + 1) * CAP, :].astype(bf16)


def sum_kernel(parts, out):
    def step(i, carry):
        value = parts[0, i].astype(f32)
        for n in range(1, parts.shape[0]):
            value += parts[n, i].astype(f32)
        out[i] = value.astype(bf16)
        return carry

    lax.fori_loop(0, out.shape[0], step, 0, unroll=4)


def share_kernel(scale, send, parts, out, total):
    for b in range(2):
        value = parts[0, b].astype(f32)
        for n in range(1, parts.shape[0]):
            value += parts[n, b].astype(f32)
        total[b] = value * scale
    for d in range(out.shape[0]):
        for p in range(PAIR):
            rank = send[d * PAIR + p]
            for b in range(2):
                out[d, b, p : p + 1, :] = total[b, pl.ds(rank, 1), :]


def select_kernel(info, code, gathered, out):
    def step(c, carry):
        out[c] = gathered[code[c] & 255]
        return carry

    lax.fori_loop(0, CAP, step, 0, unroll=4)


def forward_kernel(info, code, hidden, w0, w1, w2, w3, mine, theirs, weights, total):
    my_core, my_x = info[2], info[3]
    total[...] = jnp.zeros_like(total)

    def step(c, carry):
        word = code[c]
        r, col = (word >> 8) & 15, word >> 12
        for k, part in enumerate((w0, w1, w2, w3)):
            weights[c, (my_x + NX - k) % NX] = part[c]
        w = weights[c].reshape(BS, BS)
        h = hidden[:, pl.ds(pl.multiple_of(r * BS, BS), BS)]
        total[col] += jnp.dot(h, w, preferred_element_type=f32)
        return carry

    lax.fori_loop(0, info[0], step, 0)
    for zl in range(NZL):
        for sub in range(4):
            mine[zl, sub] = total[(2 * zl + my_core) * 4 + sub]
            theirs[zl, sub] = total[(2 * zl + 1 - my_core) * 4 + sub]


def backward_kernel(info, code, cols, weights, back, total):
    total[...] = jnp.zeros_like(total)

    def step(c, carry):
        word = code[c]
        r, col = (word >> 8) & 15, word >> 12
        w = weights[c].reshape(BS, BS)
        total[r] += lax.dot_general(cols[col], w, (((1,), (1,)), ((), ())), preferred_element_type=f32)
        return carry

    lax.fori_loop(0, info[0], step, 0)
    for r in range(total.shape[0]):
        back[:, r * BS : (r + 1) * BS] = total[r].astype(bf16)


def chip_kernel(info, mine, came, own, s1, s2, s3):
    my_zl = info[4]
    own[...] = mine[my_zl] + came[my_zl]
    for k, out in enumerate((s1, s2, s3)):
        zl = (my_zl + k + 1) % NZL
        out[...] = (mine[zl] + came[zl]).astype(bf16)


def project_kernel(own, r1, r2, r3, out):
    for sub in range(4):
        value = own[sub] + r1[sub].astype(f32) + r2[sub].astype(f32) + r3[sub].astype(f32)
        out[:, sub * BS : (sub + 1) * BS] = value.astype(bf16)


def adam_kernel(place, state, shares, new_w, new_m, new_v, rows, grad):
    slots, share = new_w.shape
    share_rows = shares.shape[0] * PAIR
    for j in range(slots):
        word = jnp.maximum(place[j] - 1, 0)
        g, row = word % share_rows, word // share_rows
        filled = place[j] > 0
        rows[pl.ds(j, 1), :] = jnp.where(filled, state[row // slots, pl.ds(row % slots, 1), :], 0.0)
        for b in range(2):
            value = shares[g // PAIR, b, pl.ds(g % PAIR, 1), :]
            grad[pl.ds(j, 1), b * BS : (b + 1) * BS] = jnp.where(filled, value, 0.0)
    w, m, v = adam_update(rows[:, :share], rows[:, share : 2 * share], rows[:, 2 * share :], grad[...])
    new_w[...] = w
    new_m[...] = m
    new_v[...] = v


def all_to_all(values, axis):
    return lax.all_to_all(values, axis, split_axis=0, concat_axis=0, tiled=True)


def shift(values, axis, count, step):
    return lax.ppermute(values, axis, [(i, (i + step) % count) for i in range(count)])


def shards(
    hidden,
    out_grad,
    block_weight,
    block_row,
    block_col,
    live_count,
    new_owner,
    new_slot,
    first_moment,
    second_moment,
):
    shard_count = lax.axis_size(SHARD)
    me = lax.axis_index(SHARD)
    dp_index = lax.axis_index(DP)
    x_index = lax.axis_index("x")
    tokens = hidden.shape[0]
    slot_count = block_weight.shape[1]
    row_local = hidden.shape[1] // BS
    share = first_moment.shape[2]
    scale = 1.0 / math.sqrt(tokens * lax.axis_size(DP))

    mine = all_to_all(jnp.broadcast_to(out_grad[None], (NZL,) + out_grad.shape), "zl")
    other = shift(mine, "core", 2, 1)
    quarter = lax.dynamic_slice_in_dim(block_weight[0], x_index * (BS // NX), BS // NX, 1)
    gathered = lax.all_gather(quarter, SHARD, axis=0, tiled=True)
    weight_share = lax.dynamic_slice_in_dim(block_weight[0], dp_index * 2, 2, 1).reshape(slot_count, share)
    stacked = jnp.concatenate([weight_share.astype(f32), first_moment[0], second_moment[0]], axis=1)
    state = lax.all_gather(stacked, SHARD, axis=0)

    fits, code, counts, send, place = make_plan(
        block_row, block_col, live_count, new_owner, new_slot, row_local, me
    )
    info = jnp.concatenate([counts, jnp.stack([lax.axis_index("core"), x_index, lax.axis_index("zl")])])

    partial, cols = call(
        grad_kernel,
        (like((NX, NY * NZH * 2, CAP, BS), bf16), like((shard_count * 4, BS, BS), bf16)),
        2,
        3,
        [pltpu.VMEM((row_local, BS, BS), bf16), pltpu.VMEM((BS * CAP, BS), f32)],
        flops=2 * CAP * BS**3,
        byts=4 * 1024 * 1024,
    )(info, code, hidden, mine, other)
    along_x = all_to_all(partial, "x")
    summed = call(sum_kernel, like(partial.shape[1:], bf16), 0, 1, byts=2 * 1024 * 1024)(along_x)
    along_yz = all_to_all(summed.reshape(NY * NZH, 2, CAP, BS), ("y", "zh"))
    shares = call(
        functools.partial(share_kernel, scale),
        like((shard_count, 2, PAIR, BS), f32),
        1,
        1,
        [pltpu.VMEM((2, CAP, BS), f32)],
        byts=1024 * 1024,
    )(send, along_yz)
    shares = all_to_all(shares, SHARD)

    w0 = call(select_kernel, like((CAP, BS // NX, BS), bf16), 2, 1, byts=1024 * 1024)(info, code, gathered)
    w1, w2, w3 = (shift(w0, "x", NX, k) for k in (1, 2, 3))

    out_mine, out_theirs, weights = call(
        forward_kernel,
        (
            like((NZL, 4, tokens, BS), f32),
            like((NZL, 4, tokens, BS), f32),
            like((CAP, NX, BS // NX, BS), bf16),
        ),
        2,
        5,
        [pltpu.VMEM((shard_count * 4, tokens, BS), f32)],
        flops=2 * CAP * BS**3,
        byts=8 * 1024 * 1024,
    )(info, code, hidden, w0, w1, w2, w3)
    came = shift(out_theirs, "core", 2, 1)
    hidden_grad = call(
        backward_kernel,
        like(hidden.shape, bf16),
        2,
        2,
        [pltpu.VMEM((row_local, tokens, BS), f32)],
        flops=2 * CAP * BS**3,
        byts=4 * 1024 * 1024,
    )(info, code, cols, weights)
    part = (4, tokens, BS)
    own, s1, s2, s3 = call(
        chip_kernel, (like(part, f32),) + (like(part, bf16),) * 3, 1, 2, byts=3 * 1024 * 1024
    )(info, out_mine, came)
    r1, r2, r3 = (shift(s, "zl", NZL, k + 1) for k, s in enumerate((s1, s2, s3)))
    projected = call(project_kernel, like(out_grad.shape, bf16), 0, 4, byts=1024 * 1024)(own, r1, r2, r3)

    shape = like((slot_count, share), f32)
    new_weight, new_first, new_second = call(
        adam_kernel,
        (shape, shape, shape),
        1,
        2,
        [pltpu.VMEM((slot_count, 3 * share), f32), pltpu.VMEM((slot_count, share), f32)],
        byts=1024 * 1024,
    )(place, state, shares)
    result = (projected, hidden_grad, new_weight[None], new_first[None], new_second[None])
    return lax.cond(
        fits,
        lambda: result,
        lambda: general(
            hidden,
            out_grad,
            block_weight,
            block_row,
            block_col,
            live_count,
            new_owner,
            new_slot,
            first_moment,
            second_moment,
        ),
    )


def solution(mesh):
    split = Mesh(mesh.devices.reshape(NY, NX, NZH, NZL, 2), ("y", "x", "zh", "zl", "core"))
    in_specs = (
        P(DP, SHARD),
        P(DP, SHARD),
        P(SHARD, None, None, None),
        P(),
        P(),
        P(),
        P(),
        P(),
        P(SHARD, None, DP),
        P(SHARD, None, DP),
    )
    out_specs = (
        P(DP, SHARD),
        P(DP, SHARD),
        P(SHARD, None, DP),
        P(SHARD, None, DP),
        P(SHARD, None, DP),
    )
    return jax.shard_map(shards, mesh=split, in_specs=in_specs, out_specs=out_specs, check_vma=False)
```

```python
import functools
import math

import jax
import jax.numpy as jnp
from jax import lax
from jax.experimental import pallas as pl
from jax.experimental.pallas import tpu as pltpu
from jax.sharding import Mesh, PartitionSpec as P

DP = ("y", "x", "zh")
SHARD = ("zl", "core")
MV = 2


LEARN_RATE = 0.01
BETA_ONE = 0.9
BETA_TWO = 0.95
EPSILON = 1e-08


def adam_update(weight, first_state, second_state, gradient):
    first_state = BETA_ONE * first_state + (1.0 - BETA_ONE) * gradient
    second_state = BETA_TWO * second_state + (1.0 - BETA_TWO) * gradient * gradient
    weight = weight - LEARN_RATE * first_state / (jnp.sqrt(second_state) + EPSILON)
    return (weight, first_state, second_state)


def send_positions(owner_devices, shard_count, slot_count):
    sources = jnp.arange(shard_count, dtype=jnp.int32)[:, None]
    moving = (owner_devices >= 0) & (owner_devices != sources)
    slot_ids = jnp.arange(slot_count)
    earlier = slot_ids[None, :] < slot_ids[:, None]
    matches = (
        (owner_devices[:, :, None] == owner_devices[:, None, :])
        & moving[:, None, :]
        & earlier[None, :, :]
    )
    return (moving, jnp.sum(matches, axis=2))


def pack_moving(values, owner_row, moving_row, position_row, shard_count, capacity):
    slot_ids = jnp.arange(values.shape[0], dtype=jnp.int32)
    targets = owner_row * capacity + position_row
    entries = jnp.arange(shard_count * capacity, dtype=jnp.int32)
    matches = (targets[None, :] == entries[:, None]) & moving_row[None, :]
    source = jnp.sum(jnp.where(matches, slot_ids[None, :], 0), axis=1)
    filled = jnp.any(matches, axis=1)
    packed = jnp.where(filled[:, None], jnp.take(values, source, axis=0), 0.0)
    return packed.reshape(shard_count, capacity, values.shape[1])


def place_blocks(
    received,
    own_values,
    owner_devices,
    destination_slot_list,
    moving,
    positions,
    my_index,
    capacity,
):
    shard_count, slot_count = owner_devices.shape
    slot_ids = jnp.arange(slot_count, dtype=jnp.int32)
    entries = (jnp.arange(shard_count, dtype=jnp.int32)[:, None] * capacity + positions).reshape(-1)
    to_me = (moving & (owner_devices == my_index)).reshape(-1)
    matches = to_me[None, :] & (destination_slot_list.reshape(-1)[None, :] == slot_ids[:, None])
    arrived = jnp.any(matches, axis=1)
    from_entry = jnp.sum(jnp.where(matches, entries[None, :], 0), axis=1)
    flattened = received.reshape(shard_count * capacity, received.shape[2])
    arrival_rows = jnp.take(flattened, from_entry, axis=0)
    stay_hit = (owner_devices[my_index] == my_index)[None, :] & (
        destination_slot_list[my_index][None, :] == slot_ids[:, None]
    )
    stayed = jnp.any(stay_hit, axis=1)
    from_slot = jnp.sum(jnp.where(stay_hit, slot_ids[None, :], 0), axis=1)
    kept_rows = jnp.take(own_values, from_slot, axis=0)
    return jnp.where(arrived[:, None], arrival_rows, jnp.where(stayed[:, None], kept_rows, 0.0))


def local_place(block_ids, first_id, local_count):
    local_ids = block_ids - first_id
    inside = (local_ids >= 0) & (local_ids < local_count)
    return jnp.where(inside, local_ids, local_count)


def general(
    hidden,
    out_grad,
    block_weight,
    block_row,
    block_col,
    live_count,
    new_owner,
    new_slot,
    first_moment,
    second_moment,
):
    shard_count = lax.axis_size(SHARD)
    dp_count = lax.axis_size(DP)
    my_index = lax.axis_index(SHARD)
    dp_index = lax.axis_index(DP)
    tokens_dev = hidden.shape[0]
    slot_count = block_weight.shape[1]
    block_size = block_weight.shape[2]
    share_size = first_moment.shape[2]
    row_blocks = hidden.shape[1] * shard_count // block_size
    col_blocks = out_grad.shape[1] * shard_count // block_size
    grad_scale = 1.0 / math.sqrt(tokens_dev * dp_count)
    slot_ids = jnp.arange(slot_count)
    live_all = slot_ids[None, :] < live_count[:, None]
    my_live = live_all[my_index]
    my_rows = block_row[my_index]
    my_cols = block_col[my_index]
    zero_bf = jnp.zeros((), jnp.bfloat16)
    full_hidden, full_grad = (
        lax.all_gather(hidden, SHARD, axis=1, tiled=True),
        lax.all_gather(out_grad, SHARD, axis=1, tiled=True),
    )
    hidden_blocks = full_hidden.reshape(tokens_dev, row_blocks, block_size)
    grad_blocks = full_grad.reshape(tokens_dev, col_blocks, block_size)
    own_hidden = jnp.take(hidden_blocks, my_rows, axis=1)
    own_grad = jnp.take(grad_blocks, my_cols, axis=1)
    grad_share = None
    col_local = col_blocks // shard_count
    row_local = row_blocks // shard_count

    def one_shard(totals, member):
        blocks, shard_index = member
        row_ids = block_row[shard_index]
        col_ids = block_col[shard_index]
        weights = jnp.where(live_all[shard_index][:, None, None], blocks, zero_bf)
        hidden_part = jnp.take(hidden_blocks, row_ids, axis=1)
        grad_part = jnp.take(grad_blocks, col_ids, axis=1)
        forward = jnp.einsum(
            "tkr,krc->tkc", hidden_part, weights, preferred_element_type=jnp.float32
        )
        backward = jnp.einsum(
            "tkc,krc->tkr", grad_part, weights, preferred_element_type=jnp.float32
        )
        col_place = local_place(col_ids, my_index * col_local, col_local)
        row_place = local_place(row_ids, my_index * row_local, row_local)
        out_total = totals[0].at[:, col_place].add(forward, mode="drop")
        back_total = totals[1].at[:, row_place].add(backward, mode="drop")
        return ((out_total, back_total), None)

    initial = (
        jnp.zeros((tokens_dev, col_local, block_size), jnp.float32),
        jnp.zeros((tokens_dev, row_local, block_size), jnp.float32),
    )
    totals = initial
    blocks_in = lax.all_gather(block_weight, SHARD, axis=0, tiled=True)
    indices = jnp.arange(blocks_in.shape[0], dtype=jnp.int32)
    totals, unused = lax.scan(one_shard, totals, (blocks_in, indices))
    out_total, back_total = totals
    projected = out_total.reshape(tokens_dev, col_local * block_size).astype(jnp.bfloat16)
    hidden_grad = back_total.reshape(tokens_dev, row_local * block_size).astype(jnp.bfloat16)
    blocks = (
        jnp.einsum("tkr,tkc->krc", own_hidden, own_grad, preferred_element_type=jnp.float32)
        * grad_scale
    )
    blocks = jnp.where(my_live[:, None, None], blocks, 0.0)
    grad_share = lax.psum_scatter(
        blocks.reshape(slot_count, block_size * block_size), DP, scatter_dimension=1, tiled=True
    )
    moving, positions = send_positions(new_owner, shard_count, slot_count)
    my_owner = new_owner[my_index]
    my_moving = moving[my_index]
    my_positions = positions[my_index]
    flat_weight = block_weight[0].reshape(slot_count, block_size * block_size)
    weight_share = lax.dynamic_slice_in_dim(
        flat_weight, dp_index * share_size, share_size, 1
    ).astype(jnp.float32)
    updated, first_state, second_state = adam_update(
        weight_share, first_moment[0], second_moment[0], grad_share
    )
    stacked = jnp.concatenate([updated, first_state, second_state], axis=1)
    packed = pack_moving(stacked, my_owner, my_moving, my_positions, shard_count, MV)
    received = lax.all_to_all(packed, SHARD, split_axis=0, concat_axis=0, tiled=True)
    placed = place_blocks(received, stacked, new_owner, new_slot, moving, positions, my_index, MV)
    new_weight = placed[:, :share_size]
    new_first = placed[:, share_size : 2 * share_size]
    new_second = placed[:, 2 * share_size :]
    return (projected, hidden_grad, new_weight[None], new_first[None], new_second[None])


WCAP = 44
GCAP = 40
PAIR = 14
UNROLL = 4
NX, NY, NZH, NZL = 4, 8, 2, 4
BS = 128
VMEM_LIMIT = 14 * 1024 * 1024
f32 = jnp.float32
bf16 = jnp.bfloat16
i32 = jnp.int32


def call(kernel, outs, n_smem, n_vmem, scratch=(), flops=0, byts=0):
    smem = pl.BlockSpec(memory_space=pltpu.SMEM)
    vmem = pl.BlockSpec(memory_space=pltpu.VMEM)
    return pl.pallas_call(
        kernel,
        out_shape=outs,
        in_specs=[smem] * n_smem + [vmem] * n_vmem,
        out_specs=jax.tree.map(lambda _: vmem, outs),
        scratch_shapes=list(scratch),
        compiler_params=pltpu.CompilerParams(vmem_limit_bytes=VMEM_LIMIT),
        cost_estimate=pl.CostEstimate(flops=flops, bytes_accessed=byts, transcendentals=0),
    )


def like(shape, dtype):
    return jax.ShapeDtypeStruct(shape, dtype)


def make_plan(block_row, block_col, live_count, new_owner, new_slot, row_local, me):
    shard_count, slot_count = block_row.shape
    total = shard_count * slot_count
    ids = jnp.arange(total, dtype=i32)
    live = (jnp.arange(slot_count)[None, :] < live_count[:, None]).reshape(total)
    row = block_row.reshape(total)
    col = block_col.reshape(total)
    owner = jnp.where(live, new_owner.reshape(total), -1)
    slot = new_slot.reshape(total)
    kept = owner >= 0
    row_shard = row // row_local
    key = jnp.where(kept, ids, ids + total)
    same = row_shard[:, None] == row_shard[None, :]
    before = same & live[None, :] & (key[None, :] < key[:, None])
    rank = jnp.sum(before.astype(i32), axis=1)
    earlier = same & (owner[:, None] == owner[None, :]) & (ids[None, :] < ids[:, None])
    pos = jnp.sum(earlier.astype(i32), axis=1)
    fits = (
        (jnp.max(jnp.where(live, rank, 0)) < WCAP)
        & (jnp.max(jnp.where(kept, rank, 0)) < GCAP)
        & (jnp.max(jnp.where(kept, pos, 0)) < PAIR)
    )

    here = live & (row_shard == me)
    words = ids + 256 * ((row - row_local * me) + 16 * col)
    hit = here[None, :] & (rank[None, :] == jnp.arange(WCAP)[:, None])
    code = jnp.sum(jnp.where(hit, words[None, :], 0), axis=1)
    counts = [jnp.minimum(jnp.sum(here.astype(i32)), WCAP), jnp.minimum(jnp.sum((here & kept).astype(i32)), GCAP)]
    going = jnp.where(here & kept, owner * PAIR + pos, -1)
    send_hit = going[None, :] == jnp.arange(shard_count * PAIR)[:, None]
    send = jnp.minimum(jnp.sum(jnp.where(send_hit, rank[None, :], 0), axis=1), GCAP - 1)
    owner2 = owner.reshape(shard_count, slot_count)
    sources = jnp.arange(shard_count, dtype=i32)[:, None]
    slots = jnp.arange(slot_count, dtype=i32)[None, :]
    moving, positions = send_positions(owner2, shard_count, slot_count)
    target = jnp.where(moving & (sources == me), owner2 * MV + positions, -1).reshape(total)
    state_hit = target[None, :] == jnp.arange(shard_count * MV)[:, None]
    state_send = jnp.sum(jnp.where(state_hit, (ids % slot_count)[None, :], 0), axis=1)
    state_row = jnp.where(sources == me, slots, slot_count + sources * MV + positions).reshape(total)
    landing = 1 + row_shard * PAIR + jnp.minimum(pos, PAIR - 1) + shard_count * PAIR * state_row
    lands = (owner == me)[None, :] & (slot[None, :] == jnp.arange(slot_count)[:, None])
    place = jnp.sum(jnp.where(lands, landing[None, :], 0), axis=1)
    return fits, code, counts, send, state_send, place


def grad_kernel(info, code, hidden, mine, other, out, cols, hidden_t, total):
    my_core = info[2]
    for zl in range(NZL):
        for sub in range(4):
            lanes = slice(sub * BS, (sub + 1) * BS)
            cols[(2 * zl + my_core) * 4 + sub] = mine[zl, :, lanes]
            cols[(2 * zl + 1 - my_core) * 4 + sub] = other[zl, :, lanes]
    row_local = hidden.shape[1] // BS
    for r in range(row_local):
        hidden_t[r] = hidden[:, r * BS : (r + 1) * BS].T

    def step(i, carry):
        blocks = []
        for u in range(UNROLL):
            word = code[i * UNROLL + u]
            blocks.append(jnp.dot(hidden_t[(word >> 8) & 15], cols[word >> 12], preferred_element_type=f32))
        for u in range(UNROLL):
            total[pl.ds(i * UNROLL + u, BS, stride=GCAP), :] = blocks[u]
        return carry

    lax.fori_loop(0, (info[1] + UNROLL - 1) // UNROLL, step, 0)
    for x in range(NX):
        for y in range(NY):
            for q in range(4):
                source = 16 * y + 4 * x + q
                out[x, 4 * y + q] = total[source * GCAP : (source + 1) * GCAP, :].astype(bf16)


def sum_kernel(parts, out):
    def step(i, carry):
        value = parts[0, i].astype(f32)
        for n in range(1, parts.shape[0]):
            value += parts[n, i].astype(f32)
        out[i] = value.astype(bf16)
        return carry

    lax.fori_loop(0, out.shape[0], step, 0, unroll=4)


def share_kernel(scale, send, state_send, parts, stacked, out, total):
    for b in range(2):
        value = parts[0, b].astype(f32)
        for n in range(1, parts.shape[0]):
            value += parts[n, b].astype(f32)
        total[b] = value * scale
    width = stacked.shape[1] // BS
    for d in range(out.shape[0]):
        for p in range(PAIR):
            rank = send[d * PAIR + p]
            for b in range(2):
                out[d, 2 * p + b : 2 * p + b + 1, :] = total[b, pl.ds(rank, 1), :]
        for p in range(MV):
            row = stacked[pl.ds(state_send[d * MV + p], 1), :]
            for n in range(width):
                at = 2 * PAIR + width * p + n
                out[d, at : at + 1, :] = row[:, n * BS : (n + 1) * BS]


def select_kernel(info, code, gathered, out):
    def step(c, carry):
        value = gathered[code[c] & 255]
        out[c] = jnp.where(c < info[0], value, jnp.zeros_like(value))
        return carry

    lax.fori_loop(0, WCAP, step, 0, unroll=4)


def forward_kernel(info, code, hidden, w0, w1, w2, w3, mine, theirs, weights, total):
    my_core, my_x = info[2], info[3]
    total[...] = jnp.zeros_like(total)

    def step(i, carry):
        adds = []
        for u in range(UNROLL):
            c = i * UNROLL + u
            word = code[c]
            for k, part in enumerate((w0, w1, w2, w3)):
                weights[c, (my_x + NX - k) % NX] = part[c]
            lanes = pl.ds(pl.multiple_of(((word >> 8) & 15) * BS, BS), BS)
            w = weights[c].reshape(BS, BS)
            adds.append((word >> 12, jnp.dot(hidden[:, lanes], w, preferred_element_type=f32)))
        for col, value in adds:
            total[col] += value
        return carry

    lax.fori_loop(0, (info[0] + UNROLL - 1) // UNROLL, step, 0)
    for zl in range(NZL):
        for sub in range(4):
            mine[zl, sub] = total[(2 * zl + my_core) * 4 + sub]
            theirs[zl, sub] = total[(2 * zl + 1 - my_core) * 4 + sub]


def backward_kernel(info, code, cols, weights, back, total):
    total[...] = jnp.zeros_like(total)

    def step(i, carry):
        adds = []
        for u in range(UNROLL):
            c = i * UNROLL + u
            word = code[c]
            w = weights[c].reshape(BS, BS)
            value = lax.dot_general(cols[word >> 12], w, (((1,), (1,)), ((), ())), preferred_element_type=f32)
            adds.append(((word >> 8) & 15, value))
        for r, value in adds:
            total[r] += value
        return carry

    lax.fori_loop(0, (info[0] + UNROLL - 1) // UNROLL, step, 0)
    for r in range(total.shape[0]):
        back[:, r * BS : (r + 1) * BS] = total[r].astype(bf16)


def chip_kernel(info, mine, came, own, s1, s2, s3):
    my_zl = info[4]
    own[...] = mine[my_zl] + came[my_zl]
    for k, out in enumerate((s1, s2, s3)):
        zl = (my_zl + k + 1) % NZL
        out[...] = (mine[zl] + came[zl]).astype(bf16)


def project_kernel(own, r1, r2, r3, out):
    for sub in range(4):
        value = own[sub] + r1[sub].astype(f32) + r2[sub].astype(f32) + r3[sub].astype(f32)
        out[:, sub * BS : (sub + 1) * BS] = value.astype(bf16)


def adam_kernel(place, stacked, came, new_w, new_m, new_v, rows, grad):
    slots, share = new_w.shape
    places = came.shape[0] * PAIR
    width = stacked.shape[1] // BS
    for j in range(slots):
        word = jnp.maximum(place[j] - 1, 0)
        g, row = word % places, word // places
        filled = place[j] > 0
        here = row < slots
        entry = jnp.maximum(row - slots, 0)
        own = stacked[pl.ds(jnp.minimum(row, slots - 1), 1), :]
        for n in range(width):
            lanes = slice(n * BS, (n + 1) * BS)
            moved = came[entry // MV, pl.ds(2 * PAIR + width * (entry % MV) + n, 1), :]
            rows[j : j + 1, lanes] = jnp.where(filled, jnp.where(here, own[:, lanes], moved), 0.0)
        for b in range(2):
            value = came[g // PAIR, pl.ds(2 * (g % PAIR) + b, 1), :]
            grad[j : j + 1, b * BS : (b + 1) * BS] = jnp.where(filled, value, 0.0)
    w, m, v = adam_update(rows[:, :share], rows[:, share : 2 * share], rows[:, 2 * share :], grad[...])
    new_w[...] = w
    new_m[...] = m
    new_v[...] = v


def all_to_all(values, axis):
    return lax.all_to_all(values, axis, split_axis=0, concat_axis=0, tiled=True)


def shift(values, axis, count, step):
    return lax.ppermute(values, axis, [(i, (i + step) % count) for i in range(count)])


def shards(
    hidden,
    out_grad,
    block_weight,
    block_row,
    block_col,
    live_count,
    new_owner,
    new_slot,
    first_moment,
    second_moment,
):
    shard_count = lax.axis_size(SHARD)
    me = lax.axis_index(SHARD)
    dp_index = lax.axis_index(DP)
    x_index = lax.axis_index("x")
    tokens = hidden.shape[0]
    slot_count = block_weight.shape[1]
    row_local = hidden.shape[1] // BS
    share = first_moment.shape[2]
    scale = 1.0 / math.sqrt(tokens * lax.axis_size(DP))

    mine = all_to_all(jnp.broadcast_to(out_grad[None], (NZL,) + out_grad.shape), "zl")
    other = shift(mine, "core", 2, 1)
    quarter = lax.dynamic_slice_in_dim(block_weight[0], x_index * (BS // NX), BS // NX, 1)
    gathered = lax.all_gather(quarter, SHARD, axis=0, tiled=True)
    weight_share = lax.dynamic_slice_in_dim(block_weight[0], dp_index * 2, 2, 1).reshape(slot_count, share)
    stacked = jnp.concatenate([weight_share.astype(f32), first_moment[0], second_moment[0]], axis=1)

    fits, code, counts, send, state_send, place = make_plan(
        block_row, block_col, live_count, new_owner, new_slot, row_local, me
    )
    info = jnp.stack(counts + [lax.axis_index("core"), x_index, lax.axis_index("zl")])

    partial, cols = call(
        grad_kernel,
        (like((NX, NY * NZH * 2, GCAP, BS), bf16), like((shard_count * 4, BS, BS), bf16)),
        2,
        3,
        [pltpu.VMEM((row_local, BS, BS), bf16), pltpu.VMEM((BS * GCAP, BS), f32)],
        flops=2 * WCAP * BS**3,
        byts=4 * 1024 * 1024,
    )(info, code, hidden, mine, other)
    along_x = all_to_all(partial, "x")
    summed = call(sum_kernel, like(partial.shape[1:], bf16), 0, 1, byts=2 * 1024 * 1024)(along_x)
    along_yz = all_to_all(summed.reshape(NY * NZH, 2, GCAP, BS), ("y", "zh"))
    shares = call(
        functools.partial(share_kernel, scale),
        like((shard_count, 2 * PAIR + MV * stacked.shape[1] // BS, BS), f32),
        2,
        2,
        [pltpu.VMEM((2, GCAP, BS), f32)],
        byts=1024 * 1024,
    )(send, state_send, along_yz, stacked)
    shares = all_to_all(shares, SHARD)

    w0 = call(select_kernel, like((WCAP, BS // NX, BS), bf16), 2, 1, byts=1024 * 1024)(info, code, gathered)
    w1, w2, w3 = (shift(w0, "x", NX, k) for k in (1, 2, 3))

    out_mine, out_theirs, weights = call(
        forward_kernel,
        (
            like((NZL, 4, tokens, BS), f32),
            like((NZL, 4, tokens, BS), f32),
            like((WCAP, NX, BS // NX, BS), bf16),
        ),
        2,
        5,
        [pltpu.VMEM((shard_count * 4, tokens, BS), f32)],
        flops=2 * WCAP * BS**3,
        byts=8 * 1024 * 1024,
    )(info, code, hidden, w0, w1, w2, w3)
    came = shift(out_theirs, "core", 2, 1)
    hidden_grad = call(
        backward_kernel,
        like(hidden.shape, bf16),
        2,
        2,
        [pltpu.VMEM((row_local, tokens, BS), f32)],
        flops=2 * WCAP * BS**3,
        byts=4 * 1024 * 1024,
    )(info, code, cols, weights)
    part = (4, tokens, BS)
    own, s1, s2, s3 = call(
        chip_kernel, (like(part, f32),) + (like(part, bf16),) * 3, 1, 2, byts=3 * 1024 * 1024
    )(info, out_mine, came)
    r1, r2, r3 = (shift(s, "zl", NZL, k + 1) for k, s in enumerate((s1, s2, s3)))
    r1, r2, r3, hidden_grad = lax.optimization_barrier((r1, r2, r3, hidden_grad))
    projected = call(project_kernel, like(out_grad.shape, bf16), 0, 4, byts=1024 * 1024)(own, r1, r2, r3)

    shape = like((slot_count, share), f32)
    new_weight, new_first, new_second = call(
        adam_kernel,
        (shape, shape, shape),
        1,
        2,
        [pltpu.VMEM((slot_count, 3 * share), f32), pltpu.VMEM((slot_count, share), f32)],
        byts=1024 * 1024,
    )(place, stacked, shares)
    result = (projected, hidden_grad, new_weight[None], new_first[None], new_second[None])
    return lax.cond(
        fits,
        lambda: result,
        lambda: general(
            hidden,
            out_grad,
            block_weight,
            block_row,
            block_col,
            live_count,
            new_owner,
            new_slot,
            first_moment,
            second_moment,
        ),
    )


def solution(mesh):
    split = Mesh(mesh.devices.reshape(NY, NX, NZH, NZL, 2), ("y", "x", "zh", "zl", "core"))
    in_specs = (
        P(DP, SHARD),
        P(DP, SHARD),
        P(SHARD, None, None, None),
        P(),
        P(),
        P(),
        P(),
        P(),
        P(SHARD, None, DP),
        P(SHARD, None, DP),
    )
    out_specs = (
        P(DP, SHARD),
        P(DP, SHARD),
        P(SHARD, None, DP),
        P(SHARD, None, DP),
        P(SHARD, None, DP),
    )
    return jax.shard_map(shards, mesh=split, in_specs=in_specs, out_specs=out_specs, check_vma=False)
```

```python
import functools
import math

import jax
import jax.numpy as jnp
from jax import lax
from jax.experimental import pallas as pl
from jax.experimental.pallas import tpu as pltpu
from jax.sharding import Mesh, PartitionSpec as P

DP = ("y", "x", "zh")
SHARD = ("zl", "core")
MV = 2


LEARN_RATE = 0.01
BETA_ONE = 0.9
BETA_TWO = 0.95
EPSILON = 1e-08


def adam_update(weight, first_state, second_state, gradient):
    first_state = BETA_ONE * first_state + (1.0 - BETA_ONE) * gradient
    second_state = BETA_TWO * second_state + (1.0 - BETA_TWO) * gradient * gradient
    weight = weight - LEARN_RATE * first_state / (jnp.sqrt(second_state) + EPSILON)
    return (weight, first_state, second_state)


def send_positions(owner_devices, shard_count, slot_count):
    sources = jnp.arange(shard_count, dtype=jnp.int32)[:, None]
    moving = (owner_devices >= 0) & (owner_devices != sources)
    slot_ids = jnp.arange(slot_count)
    earlier = slot_ids[None, :] < slot_ids[:, None]
    matches = (
        (owner_devices[:, :, None] == owner_devices[:, None, :])
        & moving[:, None, :]
        & earlier[None, :, :]
    )
    return (moving, jnp.sum(matches, axis=2))


def pack_moving(values, owner_row, moving_row, position_row, shard_count, capacity):
    slot_ids = jnp.arange(values.shape[0], dtype=jnp.int32)
    targets = owner_row * capacity + position_row
    entries = jnp.arange(shard_count * capacity, dtype=jnp.int32)
    matches = (targets[None, :] == entries[:, None]) & moving_row[None, :]
    source = jnp.sum(jnp.where(matches, slot_ids[None, :], 0), axis=1)
    filled = jnp.any(matches, axis=1)
    packed = jnp.where(filled[:, None], jnp.take(values, source, axis=0), 0.0)
    return packed.reshape(shard_count, capacity, values.shape[1])


def place_blocks(
    received,
    own_values,
    owner_devices,
    destination_slot_list,
    moving,
    positions,
    my_index,
    capacity,
):
    shard_count, slot_count = owner_devices.shape
    slot_ids = jnp.arange(slot_count, dtype=jnp.int32)
    entries = (jnp.arange(shard_count, dtype=jnp.int32)[:, None] * capacity + positions).reshape(-1)
    to_me = (moving & (owner_devices == my_index)).reshape(-1)
    matches = to_me[None, :] & (destination_slot_list.reshape(-1)[None, :] == slot_ids[:, None])
    arrived = jnp.any(matches, axis=1)
    from_entry = jnp.sum(jnp.where(matches, entries[None, :], 0), axis=1)
    flattened = received.reshape(shard_count * capacity, received.shape[2])
    arrival_rows = jnp.take(flattened, from_entry, axis=0)
    stay_hit = (owner_devices[my_index] == my_index)[None, :] & (
        destination_slot_list[my_index][None, :] == slot_ids[:, None]
    )
    stayed = jnp.any(stay_hit, axis=1)
    from_slot = jnp.sum(jnp.where(stay_hit, slot_ids[None, :], 0), axis=1)
    kept_rows = jnp.take(own_values, from_slot, axis=0)
    return jnp.where(arrived[:, None], arrival_rows, jnp.where(stayed[:, None], kept_rows, 0.0))


def local_place(block_ids, first_id, local_count):
    local_ids = block_ids - first_id
    inside = (local_ids >= 0) & (local_ids < local_count)
    return jnp.where(inside, local_ids, local_count)


def general(
    hidden,
    out_grad,
    block_weight,
    block_row,
    block_col,
    live_count,
    new_owner,
    new_slot,
    first_moment,
    second_moment,
):
    shard_count = lax.axis_size(SHARD)
    dp_count = lax.axis_size(DP)
    my_index = lax.axis_index(SHARD)
    dp_index = lax.axis_index(DP)
    tokens_dev = hidden.shape[0]
    slot_count = block_weight.shape[1]
    block_size = block_weight.shape[2]
    share_size = first_moment.shape[2]
    row_blocks = hidden.shape[1] * shard_count // block_size
    col_blocks = out_grad.shape[1] * shard_count // block_size
    grad_scale = 1.0 / math.sqrt(tokens_dev * dp_count)
    slot_ids = jnp.arange(slot_count)
    live_all = slot_ids[None, :] < live_count[:, None]
    my_live = live_all[my_index]
    my_rows = block_row[my_index]
    my_cols = block_col[my_index]
    zero_bf = jnp.zeros((), jnp.bfloat16)
    full_hidden, full_grad = (
        lax.all_gather(hidden, SHARD, axis=1, tiled=True),
        lax.all_gather(out_grad, SHARD, axis=1, tiled=True),
    )
    hidden_blocks = full_hidden.reshape(tokens_dev, row_blocks, block_size)
    grad_blocks = full_grad.reshape(tokens_dev, col_blocks, block_size)
    own_hidden = jnp.take(hidden_blocks, my_rows, axis=1)
    own_grad = jnp.take(grad_blocks, my_cols, axis=1)
    grad_share = None
    col_local = col_blocks // shard_count
    row_local = row_blocks // shard_count

    def one_shard(totals, member):
        blocks, shard_index = member
        row_ids = block_row[shard_index]
        col_ids = block_col[shard_index]
        weights = jnp.where(live_all[shard_index][:, None, None], blocks, zero_bf)
        hidden_part = jnp.take(hidden_blocks, row_ids, axis=1)
        grad_part = jnp.take(grad_blocks, col_ids, axis=1)
        forward = jnp.einsum(
            "tkr,krc->tkc", hidden_part, weights, preferred_element_type=jnp.float32
        )
        backward = jnp.einsum(
            "tkc,krc->tkr", grad_part, weights, preferred_element_type=jnp.float32
        )
        col_place = local_place(col_ids, my_index * col_local, col_local)
        row_place = local_place(row_ids, my_index * row_local, row_local)
        out_total = totals[0].at[:, col_place].add(forward, mode="drop")
        back_total = totals[1].at[:, row_place].add(backward, mode="drop")
        return ((out_total, back_total), None)

    initial = (
        jnp.zeros((tokens_dev, col_local, block_size), jnp.float32),
        jnp.zeros((tokens_dev, row_local, block_size), jnp.float32),
    )
    totals = initial
    blocks_in = lax.all_gather(block_weight, SHARD, axis=0, tiled=True)
    indices = jnp.arange(blocks_in.shape[0], dtype=jnp.int32)
    totals, unused = lax.scan(one_shard, totals, (blocks_in, indices))
    out_total, back_total = totals
    projected = out_total.reshape(tokens_dev, col_local * block_size).astype(jnp.bfloat16)
    hidden_grad = back_total.reshape(tokens_dev, row_local * block_size).astype(jnp.bfloat16)
    blocks = (
        jnp.einsum("tkr,tkc->krc", own_hidden, own_grad, preferred_element_type=jnp.float32)
        * grad_scale
    )
    blocks = jnp.where(my_live[:, None, None], blocks, 0.0)
    grad_share = lax.psum_scatter(
        blocks.reshape(slot_count, block_size * block_size), DP, scatter_dimension=1, tiled=True
    )
    moving, positions = send_positions(new_owner, shard_count, slot_count)
    my_owner = new_owner[my_index]
    my_moving = moving[my_index]
    my_positions = positions[my_index]
    flat_weight = block_weight[0].reshape(slot_count, block_size * block_size)
    weight_share = lax.dynamic_slice_in_dim(
        flat_weight, dp_index * share_size, share_size, 1
    ).astype(jnp.float32)
    updated, first_state, second_state = adam_update(
        weight_share, first_moment[0], second_moment[0], grad_share
    )
    stacked = jnp.concatenate([updated, first_state, second_state], axis=1)
    packed = pack_moving(stacked, my_owner, my_moving, my_positions, shard_count, MV)
    received = lax.all_to_all(packed, SHARD, split_axis=0, concat_axis=0, tiled=True)
    placed = place_blocks(received, stacked, new_owner, new_slot, moving, positions, my_index, MV)
    new_weight = placed[:, :share_size]
    new_first = placed[:, share_size : 2 * share_size]
    new_second = placed[:, 2 * share_size :]
    return (projected, hidden_grad, new_weight[None], new_first[None], new_second[None])


WCAP = 44
GCAP = 40
PAIR = 14
UNROLL = 4
NX, NY, NZH, NZL = 4, 8, 2, 4
BS = 128
VMEM_LIMIT = 14 * 1024 * 1024
f32 = jnp.float32
bf16 = jnp.bfloat16
i32 = jnp.int32


def call(kernel, outs, n_smem, n_vmem, scratch=(), flops=0, byts=0, n_after=0):
    smem = pl.BlockSpec(memory_space=pltpu.SMEM)
    vmem = pl.BlockSpec(memory_space=pltpu.VMEM)
    return pl.pallas_call(
        kernel,
        out_shape=outs,
        in_specs=[smem] * n_smem + [vmem] * n_vmem + [pl.BlockSpec(memory_space=pl.ANY)] * n_after,
        out_specs=jax.tree.map(lambda _: vmem, outs),
        scratch_shapes=list(scratch),
        compiler_params=pltpu.CompilerParams(vmem_limit_bytes=VMEM_LIMIT),
        cost_estimate=pl.CostEstimate(flops=flops, bytes_accessed=byts, transcendentals=0),
    )


def like(shape, dtype):
    return jax.ShapeDtypeStruct(shape, dtype)


def make_plan(block_row, block_col, live_count, new_owner, new_slot, row_local, me):
    shard_count, slot_count = block_row.shape
    total = shard_count * slot_count
    ids = jnp.arange(total, dtype=i32)
    live = (jnp.arange(slot_count)[None, :] < live_count[:, None]).reshape(total)
    row = block_row.reshape(total)
    col = block_col.reshape(total)
    owner = jnp.where(live, new_owner.reshape(total), -1)
    slot = new_slot.reshape(total)
    kept = owner >= 0
    row_shard = row // row_local
    key = jnp.where(kept, ids, ids + total)
    same = row_shard[:, None] == row_shard[None, :]
    before = same & live[None, :] & (key[None, :] < key[:, None])
    rank = jnp.sum(before.astype(i32), axis=1)
    earlier = same & (owner[:, None] == owner[None, :]) & (ids[None, :] < ids[:, None])
    pos = jnp.sum(earlier.astype(i32), axis=1)
    fits = (
        (jnp.max(jnp.where(live, rank, 0)) < WCAP)
        & (jnp.max(jnp.where(kept, rank, 0)) < GCAP)
        & (jnp.max(jnp.where(kept, pos, 0)) < PAIR)
    )

    here = live & (row_shard == me)
    words = ids + 256 * ((row - row_local * me) + 16 * col)
    hit = here[None, :] & (rank[None, :] == jnp.arange(WCAP)[:, None])
    code = jnp.sum(jnp.where(hit, words[None, :], 0), axis=1)
    counts = [jnp.minimum(jnp.sum(here.astype(i32)), WCAP), jnp.minimum(jnp.sum((here & kept).astype(i32)), GCAP)]
    going = jnp.where(here & kept, owner * PAIR + pos, -1)
    send_hit = going[None, :] == jnp.arange(shard_count * PAIR)[:, None]
    send = jnp.minimum(jnp.sum(jnp.where(send_hit, rank[None, :], 0), axis=1), GCAP - 1)
    owner2 = owner.reshape(shard_count, slot_count)
    sources = jnp.arange(shard_count, dtype=i32)[:, None]
    slots = jnp.arange(slot_count, dtype=i32)[None, :]
    moving, positions = send_positions(owner2, shard_count, slot_count)
    target = jnp.where(moving & (sources == me), owner2 * MV + positions, -1).reshape(total)
    state_hit = target[None, :] == jnp.arange(shard_count * MV)[:, None]
    state_send = jnp.sum(jnp.where(state_hit, (ids % slot_count)[None, :], 0), axis=1)
    state_row = jnp.where(sources == me, slots, slot_count + sources * MV + positions).reshape(total)
    landing = 1 + row_shard * PAIR + jnp.minimum(pos, PAIR - 1) + shard_count * PAIR * state_row
    lands = (owner == me)[None, :] & (slot[None, :] == jnp.arange(slot_count)[:, None])
    place = jnp.sum(jnp.where(lands, landing[None, :], 0), axis=1)
    return fits, code, counts, send, state_send, place


def grad_kernel(info, code, hidden, mine, other, out, cols, hidden_t, total):
    my_core = info[2]
    for zl in range(NZL):
        for sub in range(4):
            lanes = slice(sub * BS, (sub + 1) * BS)
            cols[(2 * zl + my_core) * 4 + sub] = mine[zl, :, lanes]
            cols[(2 * zl + 1 - my_core) * 4 + sub] = other[zl, :, lanes]
    row_local = hidden.shape[1] // BS
    for r in range(row_local):
        hidden_t[r] = hidden[:, r * BS : (r + 1) * BS].T

    def step(i, carry):
        blocks = []
        for u in range(UNROLL):
            word = code[i * UNROLL + u]
            blocks.append(jnp.dot(hidden_t[(word >> 8) & 15], cols[word >> 12], preferred_element_type=f32))
        for u in range(UNROLL):
            total[pl.ds(i * UNROLL + u, BS, stride=GCAP), :] = blocks[u]
        return carry

    lax.fori_loop(0, (info[1] + UNROLL - 1) // UNROLL, step, 0)
    for x in range(NX):
        for y in range(NY):
            for q in range(4):
                source = 16 * y + 4 * x + q
                out[x, 4 * y + q] = total[source * GCAP : (source + 1) * GCAP, :].astype(bf16)


def sum_kernel(parts, out):
    def step(i, carry):
        value = parts[0, i].astype(f32)
        for n in range(1, parts.shape[0]):
            value += parts[n, i].astype(f32)
        out[i] = value.astype(bf16)
        return carry

    lax.fori_loop(0, out.shape[0], step, 0, unroll=4)


def share_kernel(scale, send, state_send, parts, stacked, _after, out, total):
    for b in range(2):
        value = parts[0, b].astype(f32)
        for n in range(1, parts.shape[0]):
            value += parts[n, b].astype(f32)
        total[b] = value * scale
    width = stacked.shape[1] // BS
    for d in range(out.shape[0]):
        for p in range(PAIR):
            rank = send[d * PAIR + p]
            for b in range(2):
                out[d, 2 * p + b : 2 * p + b + 1, :] = total[b, pl.ds(rank, 1), :]
        for p in range(MV):
            row = stacked[pl.ds(state_send[d * MV + p], 1), :]
            for n in range(width):
                at = 2 * PAIR + width * p + n
                out[d, at : at + 1, :] = row[:, n * BS : (n + 1) * BS]


def select_kernel(info, code, gathered, out):
    def step(c, carry):
        value = gathered[code[c] & 255]
        out[c] = jnp.where(c < info[0], value, jnp.zeros_like(value))
        return carry

    lax.fori_loop(0, WCAP, step, 0, unroll=4)


def forward_kernel(info, code, hidden, w0, w1, w2, w3, _after, mine, theirs, weights, total):
    my_core, my_x = info[2], info[3]
    total[...] = jnp.zeros_like(total)

    def step(i, carry):
        adds = []
        for u in range(UNROLL):
            c = i * UNROLL + u
            word = code[c]
            for k, part in enumerate((w0, w1, w2, w3)):
                weights[c, (my_x + NX - k) % NX] = part[c]
            lanes = pl.ds(pl.multiple_of(((word >> 8) & 15) * BS, BS), BS)
            w = weights[c].reshape(BS, BS)
            adds.append((word >> 12, jnp.dot(hidden[:, lanes], w, preferred_element_type=f32)))
        for col, value in adds:
            total[col] += value
        return carry

    lax.fori_loop(0, (info[0] + UNROLL - 1) // UNROLL, step, 0)
    for zl in range(NZL):
        for sub in range(4):
            mine[zl, sub] = total[(2 * zl + my_core) * 4 + sub]
            theirs[zl, sub] = total[(2 * zl + 1 - my_core) * 4 + sub]


def backward_kernel(info, code, cols, weights, back, total):
    total[...] = jnp.zeros_like(total)

    def step(i, carry):
        adds = []
        for u in range(UNROLL):
            c = i * UNROLL + u
            word = code[c]
            w = weights[c].reshape(BS, BS)
            value = lax.dot_general(cols[word >> 12], w, (((1,), (1,)), ((), ())), preferred_element_type=f32)
            adds.append(((word >> 8) & 15, value))
        for r, value in adds:
            total[r] += value
        return carry

    lax.fori_loop(0, (info[0] + UNROLL - 1) // UNROLL, step, 0)
    for r in range(total.shape[0]):
        back[:, r * BS : (r + 1) * BS] = total[r].astype(bf16)


def chip_kernel(info, mine, came, _after, own, s1, s2, s3):
    my_zl = info[4]
    own[...] = mine[my_zl] + came[my_zl]
    for k, out in enumerate((s1, s2, s3)):
        zl = (my_zl + k + 1) % NZL
        out[...] = (mine[zl] + came[zl]).astype(bf16)


def project_kernel(own, r1, r2, r3, out):
    for sub in range(4):
        value = own[sub] + r1[sub].astype(f32) + r2[sub].astype(f32) + r3[sub].astype(f32)
        out[:, sub * BS : (sub + 1) * BS] = value.astype(bf16)


def adam_kernel(place, stacked, came, new_w, new_m, new_v, rows, grad):
    slots, share = new_w.shape
    places = came.shape[0] * PAIR
    width = stacked.shape[1] // BS
    for j in range(slots):
        word = jnp.maximum(place[j] - 1, 0)
        g, row = word % places, word // places
        filled = place[j] > 0
        here = row < slots
        entry = jnp.maximum(row - slots, 0)
        own = stacked[pl.ds(jnp.minimum(row, slots - 1), 1), :]
        for n in range(width):
            lanes = slice(n * BS, (n + 1) * BS)
            moved = came[entry // MV, pl.ds(2 * PAIR + width * (entry % MV) + n, 1), :]
            rows[j : j + 1, lanes] = jnp.where(filled, jnp.where(here, own[:, lanes], moved), 0.0)
        for b in range(2):
            value = came[g // PAIR, pl.ds(2 * (g % PAIR) + b, 1), :]
            grad[j : j + 1, b * BS : (b + 1) * BS] = jnp.where(filled, value, 0.0)
    w, m, v = adam_update(rows[:, :share], rows[:, share : 2 * share], rows[:, 2 * share :], grad[...])
    new_w[...] = w
    new_m[...] = m
    new_v[...] = v


def all_to_all(values, axis):
    return lax.all_to_all(values, axis, split_axis=0, concat_axis=0, tiled=True)


def shift(values, axis, count, step):
    return lax.ppermute(values, axis, [(i, (i + step) % count) for i in range(count)])


def shards(
    hidden,
    out_grad,
    block_weight,
    block_row,
    block_col,
    live_count,
    new_owner,
    new_slot,
    first_moment,
    second_moment,
):
    shard_count = lax.axis_size(SHARD)
    me = lax.axis_index(SHARD)
    dp_index = lax.axis_index(DP)
    x_index = lax.axis_index("x")
    tokens = hidden.shape[0]
    slot_count = block_weight.shape[1]
    row_local = hidden.shape[1] // BS
    share = first_moment.shape[2]
    scale = 1.0 / math.sqrt(tokens * lax.axis_size(DP))

    mine = all_to_all(jnp.broadcast_to(out_grad[None], (NZL,) + out_grad.shape), "zl")
    other = shift(mine, "core", 2, 1)
    quarter = lax.dynamic_slice_in_dim(block_weight[0], x_index * (BS // NX), BS // NX, 1)
    gathered = lax.all_gather(quarter, SHARD, axis=0, tiled=True)
    weight_share = lax.dynamic_slice_in_dim(block_weight[0], dp_index * 2, 2, 1).reshape(slot_count, share)
    stacked = jnp.concatenate([weight_share.astype(f32), first_moment[0], second_moment[0]], axis=1)

    fits, code, counts, send, state_send, place = make_plan(
        block_row, block_col, live_count, new_owner, new_slot, row_local, me
    )
    info = jnp.stack(counts + [lax.axis_index("core"), x_index, lax.axis_index("zl")])

    partial, cols = call(
        grad_kernel,
        (like((NX, NY * NZH * 2, GCAP, BS), bf16), like((shard_count * 4, BS, BS), bf16)),
        2,
        3,
        [pltpu.VMEM((row_local, BS, BS), bf16), pltpu.VMEM((BS * GCAP, BS), f32)],
        flops=2 * WCAP * BS**3,
        byts=4 * 1024 * 1024,
    )(info, code, hidden, mine, other)
    along_x = all_to_all(partial, "x")
    summed = call(sum_kernel, like(partial.shape[1:], bf16), 0, 1, byts=2 * 1024 * 1024)(along_x)
    along_yz = all_to_all(summed.reshape(NY * NZH, 2, GCAP, BS), ("y", "zh"))

    w0 = call(select_kernel, like((WCAP, BS // NX, BS), bf16), 2, 1, byts=1024 * 1024)(info, code, gathered)
    w2, w1, w3 = (shift(w0, "x", NX, k) for k in (2, 1, 3))

    out_mine, out_theirs, weights = call(
        forward_kernel,
        (
            like((NZL, 4, tokens, BS), f32),
            like((NZL, 4, tokens, BS), f32),
            like((WCAP, NX, BS // NX, BS), bf16),
        ),
        2,
        5,
        [pltpu.VMEM((shard_count * 4, tokens, BS), f32)],
        flops=2 * WCAP * BS**3,
        byts=8 * 1024 * 1024,
        n_after=1,
    )(info, code, hidden, w0, w1, w2, w3, summed)
    came = shift(out_theirs, "core", 2, 1)
    hidden_grad = call(
        backward_kernel,
        like(hidden.shape, bf16),
        2,
        2,
        [pltpu.VMEM((row_local, tokens, BS), f32)],
        flops=2 * WCAP * BS**3,
        byts=4 * 1024 * 1024,
    )(info, code, cols, weights)
    part = (4, tokens, BS)
    own, s1, s2, s3 = call(
        chip_kernel, (like(part, f32),) + (like(part, bf16),) * 3, 1, 2, byts=3 * 1024 * 1024, n_after=1
    )(info, out_mine, came, hidden_grad)
    shares = call(
        functools.partial(share_kernel, scale),
        like((shard_count, 2 * PAIR + MV * stacked.shape[1] // BS, BS), f32),
        2,
        2,
        [pltpu.VMEM((2, GCAP, BS), f32)],
        byts=1024 * 1024,
        n_after=1,
    )(send, state_send, along_yz, stacked, s1)
    shares = all_to_all(shares, SHARD)
    r2, r1, r3 = (shift(s, "zl", NZL, k) for k, s in ((2, s2), (1, s1), (3, s3)))
    projected = call(project_kernel, like(out_grad.shape, bf16), 0, 4, byts=1024 * 1024)(own, r1, r2, r3)

    shape = like((slot_count, share), f32)
    new_weight, new_first, new_second = call(
        adam_kernel,
        (shape, shape, shape),
        1,
        2,
        [pltpu.VMEM((slot_count, 3 * share), f32), pltpu.VMEM((slot_count, share), f32)],
        byts=1024 * 1024,
    )(place, stacked, shares)
    result = (projected, hidden_grad, new_weight[None], new_first[None], new_second[None])
    return lax.cond(
        fits,
        lambda: result,
        lambda: general(
            hidden,
            out_grad,
            block_weight,
            block_row,
            block_col,
            live_count,
            new_owner,
            new_slot,
            first_moment,
            second_moment,
        ),
    )


def solution(mesh):
    split = Mesh(mesh.devices.reshape(NY, NX, NZH, NZL, 2), ("y", "x", "zh", "zl", "core"))
    in_specs = (
        P(DP, SHARD),
        P(DP, SHARD),
        P(SHARD, None, None, None),
        P(),
        P(),
        P(),
        P(),
        P(),
        P(SHARD, None, DP),
        P(SHARD, None, DP),
    )
    out_specs = (
        P(DP, SHARD),
        P(DP, SHARD),
        P(SHARD, None, DP),
        P(SHARD, None, DP),
        P(SHARD, None, DP),
    )
    return jax.shard_map(shards, mesh=split, in_specs=in_specs, out_specs=out_specs, check_vma=False)
```

```python
import functools
import math

import jax
import jax.numpy as jnp
from jax import lax
from jax.experimental import pallas as pl
from jax.experimental.pallas import tpu as pltpu
from jax.sharding import Mesh, PartitionSpec as P

DP = ("y", "x", "zh")
SHARD = ("zl", "core")
MV = 2


LEARN_RATE = 0.01
BETA_ONE = 0.9
BETA_TWO = 0.95
EPSILON = 1e-08


def adam_update(weight, first_state, second_state, gradient):
    first_state = BETA_ONE * first_state + (1.0 - BETA_ONE) * gradient
    second_state = BETA_TWO * second_state + (1.0 - BETA_TWO) * gradient * gradient
    weight = weight - LEARN_RATE * first_state / (jnp.sqrt(second_state) + EPSILON)
    return (weight, first_state, second_state)


def send_positions(owner_devices, shard_count, slot_count):
    sources = jnp.arange(shard_count, dtype=jnp.int32)[:, None]
    moving = (owner_devices >= 0) & (owner_devices != sources)
    slot_ids = jnp.arange(slot_count)
    earlier = slot_ids[None, :] < slot_ids[:, None]
    matches = (
        (owner_devices[:, :, None] == owner_devices[:, None, :])
        & moving[:, None, :]
        & earlier[None, :, :]
    )
    return (moving, jnp.sum(matches, axis=2))


def pack_moving(values, owner_row, moving_row, position_row, shard_count, capacity):
    slot_ids = jnp.arange(values.shape[0], dtype=jnp.int32)
    targets = owner_row * capacity + position_row
    entries = jnp.arange(shard_count * capacity, dtype=jnp.int32)
    matches = (targets[None, :] == entries[:, None]) & moving_row[None, :]
    source = jnp.sum(jnp.where(matches, slot_ids[None, :], 0), axis=1)
    filled = jnp.any(matches, axis=1)
    packed = jnp.where(filled[:, None], jnp.take(values, source, axis=0), 0.0)
    return packed.reshape(shard_count, capacity, values.shape[1])


def place_blocks(
    received,
    own_values,
    owner_devices,
    destination_slot_list,
    moving,
    positions,
    my_index,
    capacity,
):
    shard_count, slot_count = owner_devices.shape
    slot_ids = jnp.arange(slot_count, dtype=jnp.int32)
    entries = (jnp.arange(shard_count, dtype=jnp.int32)[:, None] * capacity + positions).reshape(-1)
    to_me = (moving & (owner_devices == my_index)).reshape(-1)
    matches = to_me[None, :] & (destination_slot_list.reshape(-1)[None, :] == slot_ids[:, None])
    arrived = jnp.any(matches, axis=1)
    from_entry = jnp.sum(jnp.where(matches, entries[None, :], 0), axis=1)
    flattened = received.reshape(shard_count * capacity, received.shape[2])
    arrival_rows = jnp.take(flattened, from_entry, axis=0)
    stay_hit = (owner_devices[my_index] == my_index)[None, :] & (
        destination_slot_list[my_index][None, :] == slot_ids[:, None]
    )
    stayed = jnp.any(stay_hit, axis=1)
    from_slot = jnp.sum(jnp.where(stay_hit, slot_ids[None, :], 0), axis=1)
    kept_rows = jnp.take(own_values, from_slot, axis=0)
    return jnp.where(arrived[:, None], arrival_rows, jnp.where(stayed[:, None], kept_rows, 0.0))


def local_place(block_ids, first_id, local_count):
    local_ids = block_ids - first_id
    inside = (local_ids >= 0) & (local_ids < local_count)
    return jnp.where(inside, local_ids, local_count)


def general(
    hidden,
    out_grad,
    block_weight,
    block_row,
    block_col,
    live_count,
    new_owner,
    new_slot,
    first_moment,
    second_moment,
):
    shard_count = lax.axis_size(SHARD)
    dp_count = lax.axis_size(DP)
    my_index = lax.axis_index(SHARD)
    dp_index = lax.axis_index(DP)
    tokens_dev = hidden.shape[0]
    slot_count = block_weight.shape[1]
    block_size = block_weight.shape[2]
    share_size = first_moment.shape[2]
    row_blocks = hidden.shape[1] * shard_count // block_size
    col_blocks = out_grad.shape[1] * shard_count // block_size
    grad_scale = 1.0 / math.sqrt(tokens_dev * dp_count)
    slot_ids = jnp.arange(slot_count)
    live_all = slot_ids[None, :] < live_count[:, None]
    my_live = live_all[my_index]
    my_rows = block_row[my_index]
    my_cols = block_col[my_index]
    zero_bf = jnp.zeros((), jnp.bfloat16)
    full_hidden, full_grad = (
        lax.all_gather(hidden, SHARD, axis=1, tiled=True),
        lax.all_gather(out_grad, SHARD, axis=1, tiled=True),
    )
    hidden_blocks = full_hidden.reshape(tokens_dev, row_blocks, block_size)
    grad_blocks = full_grad.reshape(tokens_dev, col_blocks, block_size)
    own_hidden = jnp.take(hidden_blocks, my_rows, axis=1)
    own_grad = jnp.take(grad_blocks, my_cols, axis=1)
    grad_share = None
    col_local = col_blocks // shard_count
    row_local = row_blocks // shard_count

    def one_shard(totals, member):
        blocks, shard_index = member
        row_ids = block_row[shard_index]
        col_ids = block_col[shard_index]
        weights = jnp.where(live_all[shard_index][:, None, None], blocks, zero_bf)
        hidden_part = jnp.take(hidden_blocks, row_ids, axis=1)
        grad_part = jnp.take(grad_blocks, col_ids, axis=1)
        forward = jnp.einsum(
            "tkr,krc->tkc", hidden_part, weights, preferred_element_type=jnp.float32
        )
        backward = jnp.einsum(
            "tkc,krc->tkr", grad_part, weights, preferred_element_type=jnp.float32
        )
        col_place = local_place(col_ids, my_index * col_local, col_local)
        row_place = local_place(row_ids, my_index * row_local, row_local)
        out_total = totals[0].at[:, col_place].add(forward, mode="drop")
        back_total = totals[1].at[:, row_place].add(backward, mode="drop")
        return ((out_total, back_total), None)

    initial = (
        jnp.zeros((tokens_dev, col_local, block_size), jnp.float32),
        jnp.zeros((tokens_dev, row_local, block_size), jnp.float32),
    )
    totals = initial
    blocks_in = lax.all_gather(block_weight, SHARD, axis=0, tiled=True)
    indices = jnp.arange(blocks_in.shape[0], dtype=jnp.int32)
    totals, unused = lax.scan(one_shard, totals, (blocks_in, indices))
    out_total, back_total = totals
    projected = out_total.reshape(tokens_dev, col_local * block_size).astype(jnp.bfloat16)
    hidden_grad = back_total.reshape(tokens_dev, row_local * block_size).astype(jnp.bfloat16)
    blocks = (
        jnp.einsum("tkr,tkc->krc", own_hidden, own_grad, preferred_element_type=jnp.float32)
        * grad_scale
    )
    blocks = jnp.where(my_live[:, None, None], blocks, 0.0)
    grad_share = lax.psum_scatter(
        blocks.reshape(slot_count, block_size * block_size), DP, scatter_dimension=1, tiled=True
    )
    moving, positions = send_positions(new_owner, shard_count, slot_count)
    my_owner = new_owner[my_index]
    my_moving = moving[my_index]
    my_positions = positions[my_index]
    flat_weight = block_weight[0].reshape(slot_count, block_size * block_size)
    weight_share = lax.dynamic_slice_in_dim(
        flat_weight, dp_index * share_size, share_size, 1
    ).astype(jnp.float32)
    updated, first_state, second_state = adam_update(
        weight_share, first_moment[0], second_moment[0], grad_share
    )
    stacked = jnp.concatenate([updated, first_state, second_state], axis=1)
    packed = pack_moving(stacked, my_owner, my_moving, my_positions, shard_count, MV)
    received = lax.all_to_all(packed, SHARD, split_axis=0, concat_axis=0, tiled=True)
    placed = place_blocks(received, stacked, new_owner, new_slot, moving, positions, my_index, MV)
    new_weight = placed[:, :share_size]
    new_first = placed[:, share_size : 2 * share_size]
    new_second = placed[:, 2 * share_size :]
    return (projected, hidden_grad, new_weight[None], new_first[None], new_second[None])


WCAP = 44
GCAP = 40
PAIR = 14
UNROLL = 4
NX, NY, NZH, NZL = 4, 8, 2, 4
BS = 128
VMEM_LIMIT = 14 * 1024 * 1024
f32 = jnp.float32
bf16 = jnp.bfloat16
i32 = jnp.int32


def call(kernel, outs, n_smem, n_vmem, scratch=(), flops=0, byts=0, n_after=0):
    smem = pl.BlockSpec(memory_space=pltpu.SMEM)
    vmem = pl.BlockSpec(memory_space=pltpu.VMEM)
    return pl.pallas_call(
        kernel,
        out_shape=outs,
        in_specs=[smem] * n_smem + [vmem] * n_vmem + [pl.BlockSpec(memory_space=pl.ANY)] * n_after,
        out_specs=jax.tree.map(lambda _: vmem, outs),
        scratch_shapes=list(scratch),
        compiler_params=pltpu.CompilerParams(vmem_limit_bytes=VMEM_LIMIT),
        cost_estimate=pl.CostEstimate(flops=flops, bytes_accessed=byts, transcendentals=0),
    )


def like(shape, dtype):
    return jax.ShapeDtypeStruct(shape, dtype)


def make_plan(block_row, block_col, live_count, new_owner, new_slot, row_local, me):
    shard_count, slot_count = block_row.shape
    total = shard_count * slot_count
    ids = jnp.arange(total, dtype=i32)
    live = (jnp.arange(slot_count)[None, :] < live_count[:, None]).reshape(total)
    row = block_row.reshape(total)
    col = block_col.reshape(total)
    owner = jnp.where(live, new_owner.reshape(total), -1)
    slot = new_slot.reshape(total)
    kept = owner >= 0
    row_shard = row // row_local
    key = jnp.where(kept, ids, ids + total)
    same = row_shard[:, None] == row_shard[None, :]
    before = same & live[None, :] & (key[None, :] < key[:, None])
    rank = jnp.sum(before.astype(i32), axis=1)
    earlier = same & (owner[:, None] == owner[None, :]) & (ids[None, :] < ids[:, None])
    pos = jnp.sum(earlier.astype(i32), axis=1)
    fits = (
        (jnp.max(jnp.where(live, rank, 0)) < WCAP)
        & (jnp.max(jnp.where(kept, rank, 0)) < GCAP)
        & (jnp.max(jnp.where(kept, pos, 0)) < PAIR)
    )

    here = live & (row_shard == me)
    words = ids + 256 * ((row - row_local * me) + 16 * col)
    hit = here[None, :] & (rank[None, :] == jnp.arange(WCAP)[:, None])
    code = jnp.sum(jnp.where(hit, words[None, :], 0), axis=1)
    counts = [jnp.minimum(jnp.sum(here.astype(i32)), WCAP), jnp.minimum(jnp.sum((here & kept).astype(i32)), GCAP)]
    going = jnp.where(here & kept, owner * PAIR + pos, -1)
    send_hit = going[None, :] == jnp.arange(shard_count * PAIR)[:, None]
    send = jnp.minimum(jnp.sum(jnp.where(send_hit, rank[None, :], 0), axis=1), GCAP - 1)
    owner2 = owner.reshape(shard_count, slot_count)
    sources = jnp.arange(shard_count, dtype=i32)[:, None]
    slots = jnp.arange(slot_count, dtype=i32)[None, :]
    moving, positions = send_positions(owner2, shard_count, slot_count)
    target = jnp.where(moving & (sources == me), owner2 * MV + positions, -1).reshape(total)
    state_hit = target[None, :] == jnp.arange(shard_count * MV)[:, None]
    state_send = jnp.sum(jnp.where(state_hit, (ids % slot_count)[None, :], 0), axis=1)
    state_row = jnp.where(sources == me, slots, slot_count + sources * MV + positions).reshape(total)
    landing = 1 + row_shard * PAIR + jnp.minimum(pos, PAIR - 1) + shard_count * PAIR * state_row
    lands = (owner == me)[None, :] & (slot[None, :] == jnp.arange(slot_count)[:, None])
    place = jnp.sum(jnp.where(lands, landing[None, :], 0), axis=1)
    return fits, code, counts, send, state_send, place


def grad_kernel(info, code, hidden, mine, other, out, cols, hidden_t, total):
    my_core = info[2]
    for zl in range(NZL):
        for sub in range(4):
            lanes = slice(sub * BS, (sub + 1) * BS)
            cols[(2 * zl + my_core) * 4 + sub] = mine[zl, :, lanes]
            cols[(2 * zl + 1 - my_core) * 4 + sub] = other[zl, :, lanes]
    row_local = hidden.shape[1] // BS
    for r in range(row_local):
        hidden_t[r] = hidden[:, r * BS : (r + 1) * BS].T

    def step(i, carry):
        blocks = []
        for u in range(UNROLL):
            word = code[i * UNROLL + u]
            blocks.append(jnp.dot(hidden_t[(word >> 8) & 15], cols[word >> 12], preferred_element_type=f32))
        for u in range(UNROLL):
            total[pl.ds(i * UNROLL + u, BS, stride=GCAP), :] = blocks[u]
        return carry

    lax.fori_loop(0, (info[1] + UNROLL - 1) // UNROLL, step, 0)
    for x in range(NX):
        for y in range(NY):
            for q in range(4):
                source = 16 * y + 4 * x + q
                out[x, 4 * y + q] = total[source * GCAP : (source + 1) * GCAP, :].astype(bf16)


def sum_kernel(info, parts, keep, send):
    my_zh = info[5]

    def step(i, carry):
        for out, zh in ((keep, my_zh), (send, 1 - my_zh)):
            for b in range(2):
                row = 4 * i + 2 * zh + b
                value = parts[0, row].astype(f32)
                for n in range(1, parts.shape[0]):
                    value += parts[n, row].astype(f32)
                out[i, b] = value.astype(out.dtype)
        return carry

    lax.fori_loop(0, keep.shape[0], step, 0, unroll=2)


def pair_kernel(keep, came, out):
    for i in range(keep.shape[0]):
        out[i] = (keep[i] + came[i].astype(f32)).astype(bf16)


def share_kernel(scale, send, state_send, parts, stacked, _after, out, total):
    for b in range(2):
        value = parts[0, b].astype(f32)
        for n in range(1, parts.shape[0]):
            value += parts[n, b].astype(f32)
        total[b] = value * scale
    width = stacked.shape[1] // BS
    for d in range(out.shape[0]):
        for p in range(PAIR):
            rank = send[d * PAIR + p]
            for b in range(2):
                out[d, 2 * p + b : 2 * p + b + 1, :] = total[b, pl.ds(rank, 1), :]
        for p in range(MV):
            row = stacked[pl.ds(state_send[d * MV + p], 1), :]
            for n in range(width):
                at = 2 * PAIR + width * p + n
                out[d, at : at + 1, :] = row[:, n * BS : (n + 1) * BS]


def select_kernel(info, code, gathered, _after, out):
    def step(c, carry):
        value = gathered[code[c] & 255]
        value = jnp.where(c < info[0], value, jnp.zeros_like(value))
        for x in range(NX):
            out[x, c] = value
        return carry

    lax.fori_loop(0, WCAP, step, 0, unroll=4)


def forward_kernel(info, code, hidden, quarters, _after, mine, theirs, weights, total):
    my_core = info[2]
    total[...] = jnp.zeros_like(total)

    def step(i, carry):
        adds = []
        for u in range(UNROLL):
            c = i * UNROLL + u
            word = code[c]
            for x in range(NX):
                weights[c, x] = quarters[x, c]
            lanes = pl.ds(pl.multiple_of(((word >> 8) & 15) * BS, BS), BS)
            w = weights[c].reshape(BS, BS)
            adds.append((word >> 12, jnp.dot(hidden[:, lanes], w, preferred_element_type=f32)))
        for col, value in adds:
            total[col] += value
        return carry

    lax.fori_loop(0, (info[0] + UNROLL - 1) // UNROLL, step, 0)
    for zl in range(NZL):
        for sub in range(4):
            mine[zl, sub] = total[(2 * zl + my_core) * 4 + sub]
            theirs[zl, sub] = total[(2 * zl + 1 - my_core) * 4 + sub]


def backward_kernel(info, code, cols, weights, back, total):
    total[...] = jnp.zeros_like(total)

    def step(i, carry):
        adds = []
        for u in range(UNROLL):
            c = i * UNROLL + u
            word = code[c]
            w = weights[c].reshape(BS, BS)
            value = lax.dot_general(cols[word >> 12], w, (((1,), (1,)), ((), ())), preferred_element_type=f32)
            adds.append(((word >> 8) & 15, value))
        for r, value in adds:
            total[r] += value
        return carry

    lax.fori_loop(0, (info[0] + UNROLL - 1) // UNROLL, step, 0)
    for r in range(total.shape[0]):
        back[:, r * BS : (r + 1) * BS] = total[r].astype(bf16)


def chip_kernel(info, mine, came, _after, own, s1, s2, s3):
    my_zl = info[4]
    own[...] = mine[my_zl] + came[my_zl]
    for k, out in enumerate((s1, s2, s3)):
        zl = (my_zl + k + 1) % NZL
        out[...] = (mine[zl] + came[zl]).astype(bf16)


def project_kernel(own, r1, r2, r3, out):
    for sub in range(4):
        value = own[sub] + r1[sub].astype(f32) + r2[sub].astype(f32) + r3[sub].astype(f32)
        out[:, sub * BS : (sub + 1) * BS] = value.astype(bf16)


def adam_kernel(place, stacked, came, new_w, new_m, new_v, rows, grad):
    slots, share = new_w.shape
    places = came.shape[0] * PAIR
    width = stacked.shape[1] // BS
    for j in range(slots):
        word = jnp.maximum(place[j] - 1, 0)
        g, row = word % places, word // places
        filled = place[j] > 0
        here = row < slots
        entry = jnp.maximum(row - slots, 0)
        own = stacked[pl.ds(jnp.minimum(row, slots - 1), 1), :]
        for n in range(width):
            lanes = slice(n * BS, (n + 1) * BS)
            moved = came[entry // MV, pl.ds(2 * PAIR + width * (entry % MV) + n, 1), :]
            rows[j : j + 1, lanes] = jnp.where(filled, jnp.where(here, own[:, lanes], moved), 0.0)
        for b in range(2):
            value = came[g // PAIR, pl.ds(2 * (g % PAIR) + b, 1), :]
            grad[j : j + 1, b * BS : (b + 1) * BS] = jnp.where(filled, value, 0.0)
    w, m, v = adam_update(rows[:, :share], rows[:, share : 2 * share], rows[:, 2 * share :], grad[...])
    new_w[...] = w
    new_m[...] = m
    new_v[...] = v


def all_to_all(values, axis):
    return lax.all_to_all(values, axis, split_axis=0, concat_axis=0, tiled=True)


def shift(values, axis, count, step):
    return lax.ppermute(values, axis, [(i, (i + step) % count) for i in range(count)])


def shards(
    hidden,
    out_grad,
    block_weight,
    block_row,
    block_col,
    live_count,
    new_owner,
    new_slot,
    first_moment,
    second_moment,
):
    shard_count = lax.axis_size(SHARD)
    me = lax.axis_index(SHARD)
    dp_index = lax.axis_index(DP)
    x_index = lax.axis_index("x")
    tokens = hidden.shape[0]
    slot_count = block_weight.shape[1]
    row_local = hidden.shape[1] // BS
    share = first_moment.shape[2]
    scale = 1.0 / math.sqrt(tokens * lax.axis_size(DP))

    mine = all_to_all(jnp.broadcast_to(out_grad[None], (NZL,) + out_grad.shape), "zl")
    other = shift(mine, "core", 2, 1)
    quarter = lax.dynamic_slice_in_dim(block_weight[0], x_index * (BS // NX), BS // NX, 1)
    gathered = lax.all_gather(quarter, SHARD, axis=0, tiled=True)
    weight_share = lax.dynamic_slice_in_dim(block_weight[0], dp_index * 2, 2, 1).reshape(slot_count, share)
    stacked = jnp.concatenate([weight_share.astype(f32), first_moment[0], second_moment[0]], axis=1)

    fits, code, counts, send, state_send, place = make_plan(
        block_row, block_col, live_count, new_owner, new_slot, row_local, me
    )
    info = jnp.stack(counts + [lax.axis_index("core"), x_index, lax.axis_index("zl"), lax.axis_index("zh")])

    partial, cols = call(
        grad_kernel,
        (like((NX, NY * NZH * 2, GCAP, BS), bf16), like((shard_count * 4, BS, BS), bf16)),
        2,
        3,
        [pltpu.VMEM((row_local, BS, BS), bf16), pltpu.VMEM((BS * GCAP, BS), f32)],
        flops=2 * WCAP * BS**3,
        byts=4 * 1024 * 1024,
    )(info, code, hidden, mine, other)
    along_x = all_to_all(partial, "x")
    part = (NY, 2, GCAP, BS)
    keep, send_zh = call(sum_kernel, (like(part, f32), like(part, bf16)), 1, 1, byts=2 * 1024 * 1024)(info, along_x)
    came_zh = shift(send_zh, "zh", NZH, 1)
    summed = call(pair_kernel, like(part, bf16), 0, 2, byts=1024 * 1024)(keep, came_zh)
    along_y = all_to_all(summed, "y")

    picked = call(select_kernel, like((NX, WCAP, BS // NX, BS), bf16), 2, 1, byts=1024 * 1024, n_after=1)(
        info, code, gathered, along_x
    )
    quarters = all_to_all(picked, "x")

    out_mine, out_theirs, weights = call(
        forward_kernel,
        (
            like((NZL, 4, tokens, BS), f32),
            like((NZL, 4, tokens, BS), f32),
            like((WCAP, NX, BS // NX, BS), bf16),
        ),
        2,
        2,
        [pltpu.VMEM((shard_count * 4, tokens, BS), f32)],
        flops=2 * WCAP * BS**3,
        byts=8 * 1024 * 1024,
        n_after=1,
    )(info, code, hidden, quarters, summed)
    came = shift(out_theirs, "core", 2, 1)
    hidden_grad = call(
        backward_kernel,
        like(hidden.shape, bf16),
        2,
        2,
        [pltpu.VMEM((row_local, tokens, BS), f32)],
        flops=2 * WCAP * BS**3,
        byts=4 * 1024 * 1024,
    )(info, code, cols, weights)
    part = (4, tokens, BS)
    own, s1, s2, s3 = call(
        chip_kernel, (like(part, f32),) + (like(part, bf16),) * 3, 1, 2, byts=3 * 1024 * 1024, n_after=1
    )(info, out_mine, came, hidden_grad)
    shares = call(
        functools.partial(share_kernel, scale),
        like((shard_count, 2 * PAIR + MV * stacked.shape[1] // BS, BS), f32),
        2,
        2,
        [pltpu.VMEM((2, GCAP, BS), f32)],
        byts=1024 * 1024,
        n_after=1,
    )(send, state_send, along_y, stacked, s1)
    shares = all_to_all(shares, SHARD)
    r2, r1, r3 = (shift(s, "zl", NZL, k) for k, s in ((2, s2), (1, s1), (3, s3)))
    projected = call(project_kernel, like(out_grad.shape, bf16), 0, 4, byts=1024 * 1024)(own, r1, r2, r3)

    shape = like((slot_count, share), f32)
    new_weight, new_first, new_second = call(
        adam_kernel,
        (shape, shape, shape),
        1,
        2,
        [pltpu.VMEM((slot_count, 3 * share), f32), pltpu.VMEM((slot_count, share), f32)],
        byts=1024 * 1024,
    )(place, stacked, shares)
    result = (projected, hidden_grad, new_weight[None], new_first[None], new_second[None])
    return lax.cond(
        fits,
        lambda: result,
        lambda: general(
            hidden,
            out_grad,
            block_weight,
            block_row,
            block_col,
            live_count,
            new_owner,
            new_slot,
            first_moment,
            second_moment,
        ),
    )


def solution(mesh):
    split = Mesh(mesh.devices.reshape(NY, NX, NZH, NZL, 2), ("y", "x", "zh", "zl", "core"))
    in_specs = (
        P(DP, SHARD),
        P(DP, SHARD),
        P(SHARD, None, None, None),
        P(),
        P(),
        P(),
        P(),
        P(),
        P(SHARD, None, DP),
        P(SHARD, None, DP),
    )
    out_specs = (
        P(DP, SHARD),
        P(DP, SHARD),
        P(SHARD, None, DP),
        P(SHARD, None, DP),
        P(SHARD, None, DP),
    )
    return jax.shard_map(shards, mesh=split, in_specs=in_specs, out_specs=out_specs, check_vma=False)
```

```python
import functools
import math

import jax
import jax.numpy as jnp
from jax import lax
from jax.experimental import pallas as pl
from jax.experimental.pallas import tpu as pltpu
from jax.sharding import Mesh, PartitionSpec as P

DP = ("y", "x", "zh")
SHARD = ("zl", "core")
MV = 2


LEARN_RATE = 0.01
BETA_ONE = 0.9
BETA_TWO = 0.95
EPSILON = 1e-08


def adam_update(weight, first_state, second_state, gradient):
    first_state = BETA_ONE * first_state + (1.0 - BETA_ONE) * gradient
    second_state = BETA_TWO * second_state + (1.0 - BETA_TWO) * gradient * gradient
    weight = weight - LEARN_RATE * first_state / (jnp.sqrt(second_state) + EPSILON)
    return (weight, first_state, second_state)


def send_positions(owner_devices, shard_count, slot_count):
    sources = jnp.arange(shard_count, dtype=jnp.int32)[:, None]
    moving = (owner_devices >= 0) & (owner_devices != sources)
    slot_ids = jnp.arange(slot_count)
    earlier = slot_ids[None, :] < slot_ids[:, None]
    matches = (
        (owner_devices[:, :, None] == owner_devices[:, None, :])
        & moving[:, None, :]
        & earlier[None, :, :]
    )
    return (moving, jnp.sum(matches, axis=2))


def pack_moving(values, owner_row, moving_row, position_row, shard_count, capacity):
    slot_ids = jnp.arange(values.shape[0], dtype=jnp.int32)
    targets = owner_row * capacity + position_row
    entries = jnp.arange(shard_count * capacity, dtype=jnp.int32)
    matches = (targets[None, :] == entries[:, None]) & moving_row[None, :]
    source = jnp.sum(jnp.where(matches, slot_ids[None, :], 0), axis=1)
    filled = jnp.any(matches, axis=1)
    packed = jnp.where(filled[:, None], jnp.take(values, source, axis=0), 0.0)
    return packed.reshape(shard_count, capacity, values.shape[1])


def place_blocks(
    received,
    own_values,
    owner_devices,
    destination_slot_list,
    moving,
    positions,
    my_index,
    capacity,
):
    shard_count, slot_count = owner_devices.shape
    slot_ids = jnp.arange(slot_count, dtype=jnp.int32)
    entries = (jnp.arange(shard_count, dtype=jnp.int32)[:, None] * capacity + positions).reshape(-1)
    to_me = (moving & (owner_devices == my_index)).reshape(-1)
    matches = to_me[None, :] & (destination_slot_list.reshape(-1)[None, :] == slot_ids[:, None])
    arrived = jnp.any(matches, axis=1)
    from_entry = jnp.sum(jnp.where(matches, entries[None, :], 0), axis=1)
    flattened = received.reshape(shard_count * capacity, received.shape[2])
    arrival_rows = jnp.take(flattened, from_entry, axis=0)
    stay_hit = (owner_devices[my_index] == my_index)[None, :] & (
        destination_slot_list[my_index][None, :] == slot_ids[:, None]
    )
    stayed = jnp.any(stay_hit, axis=1)
    from_slot = jnp.sum(jnp.where(stay_hit, slot_ids[None, :], 0), axis=1)
    kept_rows = jnp.take(own_values, from_slot, axis=0)
    return jnp.where(arrived[:, None], arrival_rows, jnp.where(stayed[:, None], kept_rows, 0.0))


def local_place(block_ids, first_id, local_count):
    local_ids = block_ids - first_id
    inside = (local_ids >= 0) & (local_ids < local_count)
    return jnp.where(inside, local_ids, local_count)


def general(
    hidden,
    out_grad,
    block_weight,
    block_row,
    block_col,
    live_count,
    new_owner,
    new_slot,
    first_moment,
    second_moment,
):
    shard_count = lax.axis_size(SHARD)
    dp_count = lax.axis_size(DP)
    my_index = lax.axis_index(SHARD)
    dp_index = lax.axis_index(DP)
    tokens_dev = hidden.shape[0]
    slot_count = block_weight.shape[1]
    block_size = block_weight.shape[2]
    share_size = first_moment.shape[2]
    row_blocks = hidden.shape[1] * shard_count // block_size
    col_blocks = out_grad.shape[1] * shard_count // block_size
    grad_scale = 1.0 / math.sqrt(tokens_dev * dp_count)
    slot_ids = jnp.arange(slot_count)
    live_all = slot_ids[None, :] < live_count[:, None]
    my_live = live_all[my_index]
    my_rows = block_row[my_index]
    my_cols = block_col[my_index]
    zero_bf = jnp.zeros((), jnp.bfloat16)
    full_hidden, full_grad = (
        lax.all_gather(hidden, SHARD, axis=1, tiled=True),
        lax.all_gather(out_grad, SHARD, axis=1, tiled=True),
    )
    hidden_blocks = full_hidden.reshape(tokens_dev, row_blocks, block_size)
    grad_blocks = full_grad.reshape(tokens_dev, col_blocks, block_size)
    own_hidden = jnp.take(hidden_blocks, my_rows, axis=1)
    own_grad = jnp.take(grad_blocks, my_cols, axis=1)
    grad_share = None
    col_local = col_blocks // shard_count
    row_local = row_blocks // shard_count

    def one_shard(totals, member):
        blocks, shard_index = member
        row_ids = block_row[shard_index]
        col_ids = block_col[shard_index]
        weights = jnp.where(live_all[shard_index][:, None, None], blocks, zero_bf)
        hidden_part = jnp.take(hidden_blocks, row_ids, axis=1)
        grad_part = jnp.take(grad_blocks, col_ids, axis=1)
        forward = jnp.einsum(
            "tkr,krc->tkc", hidden_part, weights, preferred_element_type=jnp.float32
        )
        backward = jnp.einsum(
            "tkc,krc->tkr", grad_part, weights, preferred_element_type=jnp.float32
        )
        col_place = local_place(col_ids, my_index * col_local, col_local)
        row_place = local_place(row_ids, my_index * row_local, row_local)
        out_total = totals[0].at[:, col_place].add(forward, mode="drop")
        back_total = totals[1].at[:, row_place].add(backward, mode="drop")
        return ((out_total, back_total), None)

    initial = (
        jnp.zeros((tokens_dev, col_local, block_size), jnp.float32),
        jnp.zeros((tokens_dev, row_local, block_size), jnp.float32),
    )
    totals = initial
    blocks_in = lax.all_gather(block_weight, SHARD, axis=0, tiled=True)
    indices = jnp.arange(blocks_in.shape[0], dtype=jnp.int32)
    totals, unused = lax.scan(one_shard, totals, (blocks_in, indices))
    out_total, back_total = totals
    projected = out_total.reshape(tokens_dev, col_local * block_size).astype(jnp.bfloat16)
    hidden_grad = back_total.reshape(tokens_dev, row_local * block_size).astype(jnp.bfloat16)
    blocks = (
        jnp.einsum("tkr,tkc->krc", own_hidden, own_grad, preferred_element_type=jnp.float32)
        * grad_scale
    )
    blocks = jnp.where(my_live[:, None, None], blocks, 0.0)
    grad_share = lax.psum_scatter(
        blocks.reshape(slot_count, block_size * block_size), DP, scatter_dimension=1, tiled=True
    )
    moving, positions = send_positions(new_owner, shard_count, slot_count)
    my_owner = new_owner[my_index]
    my_moving = moving[my_index]
    my_positions = positions[my_index]
    flat_weight = block_weight[0].reshape(slot_count, block_size * block_size)
    weight_share = lax.dynamic_slice_in_dim(
        flat_weight, dp_index * share_size, share_size, 1
    ).astype(jnp.float32)
    updated, first_state, second_state = adam_update(
        weight_share, first_moment[0], second_moment[0], grad_share
    )
    stacked = jnp.concatenate([updated, first_state, second_state], axis=1)
    packed = pack_moving(stacked, my_owner, my_moving, my_positions, shard_count, MV)
    received = lax.all_to_all(packed, SHARD, split_axis=0, concat_axis=0, tiled=True)
    placed = place_blocks(received, stacked, new_owner, new_slot, moving, positions, my_index, MV)
    new_weight = placed[:, :share_size]
    new_first = placed[:, share_size : 2 * share_size]
    new_second = placed[:, 2 * share_size :]
    return (projected, hidden_grad, new_weight[None], new_first[None], new_second[None])


WCAP = 44
GCAP = 40
PAIR = 14
UNROLL = 4
NX, NY, NZH, NZL = 4, 8, 2, 4
BS = 128
VMEM_LIMIT = 4 * 1024 * 1024
f32 = jnp.float32
bf16 = jnp.bfloat16
i32 = jnp.int32


def call(kernel, outs, n_smem, n_vmem, scratch=(), flops=0, byts=0, n_after=0):
    smem = pl.BlockSpec(memory_space=pltpu.SMEM)
    vmem = pl.BlockSpec(memory_space=pltpu.VMEM)
    return pl.pallas_call(
        kernel,
        out_shape=outs,
        in_specs=[smem] * n_smem + [vmem] * n_vmem + [pl.BlockSpec(memory_space=pl.ANY)] * n_after,
        out_specs=jax.tree.map(lambda _: vmem, outs),
        scratch_shapes=list(scratch),
        compiler_params=pltpu.CompilerParams(vmem_limit_bytes=VMEM_LIMIT),
        cost_estimate=pl.CostEstimate(flops=flops, bytes_accessed=byts, transcendentals=0),
    )


def like(shape, dtype):
    return jax.ShapeDtypeStruct(shape, dtype)


def make_plan(block_row, block_col, live_count, new_owner, new_slot, row_local, me):
    shard_count, slot_count = block_row.shape
    total = shard_count * slot_count
    ids = jnp.arange(total, dtype=i32)
    live = (jnp.arange(slot_count)[None, :] < live_count[:, None]).reshape(total)
    row = block_row.reshape(total)
    col = block_col.reshape(total)
    owner = jnp.where(live, new_owner.reshape(total), -1)
    slot = new_slot.reshape(total)
    kept = owner >= 0
    row_shard = row // row_local
    key = jnp.where(kept, ids, ids + total)
    same = row_shard[:, None] == row_shard[None, :]
    before = same & live[None, :] & (key[None, :] < key[:, None])
    rank = jnp.sum(before.astype(i32), axis=1)
    earlier = same & (owner[:, None] == owner[None, :]) & (ids[None, :] < ids[:, None])
    pos = jnp.sum(earlier.astype(i32), axis=1)
    fits = (
        (jnp.max(jnp.where(live, rank, 0)) < WCAP)
        & (jnp.max(jnp.where(kept, rank, 0)) < GCAP)
        & (jnp.max(jnp.where(kept, pos, 0)) < PAIR)
    )

    here = live & (row_shard == me)
    words = ids + 256 * ((row - row_local * me) + 16 * col)
    hit = here[None, :] & (rank[None, :] == jnp.arange(WCAP)[:, None])
    code = jnp.sum(jnp.where(hit, words[None, :], 0), axis=1)
    counts = [jnp.minimum(jnp.sum(here.astype(i32)), WCAP), jnp.minimum(jnp.sum((here & kept).astype(i32)), GCAP)]
    going = jnp.where(here & kept, owner * PAIR + pos, -1)
    send_hit = going[None, :] == jnp.arange(shard_count * PAIR)[:, None]
    send = jnp.minimum(jnp.sum(jnp.where(send_hit, rank[None, :], 0), axis=1), GCAP - 1)
    owner2 = owner.reshape(shard_count, slot_count)
    sources = jnp.arange(shard_count, dtype=i32)[:, None]
    slots = jnp.arange(slot_count, dtype=i32)[None, :]
    moving, positions = send_positions(owner2, shard_count, slot_count)
    target = jnp.where(moving & (sources == me), owner2 * MV + positions, -1).reshape(total)
    state_hit = target[None, :] == jnp.arange(shard_count * MV)[:, None]
    state_send = jnp.sum(jnp.where(state_hit, (ids % slot_count)[None, :], 0), axis=1)
    state_row = jnp.where(sources == me, slots, slot_count + sources * MV + positions).reshape(total)
    landing = 1 + row_shard * PAIR + jnp.minimum(pos, PAIR - 1) + shard_count * PAIR * state_row
    lands = (owner == me)[None, :] & (slot[None, :] == jnp.arange(slot_count)[:, None])
    place = jnp.sum(jnp.where(lands, landing[None, :], 0), axis=1)
    return fits, code, counts, send, state_send, place


def grad_kernel(info, code, hidden, mine, other, out, cols, hidden_t, total):
    my_core = info[2]
    for zl in range(NZL):
        for sub in range(4):
            lanes = slice(sub * BS, (sub + 1) * BS)
            cols[(2 * zl + my_core) * 4 + sub] = mine[zl, :, lanes]
            cols[(2 * zl + 1 - my_core) * 4 + sub] = other[zl, :, lanes]
    row_local = hidden.shape[1] // BS
    for r in range(row_local):
        hidden_t[r] = hidden[:, r * BS : (r + 1) * BS].T

    def step(i, carry):
        blocks = []
        for u in range(UNROLL):
            word = code[i * UNROLL + u]
            blocks.append(jnp.dot(hidden_t[(word >> 8) & 15], cols[word >> 12], preferred_element_type=f32))
        for u in range(UNROLL):
            total[pl.ds(i * UNROLL + u, BS, stride=GCAP), :] = blocks[u]
        return carry

    lax.fori_loop(0, (info[1] + UNROLL - 1) // UNROLL, step, 0)
    for x in range(NX):
        for y in range(NY):
            for q in range(4):
                source = 16 * y + 4 * x + q
                out[x, 4 * y + q] = total[source * GCAP : (source + 1) * GCAP, :].astype(bf16)


def sum_kernel(parts, out):
    def step(i, carry):
        value = parts[0, i].astype(f32)
        for n in range(1, parts.shape[0]):
            value += parts[n, i].astype(f32)
        out[i] = value.astype(bf16)
        return carry

    lax.fori_loop(0, out.shape[0], step, 0, unroll=4)


def pair_kernel(info, parts, keep, send):
    my_zh = info[5]
    for out, zh in ((keep, my_zh), (send, 1 - my_zh)):
        for b in range(2):
            value = parts[0, 2 * zh + b].astype(f32)
            for n in range(1, parts.shape[0]):
                value += parts[n, 2 * zh + b].astype(f32)
            out[b] = value


def share_kernel(scale, send, state_send, keep, came, stacked, _after, out, total):
    total[...] = (keep[...] + came[...]) * scale
    width = stacked.shape[1] // BS
    for d in range(out.shape[0]):
        for p in range(PAIR):
            rank = send[d * PAIR + p]
            for b in range(2):
                out[d, 2 * p + b : 2 * p + b + 1, :] = total[b, pl.ds(rank, 1), :]
        for p in range(MV):
            row = stacked[pl.ds(state_send[d * MV + p], 1), :]
            for n in range(width):
                at = 2 * PAIR + width * p + n
                out[d, at : at + 1, :] = row[:, n * BS : (n + 1) * BS]


def select_kernel(info, code, gathered, _after, out):
    def step(c, carry):
        value = gathered[code[c] & 255]
        out[c] = jnp.where(c < info[0], value, jnp.zeros_like(value))
        return carry

    lax.fori_loop(0, WCAP, step, 0, unroll=4)


def forward_kernel(info, code, hidden, w0, w1, w2, w3, _after, mine, theirs, weights, total, sems):
    my_core, my_x = info[2], info[3]
    copies = [
        pltpu.make_async_copy(part, weights.at[:, (my_x + NX - k) % NX], sems.at[k])
        for k, part in enumerate((w0, w1, w2, w3))
    ]
    for copy in copies:
        copy.start()
    total[...] = jnp.zeros_like(total)
    for copy in copies:
        copy.wait()

    def step(i, carry):
        adds = []
        for u in range(UNROLL):
            c = i * UNROLL + u
            word = code[c]
            lanes = pl.ds(pl.multiple_of(((word >> 8) & 15) * BS, BS), BS)
            w = weights[c].reshape(BS, BS)
            adds.append((word >> 12, jnp.dot(hidden[:, lanes], w, preferred_element_type=f32)))
        for col, value in adds:
            total[col] += value
        return carry

    lax.fori_loop(0, (info[0] + UNROLL - 1) // UNROLL, step, 0)
    for zl in range(NZL):
        for sub in range(4):
            mine[zl, sub] = total[(2 * zl + my_core) * 4 + sub]
            theirs[zl, sub] = total[(2 * zl + 1 - my_core) * 4 + sub]


def backward_kernel(info, code, cols, weights, back, total):
    total[...] = jnp.zeros_like(total)

    def step(i, carry):
        adds = []
        for u in range(UNROLL):
            c = i * UNROLL + u
            word = code[c]
            w = weights[c].reshape(BS, BS)
            value = lax.dot_general(cols[word >> 12], w, (((1,), (1,)), ((), ())), preferred_element_type=f32)
            adds.append(((word >> 8) & 15, value))
        for r, value in adds:
            total[r] += value
        return carry

    lax.fori_loop(0, (info[0] + UNROLL - 1) // UNROLL, step, 0)
    for r in range(total.shape[0]):
        back[:, r * BS : (r + 1) * BS] = total[r].astype(bf16)


def chip_kernel(info, mine, came, _after, own, s1, s2, s3):
    my_zl = info[4]
    own[...] = mine[my_zl] + came[my_zl]
    for k, out in enumerate((s1, s2, s3)):
        zl = (my_zl + k + 1) % NZL
        out[...] = (mine[zl] + came[zl]).astype(bf16)


def project_kernel(own, r1, r2, r3, out):
    for sub in range(4):
        value = own[sub] + r1[sub].astype(f32) + r2[sub].astype(f32) + r3[sub].astype(f32)
        out[:, sub * BS : (sub + 1) * BS] = value.astype(bf16)


def adam_kernel(place, stacked, came, new_w, new_m, new_v, rows, grad):
    slots, share = new_w.shape
    places = came.shape[0] * PAIR
    width = stacked.shape[1] // BS
    for j in range(slots):
        word = jnp.maximum(place[j] - 1, 0)
        g, row = word % places, word // places
        filled = place[j] > 0
        here = row < slots
        entry = jnp.maximum(row - slots, 0)
        own = stacked[pl.ds(jnp.minimum(row, slots - 1), 1), :]
        for n in range(width):
            lanes = slice(n * BS, (n + 1) * BS)
            moved = came[entry // MV, pl.ds(2 * PAIR + width * (entry % MV) + n, 1), :]
            rows[j : j + 1, lanes] = jnp.where(filled, jnp.where(here, own[:, lanes], moved), 0.0)
        for b in range(2):
            value = came[g // PAIR, pl.ds(2 * (g % PAIR) + b, 1), :]
            grad[j : j + 1, b * BS : (b + 1) * BS] = jnp.where(filled, value, 0.0)
    w, m, v = adam_update(rows[:, :share], rows[:, share : 2 * share], rows[:, 2 * share :], grad[...])
    new_w[...] = w
    new_m[...] = m
    new_v[...] = v


def all_to_all(values, axis):
    return lax.all_to_all(values, axis, split_axis=0, concat_axis=0, tiled=True)


def shift(values, axis, count, step):
    return lax.ppermute(values, axis, [(i, (i + step) % count) for i in range(count)])


def shards(
    hidden,
    out_grad,
    block_weight,
    block_row,
    block_col,
    live_count,
    new_owner,
    new_slot,
    first_moment,
    second_moment,
):
    shard_count = lax.axis_size(SHARD)
    me = lax.axis_index(SHARD)
    dp_index = lax.axis_index(DP)
    x_index = lax.axis_index("x")
    tokens = hidden.shape[0]
    slot_count = block_weight.shape[1]
    row_local = hidden.shape[1] // BS
    share = first_moment.shape[2]
    scale = 1.0 / math.sqrt(tokens * lax.axis_size(DP))

    mine = all_to_all(jnp.broadcast_to(out_grad[None], (NZL,) + out_grad.shape), "zl")
    other = shift(mine, "core", 2, 1)
    quarter = lax.dynamic_slice_in_dim(block_weight[0], x_index * (BS // NX), BS // NX, 1)
    gathered = lax.all_gather(quarter, SHARD, axis=0, tiled=True)
    weight_share = lax.dynamic_slice_in_dim(block_weight[0], dp_index * 2, 2, 1).reshape(slot_count, share)
    stacked = jnp.concatenate([weight_share.astype(f32), first_moment[0], second_moment[0]], axis=1)

    fits, code, counts, send, state_send, place = make_plan(
        block_row, block_col, live_count, new_owner, new_slot, row_local, me
    )
    info = jnp.stack(counts + [lax.axis_index("core"), x_index, lax.axis_index("zl"), lax.axis_index("zh")])

    partial, cols = call(
        grad_kernel,
        (like((NX, NY * NZH * 2, GCAP, BS), bf16), like((shard_count * 4, BS, BS), bf16)),
        2,
        3,
        [pltpu.VMEM((row_local, BS, BS), bf16), pltpu.VMEM((BS * GCAP, BS), f32)],
        flops=2 * WCAP * BS**3,
        byts=4 * 1024 * 1024,
    )(info, code, hidden, mine, other)
    along_x = all_to_all(partial, "x")
    summed = call(sum_kernel, like(partial.shape[1:], bf16), 0, 1, byts=2 * 1024 * 1024)(along_x)
    along_y = all_to_all(summed.reshape(NY, 2 * NZH, GCAP, BS), "y")
    part = (2, GCAP, BS)
    keep, send_zh = call(pair_kernel, (like(part, f32), like(part, f32)), 1, 1, byts=1024 * 1024)(info, along_y)
    came_zh = shift(send_zh, "zh", NZH, 1)

    picked = call(select_kernel, like((WCAP, BS // NX, BS), bf16), 2, 1, byts=1024 * 1024, n_after=1)(
        info, code, gathered, summed
    )
    w2, w1, w3 = (shift(picked, "x", NX, k) for k in (2, 1, 3))

    out_mine, out_theirs, weights = call(
        forward_kernel,
        (
            like((NZL, 4, tokens, BS), f32),
            like((NZL, 4, tokens, BS), f32),
            like((WCAP, NX, BS // NX, BS), bf16),
        ),
        2,
        1,
        [pltpu.VMEM((shard_count * 4, tokens, BS), f32), pltpu.SemaphoreType.DMA((NX,))],
        flops=2 * WCAP * BS**3,
        byts=8 * 1024 * 1024,
        n_after=5,
    )(info, code, hidden, picked, w1, w2, w3, keep)
    came = shift(out_theirs, "core", 2, 1)
    hidden_grad = call(
        backward_kernel,
        like(hidden.shape, bf16),
        2,
        2,
        [pltpu.VMEM((row_local, tokens, BS), f32)],
        flops=2 * WCAP * BS**3,
        byts=4 * 1024 * 1024,
    )(info, code, cols, weights)
    packed = call(
        functools.partial(share_kernel, scale),
        like((shard_count, 2 * PAIR + MV * stacked.shape[1] // BS, BS), f32),
        2,
        3,
        [pltpu.VMEM((2, GCAP, BS), f32)],
        byts=1024 * 1024,
        n_after=1,
    )(send, state_send, keep, came_zh, stacked, hidden_grad)
    shares = all_to_all(packed, SHARD)
    part = (4, tokens, BS)
    own, s1, s2, s3 = call(
        chip_kernel, (like(part, f32),) + (like(part, bf16),) * 3, 1, 2, byts=3 * 1024 * 1024, n_after=1
    )(info, out_mine, came, packed)
    r2, r1, r3 = (shift(s, "zl", NZL, k) for k, s in ((2, s2), (1, s1), (3, s3)))
    projected = call(project_kernel, like(out_grad.shape, bf16), 0, 4, byts=1024 * 1024)(own, r1, r2, r3)

    shape = like((slot_count, share), f32)
    new_weight, new_first, new_second = call(
        adam_kernel,
        (shape, shape, shape),
        1,
        2,
        [pltpu.VMEM((slot_count, 3 * share), f32), pltpu.VMEM((slot_count, share), f32)],
        byts=1024 * 1024,
    )(place, stacked, shares)
    result = (projected, hidden_grad, new_weight[None], new_first[None], new_second[None])
    return lax.cond(
        fits,
        lambda: result,
        lambda: general(
            hidden,
            out_grad,
            block_weight,
            block_row,
            block_col,
            live_count,
            new_owner,
            new_slot,
            first_moment,
            second_moment,
        ),
    )


def solution(mesh):
    split = Mesh(mesh.devices.reshape(NY, NX, NZH, NZL, 2), ("y", "x", "zh", "zl", "core"))
    in_specs = (
        P(DP, SHARD),
        P(DP, SHARD),
        P(SHARD, None, None, None),
        P(),
        P(),
        P(),
        P(),
        P(),
        P(SHARD, None, DP),
        P(SHARD, None, DP),
    )
    out_specs = (
        P(DP, SHARD),
        P(DP, SHARD),
        P(SHARD, None, DP),
        P(SHARD, None, DP),
        P(SHARD, None, DP),
    )
    return jax.shard_map(shards, mesh=split, in_specs=in_specs, out_specs=out_specs, check_vma=False)
```

```python
import functools
import math

import jax
import jax.numpy as jnp
from jax import lax
from jax.experimental import pallas as pl
from jax.experimental.pallas import tpu as pltpu
from jax.sharding import Mesh, PartitionSpec as P

DP = ("y", "x", "zh")
SHARD = ("zl", "core")
MV = 2


LEARN_RATE = 0.01
BETA_ONE = 0.9
BETA_TWO = 0.95
EPSILON = 1e-08


def adam_update(weight, first_state, second_state, gradient):
    first_state = BETA_ONE * first_state + (1.0 - BETA_ONE) * gradient
    second_state = BETA_TWO * second_state + (1.0 - BETA_TWO) * gradient * gradient
    weight = weight - LEARN_RATE * first_state / (jnp.sqrt(second_state) + EPSILON)
    return (weight, first_state, second_state)


def send_positions(owner_devices, shard_count, slot_count):
    sources = jnp.arange(shard_count, dtype=jnp.int32)[:, None]
    moving = (owner_devices >= 0) & (owner_devices != sources)
    slot_ids = jnp.arange(slot_count)
    earlier = slot_ids[None, :] < slot_ids[:, None]
    matches = (
        (owner_devices[:, :, None] == owner_devices[:, None, :])
        & moving[:, None, :]
        & earlier[None, :, :]
    )
    return (moving, jnp.sum(matches, axis=2))


def pack_moving(values, owner_row, moving_row, position_row, shard_count, capacity):
    slot_ids = jnp.arange(values.shape[0], dtype=jnp.int32)
    targets = owner_row * capacity + position_row
    entries = jnp.arange(shard_count * capacity, dtype=jnp.int32)
    matches = (targets[None, :] == entries[:, None]) & moving_row[None, :]
    source = jnp.sum(jnp.where(matches, slot_ids[None, :], 0), axis=1)
    filled = jnp.any(matches, axis=1)
    packed = jnp.where(filled[:, None], jnp.take(values, source, axis=0), 0.0)
    return packed.reshape(shard_count, capacity, values.shape[1])


def place_blocks(
    received,
    own_values,
    owner_devices,
    destination_slot_list,
    moving,
    positions,
    my_index,
    capacity,
):
    shard_count, slot_count = owner_devices.shape
    slot_ids = jnp.arange(slot_count, dtype=jnp.int32)
    entries = (jnp.arange(shard_count, dtype=jnp.int32)[:, None] * capacity + positions).reshape(-1)
    to_me = (moving & (owner_devices == my_index)).reshape(-1)
    matches = to_me[None, :] & (destination_slot_list.reshape(-1)[None, :] == slot_ids[:, None])
    arrived = jnp.any(matches, axis=1)
    from_entry = jnp.sum(jnp.where(matches, entries[None, :], 0), axis=1)
    flattened = received.reshape(shard_count * capacity, received.shape[2])
    arrival_rows = jnp.take(flattened, from_entry, axis=0)
    stay_hit = (owner_devices[my_index] == my_index)[None, :] & (
        destination_slot_list[my_index][None, :] == slot_ids[:, None]
    )
    stayed = jnp.any(stay_hit, axis=1)
    from_slot = jnp.sum(jnp.where(stay_hit, slot_ids[None, :], 0), axis=1)
    kept_rows = jnp.take(own_values, from_slot, axis=0)
    return jnp.where(arrived[:, None], arrival_rows, jnp.where(stayed[:, None], kept_rows, 0.0))


def local_place(block_ids, first_id, local_count):
    local_ids = block_ids - first_id
    inside = (local_ids >= 0) & (local_ids < local_count)
    return jnp.where(inside, local_ids, local_count)


def general(
    hidden,
    out_grad,
    block_weight,
    block_row,
    block_col,
    live_count,
    new_owner,
    new_slot,
    first_moment,
    second_moment,
):
    shard_count = lax.axis_size(SHARD)
    dp_count = lax.axis_size(DP)
    my_index = lax.axis_index(SHARD)
    dp_index = lax.axis_index(DP)
    tokens_dev = hidden.shape[0]
    slot_count = block_weight.shape[1]
    block_size = block_weight.shape[2]
    share_size = first_moment.shape[2]
    row_blocks = hidden.shape[1] * shard_count // block_size
    col_blocks = out_grad.shape[1] * shard_count // block_size
    grad_scale = 1.0 / math.sqrt(tokens_dev * dp_count)
    slot_ids = jnp.arange(slot_count)
    live_all = slot_ids[None, :] < live_count[:, None]
    my_live = live_all[my_index]
    my_rows = block_row[my_index]
    my_cols = block_col[my_index]
    zero_bf = jnp.zeros((), jnp.bfloat16)
    full_hidden, full_grad = (
        lax.all_gather(hidden, SHARD, axis=1, tiled=True),
        lax.all_gather(out_grad, SHARD, axis=1, tiled=True),
    )
    hidden_blocks = full_hidden.reshape(tokens_dev, row_blocks, block_size)
    grad_blocks = full_grad.reshape(tokens_dev, col_blocks, block_size)
    own_hidden = jnp.take(hidden_blocks, my_rows, axis=1)
    own_grad = jnp.take(grad_blocks, my_cols, axis=1)
    grad_share = None
    col_local = col_blocks // shard_count
    row_local = row_blocks // shard_count

    def one_shard(totals, member):
        blocks, shard_index = member
        row_ids = block_row[shard_index]
        col_ids = block_col[shard_index]
        weights = jnp.where(live_all[shard_index][:, None, None], blocks, zero_bf)
        hidden_part = jnp.take(hidden_blocks, row_ids, axis=1)
        grad_part = jnp.take(grad_blocks, col_ids, axis=1)
        forward = jnp.einsum(
            "tkr,krc->tkc", hidden_part, weights, preferred_element_type=jnp.float32
        )
        backward = jnp.einsum(
            "tkc,krc->tkr", grad_part, weights, preferred_element_type=jnp.float32
        )
        col_place = local_place(col_ids, my_index * col_local, col_local)
        row_place = local_place(row_ids, my_index * row_local, row_local)
        out_total = totals[0].at[:, col_place].add(forward, mode="drop")
        back_total = totals[1].at[:, row_place].add(backward, mode="drop")
        return ((out_total, back_total), None)

    initial = (
        jnp.zeros((tokens_dev, col_local, block_size), jnp.float32),
        jnp.zeros((tokens_dev, row_local, block_size), jnp.float32),
    )
    totals = initial
    blocks_in = lax.all_gather(block_weight, SHARD, axis=0, tiled=True)
    indices = jnp.arange(blocks_in.shape[0], dtype=jnp.int32)
    totals, unused = lax.scan(one_shard, totals, (blocks_in, indices))
    out_total, back_total = totals
    projected = out_total.reshape(tokens_dev, col_local * block_size).astype(jnp.bfloat16)
    hidden_grad = back_total.reshape(tokens_dev, row_local * block_size).astype(jnp.bfloat16)
    blocks = (
        jnp.einsum("tkr,tkc->krc", own_hidden, own_grad, preferred_element_type=jnp.float32)
        * grad_scale
    )
    blocks = jnp.where(my_live[:, None, None], blocks, 0.0)
    grad_share = lax.psum_scatter(
        blocks.reshape(slot_count, block_size * block_size), DP, scatter_dimension=1, tiled=True
    )
    moving, positions = send_positions(new_owner, shard_count, slot_count)
    my_owner = new_owner[my_index]
    my_moving = moving[my_index]
    my_positions = positions[my_index]
    flat_weight = block_weight[0].reshape(slot_count, block_size * block_size)
    weight_share = lax.dynamic_slice_in_dim(
        flat_weight, dp_index * share_size, share_size, 1
    ).astype(jnp.float32)
    updated, first_state, second_state = adam_update(
        weight_share, first_moment[0], second_moment[0], grad_share
    )
    stacked = jnp.concatenate([updated, first_state, second_state], axis=1)
    packed = pack_moving(stacked, my_owner, my_moving, my_positions, shard_count, MV)
    received = lax.all_to_all(packed, SHARD, split_axis=0, concat_axis=0, tiled=True)
    placed = place_blocks(received, stacked, new_owner, new_slot, moving, positions, my_index, MV)
    new_weight = placed[:, :share_size]
    new_first = placed[:, share_size : 2 * share_size]
    new_second = placed[:, 2 * share_size :]
    return (projected, hidden_grad, new_weight[None], new_first[None], new_second[None])


WCAP = 44
GCAP = 40
PAIR = 14
UNROLL = 4
NX, NY, NZH, NZL = 4, 8, 2, 4
BS = 128
VMEM_LIMIT = 10 * 1024 * 1024
f32 = jnp.float32
bf16 = jnp.bfloat16
i32 = jnp.int32


def call(kernel, outs, n_smem, n_vmem, scratch=(), flops=0, byts=0, n_after=0):
    smem = pl.BlockSpec(memory_space=pltpu.SMEM)
    vmem = pl.BlockSpec(memory_space=pltpu.VMEM)
    return pl.pallas_call(
        kernel,
        out_shape=outs,
        in_specs=[smem] * n_smem + [vmem] * n_vmem + [pl.BlockSpec(memory_space=pl.ANY)] * n_after,
        out_specs=jax.tree.map(lambda _: vmem, outs),
        scratch_shapes=list(scratch),
        compiler_params=pltpu.CompilerParams(vmem_limit_bytes=VMEM_LIMIT),
        cost_estimate=pl.CostEstimate(flops=flops, bytes_accessed=byts, transcendentals=0),
    )


def like(shape, dtype):
    return jax.ShapeDtypeStruct(shape, dtype)


def make_plan(block_row, block_col, live_count, new_owner, new_slot, row_local, me):
    shard_count, slot_count = block_row.shape
    total = shard_count * slot_count
    ids = jnp.arange(total, dtype=i32)
    live = (jnp.arange(slot_count)[None, :] < live_count[:, None]).reshape(total)
    row = block_row.reshape(total)
    col = block_col.reshape(total)
    owner = jnp.where(live, new_owner.reshape(total), -1)
    slot = new_slot.reshape(total)
    kept = owner >= 0
    row_shard = row // row_local
    key = jnp.where(kept, ids, ids + total)
    same = row_shard[:, None] == row_shard[None, :]
    before = same & live[None, :] & (key[None, :] < key[:, None])
    rank = jnp.sum(before.astype(i32), axis=1)
    earlier = same & (owner[:, None] == owner[None, :]) & (ids[None, :] < ids[:, None])
    pos = jnp.sum(earlier.astype(i32), axis=1)
    fits = (
        (jnp.max(jnp.where(live, rank, 0)) < WCAP)
        & (jnp.max(jnp.where(kept, rank, 0)) < GCAP)
        & (jnp.max(jnp.where(kept, pos, 0)) < PAIR)
    )

    here = live & (row_shard == me)
    words = ids + 256 * ((row - row_local * me) + 16 * col)
    hit = here[None, :] & (rank[None, :] == jnp.arange(WCAP)[:, None])
    code = jnp.sum(jnp.where(hit, words[None, :], 0), axis=1)
    counts = [jnp.minimum(jnp.sum(here.astype(i32)), WCAP), jnp.minimum(jnp.sum((here & kept).astype(i32)), GCAP)]
    going = jnp.where(here & kept, owner * PAIR + pos, -1)
    send_hit = going[None, :] == jnp.arange(shard_count * PAIR)[:, None]
    send = jnp.minimum(jnp.sum(jnp.where(send_hit, rank[None, :], 0), axis=1), GCAP - 1)
    owner2 = owner.reshape(shard_count, slot_count)
    sources = jnp.arange(shard_count, dtype=i32)[:, None]
    slots = jnp.arange(slot_count, dtype=i32)[None, :]
    moving, positions = send_positions(owner2, shard_count, slot_count)
    target = jnp.where(moving & (sources == me), owner2 * MV + positions, -1).reshape(total)
    state_hit = target[None, :] == jnp.arange(shard_count * MV)[:, None]
    state_send = jnp.sum(jnp.where(state_hit, (ids % slot_count)[None, :], 0), axis=1)
    state_row = jnp.where(sources == me, slots, slot_count + sources * MV + positions).reshape(total)
    landing = 1 + row_shard * PAIR + jnp.minimum(pos, PAIR - 1) + shard_count * PAIR * state_row
    lands = (owner == me)[None, :] & (slot[None, :] == jnp.arange(slot_count)[:, None])
    place = jnp.sum(jnp.where(lands, landing[None, :], 0), axis=1)
    return fits, code, counts, send, state_send, place


def grad_kernel(info, code, hidden, mine, other, out, cols, hidden_t, total):
    my_core = info[2]
    for zl in range(NZL):
        for sub in range(4):
            lanes = slice(sub * BS, (sub + 1) * BS)
            cols[(2 * zl + my_core) * 4 + sub] = mine[zl, :, lanes]
            cols[(2 * zl + 1 - my_core) * 4 + sub] = other[zl, :, lanes]
    row_local = hidden.shape[1] // BS
    for r in range(row_local):
        hidden_t[r] = hidden[:, r * BS : (r + 1) * BS].T

    def step(i, carry):
        blocks = []
        for u in range(UNROLL):
            word = code[i * UNROLL + u]
            blocks.append(jnp.dot(hidden_t[(word >> 8) & 15], cols[word >> 12], preferred_element_type=f32))
        for u in range(UNROLL):
            total[pl.ds(i * UNROLL + u, BS, stride=GCAP), :] = blocks[u]
        return carry

    lax.fori_loop(0, (info[1] + UNROLL - 1) // UNROLL, step, 0)
    for row in range(BS):
        out[row // 2, row % 2] = total[row * GCAP : (row + 1) * GCAP, :].astype(bf16)


def share_kernel(scale, send, state_send, parts, stacked, _after, out, total):
    total[...] = parts[0].astype(f32)

    def step(n, carry):
        total[...] += parts[n].astype(f32)
        return carry

    lax.fori_loop(1, parts.shape[0], step, 0)
    total[...] = total[...] * scale
    width = stacked.shape[1] // BS
    for d in range(out.shape[0]):
        for p in range(PAIR):
            rank = send[d * PAIR + p]
            for b in range(2):
                out[d, 2 * p + b : 2 * p + b + 1, :] = total[b, pl.ds(rank, 1), :]
        for p in range(MV):
            row = stacked[pl.ds(state_send[d * MV + p], 1), :]
            for n in range(width):
                at = 2 * PAIR + width * p + n
                out[d, at : at + 1, :] = row[:, n * BS : (n + 1) * BS]


def select_kernel(info, code, gathered, _after, out):
    def step(c, carry):
        value = gathered[code[c] & 255]
        out[c] = jnp.where(c < info[0], value, jnp.zeros_like(value))
        return carry

    lax.fori_loop(0, WCAP, step, 0, unroll=4)


def forward_kernel(info, code, hidden, w0, w1, w2, w3, mine, theirs, weights, total, sems):
    my_core, my_x = info[2], info[3]
    copies = [
        pltpu.make_async_copy(part, weights.at[:, (my_x + NX - k) % NX], sems.at[k])
        for k, part in enumerate((w0, w1, w2, w3))
    ]
    for copy in copies:
        copy.start()
    total[...] = jnp.zeros_like(total)
    for copy in copies:
        copy.wait()

    def step(i, carry):
        adds = []
        for u in range(UNROLL):
            c = i * UNROLL + u
            word = code[c]
            lanes = pl.ds(pl.multiple_of(((word >> 8) & 15) * BS, BS), BS)
            w = weights[c].reshape(BS, BS)
            adds.append((word >> 12, jnp.dot(hidden[:, lanes], w, preferred_element_type=f32)))
        for col, value in adds:
            total[col] += value
        return carry

    lax.fori_loop(0, (info[0] + UNROLL - 1) // UNROLL, step, 0)
    for zl in range(NZL):
        for sub in range(4):
            mine[zl, sub] = total[(2 * zl + my_core) * 4 + sub]
            theirs[zl, sub] = total[(2 * zl + 1 - my_core) * 4 + sub]


def backward_kernel(info, code, cols, weights, back, total):
    total[...] = jnp.zeros_like(total)

    def step(i, carry):
        adds = []
        for u in range(UNROLL):
            c = i * UNROLL + u
            word = code[c]
            w = weights[c].reshape(BS, BS)
            value = lax.dot_general(cols[word >> 12], w, (((1,), (1,)), ((), ())), preferred_element_type=f32)
            adds.append(((word >> 8) & 15, value))
        for r, value in adds:
            total[r] += value
        return carry

    lax.fori_loop(0, (info[0] + UNROLL - 1) // UNROLL, step, 0)
    for r in range(total.shape[0]):
        back[:, r * BS : (r + 1) * BS] = total[r].astype(bf16)


def chip_kernel(info, mine, came, _after, own, s1, s2, s3):
    my_zl = info[4]
    own[...] = mine[my_zl] + came[my_zl]
    for k, out in enumerate((s1, s2, s3)):
        zl = (my_zl + k + 1) % NZL
        out[...] = (mine[zl] + came[zl]).astype(bf16)


def project_kernel(own, r1, r2, r3, out):
    for sub in range(4):
        value = own[sub] + r1[sub].astype(f32) + r2[sub].astype(f32) + r3[sub].astype(f32)
        out[:, sub * BS : (sub + 1) * BS] = value.astype(bf16)


def adam_kernel(place, stacked, came, new_w, new_m, new_v, rows, grad):
    slots, share = new_w.shape
    places = came.shape[0] * PAIR
    width = stacked.shape[1] // BS
    for j in range(slots):
        word = jnp.maximum(place[j] - 1, 0)
        g, row = word % places, word // places
        filled = place[j] > 0
        here = row < slots
        entry = jnp.maximum(row - slots, 0)
        own = stacked[pl.ds(jnp.minimum(row, slots - 1), 1), :]
        for n in range(width):
            lanes = slice(n * BS, (n + 1) * BS)
            moved = came[entry // MV, pl.ds(2 * PAIR + width * (entry % MV) + n, 1), :]
            rows[j : j + 1, lanes] = jnp.where(filled, jnp.where(here, own[:, lanes], moved), 0.0)
        for b in range(2):
            value = came[g // PAIR, pl.ds(2 * (g % PAIR) + b, 1), :]
            grad[j : j + 1, b * BS : (b + 1) * BS] = jnp.where(filled, value, 0.0)
    w, m, v = adam_update(rows[:, :share], rows[:, share : 2 * share], rows[:, 2 * share :], grad[...])
    new_w[...] = w
    new_m[...] = m
    new_v[...] = v


def all_to_all(values, axis):
    return lax.all_to_all(values, axis, split_axis=0, concat_axis=0, tiled=True)


def shift(values, axis, count, step):
    return lax.ppermute(values, axis, [(i, (i + step) % count) for i in range(count)])


def shards(
    hidden,
    out_grad,
    block_weight,
    block_row,
    block_col,
    live_count,
    new_owner,
    new_slot,
    first_moment,
    second_moment,
):
    shard_count = lax.axis_size(SHARD)
    me = lax.axis_index(SHARD)
    dp_index = lax.axis_index(DP)
    x_index = lax.axis_index("x")
    tokens = hidden.shape[0]
    slot_count = block_weight.shape[1]
    row_local = hidden.shape[1] // BS
    share = first_moment.shape[2]
    scale = 1.0 / math.sqrt(tokens * lax.axis_size(DP))

    mine = all_to_all(jnp.broadcast_to(out_grad[None], (NZL,) + out_grad.shape), "zl")
    other = shift(mine, "core", 2, 1)
    quarter = lax.dynamic_slice_in_dim(block_weight[0], x_index * (BS // NX), BS // NX, 1)
    gathered = lax.all_gather(quarter, SHARD, axis=0, tiled=True)
    weight_share = lax.dynamic_slice_in_dim(block_weight[0], dp_index * 2, 2, 1).reshape(slot_count, share)
    stacked = jnp.concatenate([weight_share.astype(f32), first_moment[0], second_moment[0]], axis=1)

    fits, code, counts, send, state_send, place = make_plan(
        block_row, block_col, live_count, new_owner, new_slot, row_local, me
    )
    info = jnp.stack(counts + [lax.axis_index("core"), x_index, lax.axis_index("zl"), lax.axis_index("zh")])

    partial, cols = call(
        grad_kernel,
        (like((NY * NX * NZH, 2, GCAP, BS), bf16), like((shard_count * 4, BS, BS), bf16)),
        2,
        3,
        [pltpu.VMEM((row_local, BS, BS), bf16), pltpu.VMEM((BS * GCAP, BS), f32)],
        flops=2 * WCAP * BS**3,
        byts=4 * 1024 * 1024,
    )(info, code, hidden, mine, other)
    along_dp = all_to_all(partial, DP)

    picked = call(select_kernel, like((WCAP, BS // NX, BS), bf16), 2, 1, byts=1024 * 1024, n_after=1)(
        info, code, gathered, partial
    )
    w2, w1, w3 = (shift(picked, "x", NX, k) for k in (2, 1, 3))

    out_mine, out_theirs, weights = call(
        forward_kernel,
        (
            like((NZL, 4, tokens, BS), f32),
            like((NZL, 4, tokens, BS), f32),
            like((WCAP, NX, BS // NX, BS), bf16),
        ),
        2,
        1,
        [pltpu.VMEM((shard_count * 4, tokens, BS), f32), pltpu.SemaphoreType.DMA((NX,))],
        flops=2 * WCAP * BS**3,
        byts=8 * 1024 * 1024,
        n_after=4,
    )(info, code, hidden, picked, w1, w2, w3)
    came = shift(out_theirs, "core", 2, 1)
    hidden_grad = call(
        backward_kernel,
        like(hidden.shape, bf16),
        2,
        2,
        [pltpu.VMEM((row_local, tokens, BS), f32)],
        flops=2 * WCAP * BS**3,
        byts=4 * 1024 * 1024,
    )(info, code, cols, weights)
    part = (4, tokens, BS)
    own, s1, s2, s3 = call(
        chip_kernel, (like(part, f32),) + (like(part, bf16),) * 3, 1, 2, byts=3 * 1024 * 1024, n_after=1
    )(info, out_mine, came, hidden_grad)
    packed = call(
        functools.partial(share_kernel, scale),
        like((shard_count, 2 * PAIR + MV * stacked.shape[1] // BS, BS), f32),
        2,
        2,
        [pltpu.VMEM((2, GCAP, BS), f32)],
        byts=1024 * 1024,
        n_after=1,
    )(send, state_send, along_dp, stacked, s1)
    shares = all_to_all(packed, SHARD)
    r2, r1, r3 = (shift(s, "zl", NZL, k) for k, s in ((2, s2), (1, s1), (3, s3)))
    projected = call(project_kernel, like(out_grad.shape, bf16), 0, 4, byts=1024 * 1024)(own, r1, r2, r3)

    shape = like((slot_count, share), f32)
    new_weight, new_first, new_second = call(
        adam_kernel,
        (shape, shape, shape),
        1,
        2,
        [pltpu.VMEM((slot_count, 3 * share), f32), pltpu.VMEM((slot_count, share), f32)],
        byts=1024 * 1024,
    )(place, stacked, shares)
    result = (projected, hidden_grad, new_weight[None], new_first[None], new_second[None])
    return lax.cond(
        fits,
        lambda: result,
        lambda: general(
            hidden,
            out_grad,
            block_weight,
            block_row,
            block_col,
            live_count,
            new_owner,
            new_slot,
            first_moment,
            second_moment,
        ),
    )


def solution(mesh):
    split = Mesh(mesh.devices.reshape(NY, NX, NZH, NZL, 2), ("y", "x", "zh", "zl", "core"))
    in_specs = (
        P(DP, SHARD),
        P(DP, SHARD),
        P(SHARD, None, None, None),
        P(),
        P(),
        P(),
        P(),
        P(),
        P(SHARD, None, DP),
        P(SHARD, None, DP),
    )
    out_specs = (
        P(DP, SHARD),
        P(DP, SHARD),
        P(SHARD, None, DP),
        P(SHARD, None, DP),
        P(SHARD, None, DP),
    )
    return jax.shard_map(shards, mesh=split, in_specs=in_specs, out_specs=out_specs, check_vma=False)
```

```python
import functools
import math

import jax
import jax.numpy as jnp
from jax import lax
from jax.experimental import pallas as pl
from jax.experimental.pallas import tpu as pltpu
from jax.sharding import Mesh, PartitionSpec as P

DP = ("y", "x", "zh")
SHARD = ("zl", "core")
MV = 2


LEARN_RATE = 0.01
BETA_ONE = 0.9
BETA_TWO = 0.95
EPSILON = 1e-08


def adam_update(weight, first_state, second_state, gradient):
    first_state = BETA_ONE * first_state + (1.0 - BETA_ONE) * gradient
    second_state = BETA_TWO * second_state + (1.0 - BETA_TWO) * gradient * gradient
    weight = weight - LEARN_RATE * first_state / (jnp.sqrt(second_state) + EPSILON)
    return (weight, first_state, second_state)


def send_positions(owner_devices, shard_count, slot_count):
    sources = jnp.arange(shard_count, dtype=jnp.int32)[:, None]
    moving = (owner_devices >= 0) & (owner_devices != sources)
    slot_ids = jnp.arange(slot_count)
    earlier = slot_ids[None, :] < slot_ids[:, None]
    matches = (
        (owner_devices[:, :, None] == owner_devices[:, None, :])
        & moving[:, None, :]
        & earlier[None, :, :]
    )
    return (moving, jnp.sum(matches, axis=2))


def pack_moving(values, owner_row, moving_row, position_row, shard_count, capacity):
    slot_ids = jnp.arange(values.shape[0], dtype=jnp.int32)
    targets = owner_row * capacity + position_row
    entries = jnp.arange(shard_count * capacity, dtype=jnp.int32)
    matches = (targets[None, :] == entries[:, None]) & moving_row[None, :]
    source = jnp.sum(jnp.where(matches, slot_ids[None, :], 0), axis=1)
    filled = jnp.any(matches, axis=1)
    packed = jnp.where(filled[:, None], jnp.take(values, source, axis=0), 0.0)
    return packed.reshape(shard_count, capacity, values.shape[1])


def place_blocks(
    received,
    own_values,
    owner_devices,
    destination_slot_list,
    moving,
    positions,
    my_index,
    capacity,
):
    shard_count, slot_count = owner_devices.shape
    slot_ids = jnp.arange(slot_count, dtype=jnp.int32)
    entries = (jnp.arange(shard_count, dtype=jnp.int32)[:, None] * capacity + positions).reshape(-1)
    to_me = (moving & (owner_devices == my_index)).reshape(-1)
    matches = to_me[None, :] & (destination_slot_list.reshape(-1)[None, :] == slot_ids[:, None])
    arrived = jnp.any(matches, axis=1)
    from_entry = jnp.sum(jnp.where(matches, entries[None, :], 0), axis=1)
    flattened = received.reshape(shard_count * capacity, received.shape[2])
    arrival_rows = jnp.take(flattened, from_entry, axis=0)
    stay_hit = (owner_devices[my_index] == my_index)[None, :] & (
        destination_slot_list[my_index][None, :] == slot_ids[:, None]
    )
    stayed = jnp.any(stay_hit, axis=1)
    from_slot = jnp.sum(jnp.where(stay_hit, slot_ids[None, :], 0), axis=1)
    kept_rows = jnp.take(own_values, from_slot, axis=0)
    return jnp.where(arrived[:, None], arrival_rows, jnp.where(stayed[:, None], kept_rows, 0.0))


def local_place(block_ids, first_id, local_count):
    local_ids = block_ids - first_id
    inside = (local_ids >= 0) & (local_ids < local_count)
    return jnp.where(inside, local_ids, local_count)


def general(
    hidden,
    out_grad,
    block_weight,
    block_row,
    block_col,
    live_count,
    new_owner,
    new_slot,
    first_moment,
    second_moment,
):
    shard_count = lax.axis_size(SHARD)
    dp_count = lax.axis_size(DP)
    my_index = lax.axis_index(SHARD)
    dp_index = lax.axis_index(DP)
    tokens_dev = hidden.shape[0]
    slot_count = block_weight.shape[1]
    block_size = block_weight.shape[2]
    share_size = first_moment.shape[2]
    row_blocks = hidden.shape[1] * shard_count // block_size
    col_blocks = out_grad.shape[1] * shard_count // block_size
    grad_scale = 1.0 / math.sqrt(tokens_dev * dp_count)
    slot_ids = jnp.arange(slot_count)
    live_all = slot_ids[None, :] < live_count[:, None]
    my_live = live_all[my_index]
    my_rows = block_row[my_index]
    my_cols = block_col[my_index]
    zero_bf = jnp.zeros((), jnp.bfloat16)
    full_hidden, full_grad = (
        lax.all_gather(hidden, SHARD, axis=1, tiled=True),
        lax.all_gather(out_grad, SHARD, axis=1, tiled=True),
    )
    hidden_blocks = full_hidden.reshape(tokens_dev, row_blocks, block_size)
    grad_blocks = full_grad.reshape(tokens_dev, col_blocks, block_size)
    own_hidden = jnp.take(hidden_blocks, my_rows, axis=1)
    own_grad = jnp.take(grad_blocks, my_cols, axis=1)
    grad_share = None
    col_local = col_blocks // shard_count
    row_local = row_blocks // shard_count

    def one_shard(totals, member):
        blocks, shard_index = member
        row_ids = block_row[shard_index]
        col_ids = block_col[shard_index]
        weights = jnp.where(live_all[shard_index][:, None, None], blocks, zero_bf)
        hidden_part = jnp.take(hidden_blocks, row_ids, axis=1)
        grad_part = jnp.take(grad_blocks, col_ids, axis=1)
        forward = jnp.einsum(
            "tkr,krc->tkc", hidden_part, weights, preferred_element_type=jnp.float32
        )
        backward = jnp.einsum(
            "tkc,krc->tkr", grad_part, weights, preferred_element_type=jnp.float32
        )
        col_place = local_place(col_ids, my_index * col_local, col_local)
        row_place = local_place(row_ids, my_index * row_local, row_local)
        out_total = totals[0].at[:, col_place].add(forward, mode="drop")
        back_total = totals[1].at[:, row_place].add(backward, mode="drop")
        return ((out_total, back_total), None)

    initial = (
        jnp.zeros((tokens_dev, col_local, block_size), jnp.float32),
        jnp.zeros((tokens_dev, row_local, block_size), jnp.float32),
    )
    totals = initial
    blocks_in = lax.all_gather(block_weight, SHARD, axis=0, tiled=True)
    indices = jnp.arange(blocks_in.shape[0], dtype=jnp.int32)
    totals, unused = lax.scan(one_shard, totals, (blocks_in, indices))
    out_total, back_total = totals
    projected = out_total.reshape(tokens_dev, col_local * block_size).astype(jnp.bfloat16)
    hidden_grad = back_total.reshape(tokens_dev, row_local * block_size).astype(jnp.bfloat16)
    blocks = (
        jnp.einsum("tkr,tkc->krc", own_hidden, own_grad, preferred_element_type=jnp.float32)
        * grad_scale
    )
    blocks = jnp.where(my_live[:, None, None], blocks, 0.0)
    grad_share = lax.psum_scatter(
        blocks.reshape(slot_count, block_size * block_size), DP, scatter_dimension=1, tiled=True
    )
    moving, positions = send_positions(new_owner, shard_count, slot_count)
    my_owner = new_owner[my_index]
    my_moving = moving[my_index]
    my_positions = positions[my_index]
    flat_weight = block_weight[0].reshape(slot_count, block_size * block_size)
    weight_share = lax.dynamic_slice_in_dim(
        flat_weight, dp_index * share_size, share_size, 1
    ).astype(jnp.float32)
    updated, first_state, second_state = adam_update(
        weight_share, first_moment[0], second_moment[0], grad_share
    )
    stacked = jnp.concatenate([updated, first_state, second_state], axis=1)
    packed = pack_moving(stacked, my_owner, my_moving, my_positions, shard_count, MV)
    received = lax.all_to_all(packed, SHARD, split_axis=0, concat_axis=0, tiled=True)
    placed = place_blocks(received, stacked, new_owner, new_slot, moving, positions, my_index, MV)
    new_weight = placed[:, :share_size]
    new_first = placed[:, share_size : 2 * share_size]
    new_second = placed[:, 2 * share_size :]
    return (projected, hidden_grad, new_weight[None], new_first[None], new_second[None])


WCAP = 44
GCAP = 40
PAIR = 14
UNROLL = 4
NX, NY, NZH, NZL = 4, 8, 2, 4
BS = 128
VMEM_LIMIT = 10 * 1024 * 1024
f32 = jnp.float32
bf16 = jnp.bfloat16
i32 = jnp.int32


def call(kernel, outs, n_smem, n_vmem, scratch=(), flops=0, byts=0, n_after=0):
    smem = pl.BlockSpec(memory_space=pltpu.SMEM)
    vmem = pl.BlockSpec(memory_space=pltpu.VMEM)
    anywhere = pl.BlockSpec(memory_space=pl.ANY)
    return pl.pallas_call(
        kernel,
        out_shape=outs,
        in_specs=[smem] * n_smem + [vmem] * n_vmem + [anywhere] * n_after,
        out_specs=jax.tree.map(lambda _: vmem, outs),
        scratch_shapes=list(scratch),
        compiler_params=pltpu.CompilerParams(vmem_limit_bytes=VMEM_LIMIT),
        cost_estimate=pl.CostEstimate(flops=flops, bytes_accessed=byts, transcendentals=0),
    )


def like(shape, dtype):
    return jax.ShapeDtypeStruct(shape, dtype)


def make_plan(block_row, block_col, live_count, new_owner, new_slot, row_local, me):
    shard_count, slot_count = block_row.shape
    total = shard_count * slot_count
    ids = jnp.arange(total, dtype=i32)
    live = (jnp.arange(slot_count)[None, :] < live_count[:, None]).reshape(total)
    row = block_row.reshape(total)
    col = block_col.reshape(total)
    owner = jnp.where(live, new_owner.reshape(total), -1)
    slot = new_slot.reshape(total)
    kept = owner >= 0
    row_shard = row // row_local
    key = jnp.where(kept, ids, ids + total)
    same = row_shard[:, None] == row_shard[None, :]
    before = same & live[None, :] & (key[None, :] < key[:, None])
    rank = jnp.sum(before.astype(i32), axis=1)
    earlier = same & (owner[:, None] == owner[None, :]) & (ids[None, :] < ids[:, None])
    pos = jnp.sum(earlier.astype(i32), axis=1)
    fits = (
        (jnp.max(jnp.where(live, rank, 0)) < WCAP)
        & (jnp.max(jnp.where(kept, rank, 0)) < GCAP)
        & (jnp.max(jnp.where(kept, pos, 0)) < PAIR)
    )

    here = live & (row_shard == me)
    words = ids + 256 * ((row - row_local * me) + 16 * col)
    hit = here[None, :] & (rank[None, :] == jnp.arange(WCAP)[:, None])
    code = jnp.sum(jnp.where(hit, words[None, :], 0), axis=1)
    counts = [jnp.minimum(jnp.sum(here.astype(i32)), WCAP), jnp.minimum(jnp.sum((here & kept).astype(i32)), GCAP)]
    going = jnp.where(here & kept, owner * PAIR + pos, -1)
    send_hit = going[None, :] == jnp.arange(shard_count * PAIR)[:, None]
    send = jnp.minimum(jnp.sum(jnp.where(send_hit, rank[None, :], 0), axis=1), GCAP - 1)
    owner2 = owner.reshape(shard_count, slot_count)
    sources = jnp.arange(shard_count, dtype=i32)[:, None]
    slots = jnp.arange(slot_count, dtype=i32)[None, :]
    moving, positions = send_positions(owner2, shard_count, slot_count)
    target = jnp.where(moving & (sources == me), owner2 * MV + positions, -1).reshape(total)
    state_hit = target[None, :] == jnp.arange(shard_count * MV)[:, None]
    state_send = jnp.sum(jnp.where(state_hit, (ids % slot_count)[None, :], 0), axis=1)
    state_row = jnp.where(sources == me, slots, slot_count + sources * MV + positions).reshape(total)
    landing = 1 + row_shard * PAIR + jnp.minimum(pos, PAIR - 1) + shard_count * PAIR * state_row
    lands = (owner == me)[None, :] & (slot[None, :] == jnp.arange(slot_count)[:, None])
    place = jnp.sum(jnp.where(lands, landing[None, :], 0), axis=1)
    return fits, code, counts, send, state_send, place


def grad_kernel(info, code, hidden, mine, other, out, cols, hidden_t, total):
    my_core = info[2]
    for zl in range(NZL):
        for sub in range(4):
            lanes = slice(sub * BS, (sub + 1) * BS)
            cols[(2 * zl + my_core) * 4 + sub] = mine[zl, :, lanes]
            cols[(2 * zl + 1 - my_core) * 4 + sub] = other[zl, :, lanes]
    row_local = hidden.shape[1] // BS
    for r in range(row_local):
        hidden_t[r] = hidden[:, r * BS : (r + 1) * BS].T

    def step(i, carry):
        blocks = []
        for u in range(UNROLL):
            word = code[i * UNROLL + u]
            blocks.append(jnp.dot(hidden_t[(word >> 8) & 15], cols[word >> 12], preferred_element_type=f32))
        for u in range(UNROLL):
            total[pl.ds(i * UNROLL + u, BS, stride=GCAP), :] = blocks[u]
        return carry

    lax.fori_loop(0, (info[1] + UNROLL - 1) // UNROLL, step, 0)
    for x in range(NX):
        for y in range(NY):
            for q in range(4):
                source = 16 * y + 4 * x + q
                out[x, 4 * y + q] = total[source * GCAP : (source + 1) * GCAP, :].astype(bf16)


def sum_kernel(parts, _after, out):
    def step(i, carry):
        value = parts[0, i].astype(f32)
        for n in range(1, parts.shape[0]):
            value += parts[n, i].astype(f32)
        out[i] = value.astype(bf16)
        return carry

    lax.fori_loop(0, out.shape[0], step, 0, unroll=4)


def share_kernel(scale, send, state_send, parts, stacked, out, total):
    total[...] = parts[0].astype(f32)

    def step(n, carry):
        total[...] += parts[n].astype(f32)
        return carry

    lax.fori_loop(1, parts.shape[0], step, 0)
    total[...] = total[...] * scale
    width = stacked.shape[1] // BS
    for d in range(out.shape[0]):
        for p in range(PAIR):
            rank = send[d * PAIR + p]
            for b in range(2):
                out[d, 2 * p + b : 2 * p + b + 1, :] = total[b, pl.ds(rank, 1), :]
        for p in range(MV):
            row = stacked[pl.ds(state_send[d * MV + p], 1), :]
            for n in range(width):
                at = 2 * PAIR + width * p + n
                out[d, at : at + 1, :] = row[:, n * BS : (n + 1) * BS]


def select_kernel(info, code, gathered, _after, out):
    def step(c, carry):
        value = gathered[code[c] & 255]
        out[c] = jnp.where(c < info[0], value, jnp.zeros_like(value))
        return carry

    lax.fori_loop(0, WCAP, step, 0, unroll=4)


def forward_kernel(info, code, hidden, quarters, _after, mine, theirs, weights, total, sems):
    my_core = info[2]
    copies = [pltpu.make_async_copy(quarters.at[x], weights.at[:, x], sems.at[x]) for x in range(NX)]
    for copy in copies:
        copy.start()
    total[...] = jnp.zeros_like(total)
    for copy in copies:
        copy.wait()

    def step(i, carry):
        adds = []
        for u in range(UNROLL):
            c = i * UNROLL + u
            word = code[c]
            lanes = pl.ds(pl.multiple_of(((word >> 8) & 15) * BS, BS), BS)
            w = weights[c].reshape(BS, BS)
            adds.append((word >> 12, jnp.dot(hidden[:, lanes], w, preferred_element_type=f32)))
        for col, value in adds:
            total[col] += value
        return carry

    lax.fori_loop(0, (info[0] + UNROLL - 1) // UNROLL, step, 0)
    for zl in range(NZL):
        for sub in range(4):
            mine[zl, sub] = total[(2 * zl + my_core) * 4 + sub]
            theirs[zl, sub] = total[(2 * zl + 1 - my_core) * 4 + sub]


def backward_kernel(info, code, cols, weights, back, total):
    total[...] = jnp.zeros_like(total)

    def step(i, carry):
        adds = []
        for u in range(UNROLL):
            c = i * UNROLL + u
            word = code[c]
            w = weights[c].reshape(BS, BS)
            value = lax.dot_general(cols[word >> 12], w, (((1,), (1,)), ((), ())), preferred_element_type=f32)
            adds.append(((word >> 8) & 15, value))
        for r, value in adds:
            total[r] += value
        return carry

    lax.fori_loop(0, (info[0] + UNROLL - 1) // UNROLL, step, 0)
    for r in range(total.shape[0]):
        back[:, r * BS : (r + 1) * BS] = total[r].astype(bf16)


def chip_kernel(info, mine, came, _after, own, s1, s2, s3):
    my_zl = info[4]
    own[...] = mine[my_zl] + came[my_zl]
    for k, out in enumerate((s1, s2, s3)):
        zl = (my_zl + k + 1) % NZL
        out[...] = (mine[zl] + came[zl]).astype(bf16)


def project_kernel(own, r1, r2, r3, out):
    for sub in range(4):
        value = own[sub] + r1[sub].astype(f32) + r2[sub].astype(f32) + r3[sub].astype(f32)
        out[:, sub * BS : (sub + 1) * BS] = value.astype(bf16)


def adam_kernel(place, stacked, came, new_w, new_m, new_v, rows, grad):
    slots, share = new_w.shape
    places = came.shape[0] * PAIR
    width = stacked.shape[1] // BS
    for j in range(slots):
        word = jnp.maximum(place[j] - 1, 0)
        g, row = word % places, word // places
        filled = place[j] > 0
        here = row < slots
        entry = jnp.maximum(row - slots, 0)
        own = stacked[pl.ds(jnp.minimum(row, slots - 1), 1), :]
        for n in range(width):
            lanes = slice(n * BS, (n + 1) * BS)
            moved = came[entry // MV, pl.ds(2 * PAIR + width * (entry % MV) + n, 1), :]
            rows[j : j + 1, lanes] = jnp.where(filled, jnp.where(here, own[:, lanes], moved), 0.0)
        for b in range(2):
            value = came[g // PAIR, pl.ds(2 * (g % PAIR) + b, 1), :]
            grad[j : j + 1, b * BS : (b + 1) * BS] = jnp.where(filled, value, 0.0)
    w, m, v = adam_update(rows[:, :share], rows[:, share : 2 * share], rows[:, 2 * share :], grad[...])
    new_w[...] = w
    new_m[...] = m
    new_v[...] = v


def all_to_all(values, axis):
    return lax.all_to_all(values, axis, split_axis=0, concat_axis=0, tiled=True)


def shift(values, axis, count, step):
    return lax.ppermute(values, axis, [(i, (i + step) % count) for i in range(count)])


def shards(
    hidden,
    out_grad,
    block_weight,
    block_row,
    block_col,
    live_count,
    new_owner,
    new_slot,
    first_moment,
    second_moment,
):
    shard_count = lax.axis_size(SHARD)
    me = lax.axis_index(SHARD)
    dp_index = lax.axis_index(DP)
    x_index = lax.axis_index("x")
    tokens = hidden.shape[0]
    slot_count = block_weight.shape[1]
    row_local = hidden.shape[1] // BS
    share = first_moment.shape[2]
    scale = 1.0 / math.sqrt(tokens * lax.axis_size(DP))

    mine = all_to_all(jnp.broadcast_to(out_grad[None], (NZL,) + out_grad.shape), "zl")
    other = shift(mine, "core", 2, 1)
    quarter = lax.dynamic_slice_in_dim(block_weight[0], x_index * (BS // NX), BS // NX, 1)
    gathered = lax.all_gather(quarter, SHARD, axis=0, tiled=True)
    weight_share = lax.dynamic_slice_in_dim(block_weight[0], dp_index * 2, 2, 1).reshape(slot_count, share)
    stacked = jnp.concatenate([weight_share.astype(f32), first_moment[0], second_moment[0]], axis=1)

    fits, code, counts, send, state_send, place = make_plan(
        block_row, block_col, live_count, new_owner, new_slot, row_local, me
    )
    info = jnp.stack(counts + [lax.axis_index("core"), x_index, lax.axis_index("zl"), lax.axis_index("zh")])

    partial, cols = call(
        grad_kernel,
        (like((NX, NY * NZH * 2, GCAP, BS), bf16), like((shard_count * 4, BS, BS), bf16)),
        2,
        3,
        [pltpu.VMEM((row_local, BS, BS), bf16), pltpu.VMEM((BS * GCAP, BS), f32)],
        flops=2 * WCAP * BS**3,
        byts=4 * 1024 * 1024,
    )(info, code, hidden, mine, other)
    along_x = all_to_all(partial, "x")
    picked = call(select_kernel, like((WCAP, BS // NX, BS), bf16), 2, 1, byts=1024 * 1024, n_after=1)(
        info, code, gathered, along_x
    )
    quarters = lax.all_gather(picked, "x", axis=0)

    summed = call(sum_kernel, like(partial.shape[1:], bf16), 0, 1, byts=2 * 1024 * 1024, n_after=1)(along_x, picked)
    along_yz = all_to_all(summed.reshape(NY * NZH, 2, GCAP, BS), ("y", "zh"))
    packed = call(
        functools.partial(share_kernel, scale),
        like((shard_count, 2 * PAIR + MV * stacked.shape[1] // BS, BS), f32),
        2,
        2,
        [pltpu.VMEM((2, GCAP, BS), f32)],
        byts=1024 * 1024,
    )(send, state_send, along_yz, stacked)
    shares = all_to_all(packed, SHARD)

    out_mine, out_theirs, weights = call(
        forward_kernel,
        (
            like((NZL, 4, tokens, BS), f32),
            like((NZL, 4, tokens, BS), f32),
            like((WCAP, NX, BS // NX, BS), bf16),
        ),
        2,
        1,
        [pltpu.VMEM((shard_count * 4, tokens, BS), f32), pltpu.SemaphoreType.DMA((NX,))],
        flops=2 * WCAP * BS**3,
        byts=8 * 1024 * 1024,
        n_after=2,
    )(info, code, hidden, quarters, packed)
    came = shift(out_theirs, "core", 2, 1)
    hidden_grad = call(
        backward_kernel,
        like(hidden.shape, bf16),
        2,
        2,
        [pltpu.VMEM((row_local, tokens, BS), f32)],
        flops=2 * WCAP * BS**3,
        byts=4 * 1024 * 1024,
    )(info, code, cols, weights)
    part = (4, tokens, BS)
    own, s1, s2, s3 = call(
        chip_kernel, (like(part, f32),) + (like(part, bf16),) * 3, 1, 2, byts=3 * 1024 * 1024, n_after=1
    )(info, out_mine, came, hidden_grad)
    r2, r1, r3 = (shift(s, "zl", NZL, k) for k, s in ((2, s2), (1, s1), (3, s3)))
    projected = call(project_kernel, like(out_grad.shape, bf16), 0, 4, byts=1024 * 1024)(own, r1, r2, r3)

    shape = like((slot_count, share), f32)
    new_weight, new_first, new_second = call(
        adam_kernel,
        (shape, shape, shape),
        1,
        2,
        [pltpu.VMEM((slot_count, 3 * share), f32), pltpu.VMEM((slot_count, share), f32)],
        byts=1024 * 1024,
    )(place, stacked, shares)
    result = (projected, hidden_grad, new_weight[None], new_first[None], new_second[None])
    return lax.cond(
        fits,
        lambda: result,
        lambda: general(
            hidden,
            out_grad,
            block_weight,
            block_row,
            block_col,
            live_count,
            new_owner,
            new_slot,
            first_moment,
            second_moment,
        ),
    )


def solution(mesh):
    split = Mesh(mesh.devices.reshape(NY, NX, NZH, NZL, 2), ("y", "x", "zh", "zl", "core"))
    in_specs = (
        P(DP, SHARD),
        P(DP, SHARD),
        P(SHARD, None, None, None),
        P(),
        P(),
        P(),
        P(),
        P(),
        P(SHARD, None, DP),
        P(SHARD, None, DP),
    )
    out_specs = (
        P(DP, SHARD),
        P(DP, SHARD),
        P(SHARD, None, DP),
        P(SHARD, None, DP),
        P(SHARD, None, DP),
    )
    return jax.shard_map(shards, mesh=split, in_specs=in_specs, out_specs=out_specs, check_vma=False)
```

```python
import functools
import math

import jax
import jax.numpy as jnp
from jax import lax
from jax.experimental import pallas as pl
from jax.experimental.pallas import tpu as pltpu
from jax.sharding import Mesh, PartitionSpec as P

DP = ("y", "x", "zh")
SHARD = ("zl", "core")
MV = 2


LEARN_RATE = 0.01
BETA_ONE = 0.9
BETA_TWO = 0.95
EPSILON = 1e-08


def adam_update(weight, first_state, second_state, gradient):
    first_state = BETA_ONE * first_state + (1.0 - BETA_ONE) * gradient
    second_state = BETA_TWO * second_state + (1.0 - BETA_TWO) * gradient * gradient
    weight = weight - LEARN_RATE * first_state / (jnp.sqrt(second_state) + EPSILON)
    return (weight, first_state, second_state)


def send_positions(owner_devices, shard_count, slot_count):
    sources = jnp.arange(shard_count, dtype=jnp.int32)[:, None]
    moving = (owner_devices >= 0) & (owner_devices != sources)
    slot_ids = jnp.arange(slot_count)
    earlier = slot_ids[None, :] < slot_ids[:, None]
    matches = (
        (owner_devices[:, :, None] == owner_devices[:, None, :])
        & moving[:, None, :]
        & earlier[None, :, :]
    )
    return (moving, jnp.sum(matches, axis=2))


def pack_moving(values, owner_row, moving_row, position_row, shard_count, capacity):
    slot_ids = jnp.arange(values.shape[0], dtype=jnp.int32)
    targets = owner_row * capacity + position_row
    entries = jnp.arange(shard_count * capacity, dtype=jnp.int32)
    matches = (targets[None, :] == entries[:, None]) & moving_row[None, :]
    source = jnp.sum(jnp.where(matches, slot_ids[None, :], 0), axis=1)
    filled = jnp.any(matches, axis=1)
    packed = jnp.where(filled[:, None], jnp.take(values, source, axis=0), 0.0)
    return packed.reshape(shard_count, capacity, values.shape[1])


def place_blocks(
    received,
    own_values,
    owner_devices,
    destination_slot_list,
    moving,
    positions,
    my_index,
    capacity,
):
    shard_count, slot_count = owner_devices.shape
    slot_ids = jnp.arange(slot_count, dtype=jnp.int32)
    entries = (jnp.arange(shard_count, dtype=jnp.int32)[:, None] * capacity + positions).reshape(-1)
    to_me = (moving & (owner_devices == my_index)).reshape(-1)
    matches = to_me[None, :] & (destination_slot_list.reshape(-1)[None, :] == slot_ids[:, None])
    arrived = jnp.any(matches, axis=1)
    from_entry = jnp.sum(jnp.where(matches, entries[None, :], 0), axis=1)
    flattened = received.reshape(shard_count * capacity, received.shape[2])
    arrival_rows = jnp.take(flattened, from_entry, axis=0)
    stay_hit = (owner_devices[my_index] == my_index)[None, :] & (
        destination_slot_list[my_index][None, :] == slot_ids[:, None]
    )
    stayed = jnp.any(stay_hit, axis=1)
    from_slot = jnp.sum(jnp.where(stay_hit, slot_ids[None, :], 0), axis=1)
    kept_rows = jnp.take(own_values, from_slot, axis=0)
    return jnp.where(arrived[:, None], arrival_rows, jnp.where(stayed[:, None], kept_rows, 0.0))


def local_place(block_ids, first_id, local_count):
    local_ids = block_ids - first_id
    inside = (local_ids >= 0) & (local_ids < local_count)
    return jnp.where(inside, local_ids, local_count)


def general(
    hidden,
    out_grad,
    block_weight,
    block_row,
    block_col,
    live_count,
    new_owner,
    new_slot,
    first_moment,
    second_moment,
):
    shard_count = lax.axis_size(SHARD)
    dp_count = lax.axis_size(DP)
    my_index = lax.axis_index(SHARD)
    dp_index = lax.axis_index(DP)
    tokens_dev = hidden.shape[0]
    slot_count = block_weight.shape[1]
    block_size = block_weight.shape[2]
    share_size = first_moment.shape[2]
    row_blocks = hidden.shape[1] * shard_count // block_size
    col_blocks = out_grad.shape[1] * shard_count // block_size
    grad_scale = 1.0 / math.sqrt(tokens_dev * dp_count)
    slot_ids = jnp.arange(slot_count)
    live_all = slot_ids[None, :] < live_count[:, None]
    my_live = live_all[my_index]
    my_rows = block_row[my_index]
    my_cols = block_col[my_index]
    zero_bf = jnp.zeros((), jnp.bfloat16)
    full_hidden, full_grad = (
        lax.all_gather(hidden, SHARD, axis=1, tiled=True),
        lax.all_gather(out_grad, SHARD, axis=1, tiled=True),
    )
    hidden_blocks = full_hidden.reshape(tokens_dev, row_blocks, block_size)
    grad_blocks = full_grad.reshape(tokens_dev, col_blocks, block_size)
    own_hidden = jnp.take(hidden_blocks, my_rows, axis=1)
    own_grad = jnp.take(grad_blocks, my_cols, axis=1)
    grad_share = None
    col_local = col_blocks // shard_count
    row_local = row_blocks // shard_count

    def one_shard(totals, member):
        blocks, shard_index = member
        row_ids = block_row[shard_index]
        col_ids = block_col[shard_index]
        weights = jnp.where(live_all[shard_index][:, None, None], blocks, zero_bf)
        hidden_part = jnp.take(hidden_blocks, row_ids, axis=1)
        grad_part = jnp.take(grad_blocks, col_ids, axis=1)
        forward = jnp.einsum(
            "tkr,krc->tkc", hidden_part, weights, preferred_element_type=jnp.float32
        )
        backward = jnp.einsum(
            "tkc,krc->tkr", grad_part, weights, preferred_element_type=jnp.float32
        )
        col_place = local_place(col_ids, my_index * col_local, col_local)
        row_place = local_place(row_ids, my_index * row_local, row_local)
        out_total = totals[0].at[:, col_place].add(forward, mode="drop")
        back_total = totals[1].at[:, row_place].add(backward, mode="drop")
        return ((out_total, back_total), None)

    initial = (
        jnp.zeros((tokens_dev, col_local, block_size), jnp.float32),
        jnp.zeros((tokens_dev, row_local, block_size), jnp.float32),
    )
    totals = initial
    blocks_in = lax.all_gather(block_weight, SHARD, axis=0, tiled=True)
    indices = jnp.arange(blocks_in.shape[0], dtype=jnp.int32)
    totals, unused = lax.scan(one_shard, totals, (blocks_in, indices))
    out_total, back_total = totals
    projected = out_total.reshape(tokens_dev, col_local * block_size).astype(jnp.bfloat16)
    hidden_grad = back_total.reshape(tokens_dev, row_local * block_size).astype(jnp.bfloat16)
    blocks = (
        jnp.einsum("tkr,tkc->krc", own_hidden, own_grad, preferred_element_type=jnp.float32)
        * grad_scale
    )
    blocks = jnp.where(my_live[:, None, None], blocks, 0.0)
    grad_share = lax.psum_scatter(
        blocks.reshape(slot_count, block_size * block_size), DP, scatter_dimension=1, tiled=True
    )
    moving, positions = send_positions(new_owner, shard_count, slot_count)
    my_owner = new_owner[my_index]
    my_moving = moving[my_index]
    my_positions = positions[my_index]
    flat_weight = block_weight[0].reshape(slot_count, block_size * block_size)
    weight_share = lax.dynamic_slice_in_dim(
        flat_weight, dp_index * share_size, share_size, 1
    ).astype(jnp.float32)
    updated, first_state, second_state = adam_update(
        weight_share, first_moment[0], second_moment[0], grad_share
    )
    stacked = jnp.concatenate([updated, first_state, second_state], axis=1)
    packed = pack_moving(stacked, my_owner, my_moving, my_positions, shard_count, MV)
    received = lax.all_to_all(packed, SHARD, split_axis=0, concat_axis=0, tiled=True)
    placed = place_blocks(received, stacked, new_owner, new_slot, moving, positions, my_index, MV)
    new_weight = placed[:, :share_size]
    new_first = placed[:, share_size : 2 * share_size]
    new_second = placed[:, 2 * share_size :]
    return (projected, hidden_grad, new_weight[None], new_first[None], new_second[None])


WCAP = 44
GCAP = 40
PAIR = 14
UNROLL = 4
NX, NY, NZH, NZL = 4, 8, 2, 4
BS = 128
VMEM_LIMIT = 10 * 1024 * 1024
f32 = jnp.float32
bf16 = jnp.bfloat16
i32 = jnp.int32


def call(kernel, outs, n_smem, n_vmem, scratch=(), flops=0, byts=0, n_after=0):
    smem = pl.BlockSpec(memory_space=pltpu.SMEM)
    vmem = pl.BlockSpec(memory_space=pltpu.VMEM)
    anywhere = pl.BlockSpec(memory_space=pl.ANY)
    return pl.pallas_call(
        kernel,
        out_shape=outs,
        in_specs=[smem] * n_smem + [vmem] * n_vmem + [anywhere] * n_after,
        out_specs=jax.tree.map(lambda _: vmem, outs),
        scratch_shapes=list(scratch),
        compiler_params=pltpu.CompilerParams(vmem_limit_bytes=VMEM_LIMIT),
        cost_estimate=pl.CostEstimate(flops=flops, bytes_accessed=byts, transcendentals=0),
    )


def like(shape, dtype):
    return jax.ShapeDtypeStruct(shape, dtype)


def make_plan(block_row, block_col, live_count, new_owner, new_slot, row_local, me):
    shard_count, slot_count = block_row.shape
    total = shard_count * slot_count
    ids = jnp.arange(total, dtype=i32)
    live = (jnp.arange(slot_count)[None, :] < live_count[:, None]).reshape(total)
    row = block_row.reshape(total)
    col = block_col.reshape(total)
    owner = jnp.where(live, new_owner.reshape(total), -1)
    slot = new_slot.reshape(total)
    kept = owner >= 0
    row_shard = row // row_local
    key = jnp.where(kept, ids, ids + total)
    same = row_shard[:, None] == row_shard[None, :]
    before = same & live[None, :] & (key[None, :] < key[:, None])
    rank = jnp.sum(before.astype(i32), axis=1)
    earlier = same & (owner[:, None] == owner[None, :]) & (ids[None, :] < ids[:, None])
    pos = jnp.sum(earlier.astype(i32), axis=1)
    fits = (
        (jnp.max(jnp.where(live, rank, 0)) < WCAP)
        & (jnp.max(jnp.where(kept, rank, 0)) < GCAP)
        & (jnp.max(jnp.where(kept, pos, 0)) < PAIR)
    )

    here = live & (row_shard == me)
    words = ids + 256 * ((row - row_local * me) + 16 * col)
    hit = here[None, :] & (rank[None, :] == jnp.arange(WCAP)[:, None])
    code = jnp.sum(jnp.where(hit, words[None, :], 0), axis=1)
    counts = [jnp.minimum(jnp.sum(here.astype(i32)), WCAP), jnp.minimum(jnp.sum((here & kept).astype(i32)), GCAP)]
    going = jnp.where(here & kept, owner * PAIR + pos, -1)
    send_hit = going[None, :] == jnp.arange(shard_count * PAIR)[:, None]
    send = jnp.minimum(jnp.sum(jnp.where(send_hit, rank[None, :], 0), axis=1), GCAP - 1)
    owner2 = owner.reshape(shard_count, slot_count)
    sources = jnp.arange(shard_count, dtype=i32)[:, None]
    slots = jnp.arange(slot_count, dtype=i32)[None, :]
    moving, positions = send_positions(owner2, shard_count, slot_count)
    target = jnp.where(moving & (sources == me), owner2 * MV + positions, -1).reshape(total)
    state_hit = target[None, :] == jnp.arange(shard_count * MV)[:, None]
    state_send = jnp.sum(jnp.where(state_hit, (ids % slot_count)[None, :], 0), axis=1)
    state_row = jnp.where(sources == me, slots, slot_count + sources * MV + positions).reshape(total)
    landing = 1 + row_shard * PAIR + jnp.minimum(pos, PAIR - 1) + shard_count * PAIR * state_row
    lands = (owner == me)[None, :] & (slot[None, :] == jnp.arange(slot_count)[:, None])
    place = jnp.sum(jnp.where(lands, landing[None, :], 0), axis=1)
    return fits, code, counts, send, state_send, place


def grad_kernel(info, code, hidden, mine, other, out, cols, hidden_t, total):
    my_core = info[2]
    for zl in range(NZL):
        for sub in range(4):
            lanes = slice(sub * BS, (sub + 1) * BS)
            cols[(2 * zl + my_core) * 4 + sub] = mine[zl, :, lanes]
            cols[(2 * zl + 1 - my_core) * 4 + sub] = other[zl, :, lanes]
    row_local = hidden.shape[1] // BS
    for r in range(row_local):
        hidden_t[r] = hidden[:, r * BS : (r + 1) * BS].T

    def step(i, carry):
        blocks = []
        for u in range(UNROLL):
            word = code[i * UNROLL + u]
            blocks.append(jnp.dot(hidden_t[(word >> 8) & 15], cols[word >> 12], preferred_element_type=f32))
        for u in range(UNROLL):
            total[pl.ds(i * UNROLL + u, BS, stride=GCAP), :] = blocks[u]
        return carry

    lax.fori_loop(0, (info[1] + UNROLL - 1) // UNROLL, step, 0)
    for x in range(NX):
        for y in range(NY):
            for q in range(4):
                source = 16 * y + 4 * x + q
                out[x, 4 * y + q] = total[source * GCAP : (source + 1) * GCAP, :].astype(bf16)


def share_kernel(scale, send, state_send, parts, stacked, out, total):
    total[...] = parts[0].astype(f32)

    def step(n, carry):
        total[...] += parts[n].astype(f32)
        return carry

    lax.fori_loop(1, parts.shape[0], step, 0)
    total[...] = total[...] * scale
    width = stacked.shape[1] // BS
    for d in range(out.shape[0]):
        for p in range(PAIR):
            rank = send[d * PAIR + p]
            for b in range(2):
                out[d, 2 * p + b : 2 * p + b + 1, :] = total[b, pl.ds(rank, 1), :]
        for p in range(MV):
            row = stacked[pl.ds(state_send[d * MV + p], 1), :]
            for n in range(width):
                at = 2 * PAIR + width * p + n
                out[d, at : at + 1, :] = row[:, n * BS : (n + 1) * BS]


def select_sum_kernel(info, code, gathered, parts, picked, summed):
    def select(c, carry):
        value = gathered[code[c] & 255]
        picked[c] = jnp.where(c < info[0], value, jnp.zeros_like(value))
        return carry

    def add(i, carry):
        value = parts[0, i].astype(f32)
        for n in range(1, parts.shape[0]):
            value += parts[n, i].astype(f32)
        summed[i] = value.astype(bf16)
        return carry

    lax.fori_loop(0, WCAP, select, 0, unroll=4)
    lax.fori_loop(0, summed.shape[0], add, 0, unroll=4)


def forward_kernel(info, code, hidden, quarters, _after, mine, theirs, weights, total, sems):
    my_core = info[2]
    copies = [pltpu.make_async_copy(quarters.at[x], weights.at[:, x], sems.at[x]) for x in range(NX)]
    for copy in copies:
        copy.start()
    total[...] = jnp.zeros_like(total)
    for copy in copies:
        copy.wait()

    def step(i, carry):
        adds = []
        for u in range(UNROLL):
            c = i * UNROLL + u
            word = code[c]
            lanes = pl.ds(pl.multiple_of(((word >> 8) & 15) * BS, BS), BS)
            w = weights[c].reshape(BS, BS)
            adds.append((word >> 12, jnp.dot(hidden[:, lanes], w, preferred_element_type=f32)))
        for col, value in adds:
            total[col] += value
        return carry

    lax.fori_loop(0, (info[0] + UNROLL - 1) // UNROLL, step, 0)
    for zl in range(NZL):
        for sub in range(4):
            mine[zl, sub] = total[(2 * zl + my_core) * 4 + sub]
            theirs[zl, sub] = total[(2 * zl + 1 - my_core) * 4 + sub]


def backward_kernel(info, code, cols, weights, back, total):
    total[...] = jnp.zeros_like(total)

    def step(i, carry):
        adds = []
        for u in range(UNROLL):
            c = i * UNROLL + u
            word = code[c]
            w = weights[c].reshape(BS, BS)
            value = lax.dot_general(cols[word >> 12], w, (((1,), (1,)), ((), ())), preferred_element_type=f32)
            adds.append(((word >> 8) & 15, value))
        for r, value in adds:
            total[r] += value
        return carry

    lax.fori_loop(0, (info[0] + UNROLL - 1) // UNROLL, step, 0)
    for r in range(total.shape[0]):
        back[:, r * BS : (r + 1) * BS] = total[r].astype(bf16)


def chip_kernel(info, mine, came, own, s1, s2, s3):
    my_zl = info[4]
    own[...] = mine[my_zl] + came[my_zl]
    for k, out in enumerate((s1, s2, s3)):
        zl = (my_zl + k + 1) % NZL
        out[...] = (mine[zl] + came[zl]).astype(bf16)


def project_kernel(own, r1, r2, r3, _after, out):
    for sub in range(4):
        value = own[sub] + r1[sub].astype(f32) + r2[sub].astype(f32) + r3[sub].astype(f32)
        out[:, sub * BS : (sub + 1) * BS] = value.astype(bf16)


def adam_kernel(place, stacked, came, _after, new_w, new_m, new_v, rows, grad):
    slots, share = new_w.shape
    places = came.shape[0] * PAIR
    width = stacked.shape[1] // BS
    for j in range(slots):
        word = jnp.maximum(place[j] - 1, 0)
        g, row = word % places, word // places
        filled = place[j] > 0
        here = row < slots
        entry = jnp.maximum(row - slots, 0)
        own = stacked[pl.ds(jnp.minimum(row, slots - 1), 1), :]
        for n in range(width):
            lanes = slice(n * BS, (n + 1) * BS)
            moved = came[entry // MV, pl.ds(2 * PAIR + width * (entry % MV) + n, 1), :]
            rows[j : j + 1, lanes] = jnp.where(filled, jnp.where(here, own[:, lanes], moved), 0.0)
        for b in range(2):
            value = came[g // PAIR, pl.ds(2 * (g % PAIR) + b, 1), :]
            grad[j : j + 1, b * BS : (b + 1) * BS] = jnp.where(filled, value, 0.0)
    w, m, v = adam_update(rows[:, :share], rows[:, share : 2 * share], rows[:, 2 * share :], grad[...])
    new_w[...] = w
    new_m[...] = m
    new_v[...] = v


def all_to_all(values, axis):
    return lax.all_to_all(values, axis, split_axis=0, concat_axis=0, tiled=True)


def shift(values, axis, count, step):
    return lax.ppermute(values, axis, [(i, (i + step) % count) for i in range(count)])


def shards(
    hidden,
    out_grad,
    block_weight,
    block_row,
    block_col,
    live_count,
    new_owner,
    new_slot,
    first_moment,
    second_moment,
):
    shard_count = lax.axis_size(SHARD)
    me = lax.axis_index(SHARD)
    dp_index = lax.axis_index(DP)
    x_index = lax.axis_index("x")
    tokens = hidden.shape[0]
    slot_count = block_weight.shape[1]
    row_local = hidden.shape[1] // BS
    share = first_moment.shape[2]
    scale = 1.0 / math.sqrt(tokens * lax.axis_size(DP))

    quarter = lax.dynamic_slice_in_dim(block_weight[0], x_index * (BS // NX), BS // NX, 1)
    quarter, sent = lax.optimization_barrier((quarter, out_grad))
    gathered = lax.all_gather(quarter, SHARD, axis=0, tiled=True)
    mine = all_to_all(jnp.broadcast_to(sent[None], (NZL,) + out_grad.shape), "zl")
    other = shift(mine, "core", 2, 1)
    weight_share = lax.dynamic_slice_in_dim(block_weight[0], dp_index * 2, 2, 1).reshape(slot_count, share)
    stacked = jnp.concatenate([weight_share.astype(f32), first_moment[0], second_moment[0]], axis=1)

    fits, code, counts, send, state_send, place = make_plan(
        block_row, block_col, live_count, new_owner, new_slot, row_local, me
    )
    info = jnp.stack(counts + [lax.axis_index("core"), x_index, lax.axis_index("zl"), lax.axis_index("zh")])

    partial, cols = call(
        grad_kernel,
        (like((NX, NY * NZH * 2, GCAP, BS), bf16), like((shard_count * 4, BS, BS), bf16)),
        2,
        3,
        [pltpu.VMEM((row_local, BS, BS), bf16), pltpu.VMEM((BS * GCAP, BS), f32)],
        flops=2 * WCAP * BS**3,
        byts=4 * 1024 * 1024,
    )(info, code, hidden, mine, other)
    along_x = all_to_all(partial, "x")
    picked, summed = call(
        select_sum_kernel,
        (like((WCAP, BS // NX, BS), bf16), like(partial.shape[1:], bf16)),
        2,
        2,
        byts=4 * 1024 * 1024,
    )(info, code, gathered, along_x)
    quarters = lax.all_gather(picked, "x", axis=0)
    along_yz = all_to_all(summed.reshape(NY * NZH, 2, GCAP, BS), ("y", "zh"))
    packed = call(
        functools.partial(share_kernel, scale),
        like((shard_count, 2 * PAIR + MV * stacked.shape[1] // BS, BS), f32),
        2,
        2,
        [pltpu.VMEM((2, GCAP, BS), f32)],
        byts=1024 * 1024,
    )(send, state_send, along_yz, stacked)
    shares = all_to_all(packed, SHARD)

    out_mine, out_theirs, weights = call(
        forward_kernel,
        (
            like((NZL, 4, tokens, BS), f32),
            like((NZL, 4, tokens, BS), f32),
            like((WCAP, NX, BS // NX, BS), bf16),
        ),
        2,
        1,
        [pltpu.VMEM((shard_count * 4, tokens, BS), f32), pltpu.SemaphoreType.DMA((NX,))],
        flops=2 * WCAP * BS**3,
        byts=8 * 1024 * 1024,
        n_after=2,
    )(info, code, hidden, quarters, packed)
    came = shift(out_theirs, "core", 2, 1)
    hidden_grad = call(
        backward_kernel,
        like(hidden.shape, bf16),
        2,
        2,
        [pltpu.VMEM((row_local, tokens, BS), f32)],
        flops=2 * WCAP * BS**3,
        byts=4 * 1024 * 1024,
    )(info, code, cols, weights)
    part = (4, tokens, BS)
    own, s1, s2, s3 = call(
        chip_kernel, (like(part, f32),) + (like(part, bf16),) * 3, 1, 2, byts=3 * 1024 * 1024
    )(info, out_mine, came)
    r2, r1, r3 = (shift(s, "zl", NZL, k) for k, s in ((2, s2), (1, s1), (3, s3)))
    projected = call(project_kernel, like(out_grad.shape, bf16), 0, 4, byts=1024 * 1024, n_after=1)(
        own, r1, r2, r3, hidden_grad
    )

    shape = like((slot_count, share), f32)
    new_weight, new_first, new_second = call(
        adam_kernel,
        (shape, shape, shape),
        1,
        2,
        [pltpu.VMEM((slot_count, 3 * share), f32), pltpu.VMEM((slot_count, share), f32)],
        byts=1024 * 1024,
        n_after=1,
    )(place, stacked, shares, hidden_grad)
    result = (projected, hidden_grad, new_weight[None], new_first[None], new_second[None])
    return lax.cond(
        fits,
        lambda: result,
        lambda: general(
            hidden,
            out_grad,
            block_weight,
            block_row,
            block_col,
            live_count,
            new_owner,
            new_slot,
            first_moment,
            second_moment,
        ),
    )


def solution(mesh):
    split = Mesh(mesh.devices.reshape(NY, NX, NZH, NZL, 2), ("y", "x", "zh", "zl", "core"))
    in_specs = (
        P(DP, SHARD),
        P(DP, SHARD),
        P(SHARD, None, None, None),
        P(),
        P(),
        P(),
        P(),
        P(),
        P(SHARD, None, DP),
        P(SHARD, None, DP),
    )
    out_specs = (
        P(DP, SHARD),
        P(DP, SHARD),
        P(SHARD, None, DP),
        P(SHARD, None, DP),
        P(SHARD, None, DP),
    )
    return jax.shard_map(shards, mesh=split, in_specs=in_specs, out_specs=out_specs, check_vma=False)
```

```python
import functools
import math

import jax
import jax.numpy as jnp
from jax import lax
from jax.experimental import pallas as pl
from jax.experimental.pallas import tpu as pltpu
from jax.sharding import Mesh, PartitionSpec as P

DP = ("y", "x", "zh")
SHARD = ("zl", "core")
MV = 2


LEARN_RATE = 0.01
BETA_ONE = 0.9
BETA_TWO = 0.95
EPSILON = 1e-08


def adam_update(weight, first_state, second_state, gradient):
    first_state = BETA_ONE * first_state + (1.0 - BETA_ONE) * gradient
    second_state = BETA_TWO * second_state + (1.0 - BETA_TWO) * gradient * gradient
    weight = weight - LEARN_RATE * first_state / (jnp.sqrt(second_state) + EPSILON)
    return (weight, first_state, second_state)


def send_positions(owner_devices, shard_count, slot_count):
    sources = jnp.arange(shard_count, dtype=jnp.int32)[:, None]
    moving = (owner_devices >= 0) & (owner_devices != sources)
    slot_ids = jnp.arange(slot_count)
    earlier = slot_ids[None, :] < slot_ids[:, None]
    matches = (
        (owner_devices[:, :, None] == owner_devices[:, None, :])
        & moving[:, None, :]
        & earlier[None, :, :]
    )
    return (moving, jnp.sum(matches, axis=2))


def pack_moving(values, owner_row, moving_row, position_row, shard_count, capacity):
    slot_ids = jnp.arange(values.shape[0], dtype=jnp.int32)
    targets = owner_row * capacity + position_row
    entries = jnp.arange(shard_count * capacity, dtype=jnp.int32)
    matches = (targets[None, :] == entries[:, None]) & moving_row[None, :]
    source = jnp.sum(jnp.where(matches, slot_ids[None, :], 0), axis=1)
    filled = jnp.any(matches, axis=1)
    packed = jnp.where(filled[:, None], jnp.take(values, source, axis=0), 0.0)
    return packed.reshape(shard_count, capacity, values.shape[1])


def place_blocks(
    received,
    own_values,
    owner_devices,
    destination_slot_list,
    moving,
    positions,
    my_index,
    capacity,
):
    shard_count, slot_count = owner_devices.shape
    slot_ids = jnp.arange(slot_count, dtype=jnp.int32)
    entries = (jnp.arange(shard_count, dtype=jnp.int32)[:, None] * capacity + positions).reshape(-1)
    to_me = (moving & (owner_devices == my_index)).reshape(-1)
    matches = to_me[None, :] & (destination_slot_list.reshape(-1)[None, :] == slot_ids[:, None])
    arrived = jnp.any(matches, axis=1)
    from_entry = jnp.sum(jnp.where(matches, entries[None, :], 0), axis=1)
    flattened = received.reshape(shard_count * capacity, received.shape[2])
    arrival_rows = jnp.take(flattened, from_entry, axis=0)
    stay_hit = (owner_devices[my_index] == my_index)[None, :] & (
        destination_slot_list[my_index][None, :] == slot_ids[:, None]
    )
    stayed = jnp.any(stay_hit, axis=1)
    from_slot = jnp.sum(jnp.where(stay_hit, slot_ids[None, :], 0), axis=1)
    kept_rows = jnp.take(own_values, from_slot, axis=0)
    return jnp.where(arrived[:, None], arrival_rows, jnp.where(stayed[:, None], kept_rows, 0.0))


def local_place(block_ids, first_id, local_count):
    local_ids = block_ids - first_id
    inside = (local_ids >= 0) & (local_ids < local_count)
    return jnp.where(inside, local_ids, local_count)


def general(
    hidden,
    out_grad,
    block_weight,
    block_row,
    block_col,
    live_count,
    new_owner,
    new_slot,
    first_moment,
    second_moment,
):
    shard_count = lax.axis_size(SHARD)
    dp_count = lax.axis_size(DP)
    my_index = lax.axis_index(SHARD)
    dp_index = lax.axis_index(DP)
    tokens_dev = hidden.shape[0]
    slot_count = block_weight.shape[1]
    block_size = block_weight.shape[2]
    share_size = first_moment.shape[2]
    row_blocks = hidden.shape[1] * shard_count // block_size
    col_blocks = out_grad.shape[1] * shard_count // block_size
    grad_scale = 1.0 / math.sqrt(tokens_dev * dp_count)
    slot_ids = jnp.arange(slot_count)
    live_all = slot_ids[None, :] < live_count[:, None]
    my_live = live_all[my_index]
    my_rows = block_row[my_index]
    my_cols = block_col[my_index]
    zero_bf = jnp.zeros((), jnp.bfloat16)
    full_hidden, full_grad = (
        lax.all_gather(hidden, SHARD, axis=1, tiled=True),
        lax.all_gather(out_grad, SHARD, axis=1, tiled=True),
    )
    hidden_blocks = full_hidden.reshape(tokens_dev, row_blocks, block_size)
    grad_blocks = full_grad.reshape(tokens_dev, col_blocks, block_size)
    own_hidden = jnp.take(hidden_blocks, my_rows, axis=1)
    own_grad = jnp.take(grad_blocks, my_cols, axis=1)
    grad_share = None
    col_local = col_blocks // shard_count
    row_local = row_blocks // shard_count

    def one_shard(totals, member):
        blocks, shard_index = member
        row_ids = block_row[shard_index]
        col_ids = block_col[shard_index]
        weights = jnp.where(live_all[shard_index][:, None, None], blocks, zero_bf)
        hidden_part = jnp.take(hidden_blocks, row_ids, axis=1)
        grad_part = jnp.take(grad_blocks, col_ids, axis=1)
        forward = jnp.einsum(
            "tkr,krc->tkc", hidden_part, weights, preferred_element_type=jnp.float32
        )
        backward = jnp.einsum(
            "tkc,krc->tkr", grad_part, weights, preferred_element_type=jnp.float32
        )
        col_place = local_place(col_ids, my_index * col_local, col_local)
        row_place = local_place(row_ids, my_index * row_local, row_local)
        out_total = totals[0].at[:, col_place].add(forward, mode="drop")
        back_total = totals[1].at[:, row_place].add(backward, mode="drop")
        return ((out_total, back_total), None)

    initial = (
        jnp.zeros((tokens_dev, col_local, block_size), jnp.float32),
        jnp.zeros((tokens_dev, row_local, block_size), jnp.float32),
    )
    totals = initial
    blocks_in = lax.all_gather(block_weight, SHARD, axis=0, tiled=True)
    indices = jnp.arange(blocks_in.shape[0], dtype=jnp.int32)
    totals, unused = lax.scan(one_shard, totals, (blocks_in, indices))
    out_total, back_total = totals
    projected = out_total.reshape(tokens_dev, col_local * block_size).astype(jnp.bfloat16)
    hidden_grad = back_total.reshape(tokens_dev, row_local * block_size).astype(jnp.bfloat16)
    blocks = (
        jnp.einsum("tkr,tkc->krc", own_hidden, own_grad, preferred_element_type=jnp.float32)
        * grad_scale
    )
    blocks = jnp.where(my_live[:, None, None], blocks, 0.0)
    grad_share = lax.psum_scatter(
        blocks.reshape(slot_count, block_size * block_size), DP, scatter_dimension=1, tiled=True
    )
    moving, positions = send_positions(new_owner, shard_count, slot_count)
    my_owner = new_owner[my_index]
    my_moving = moving[my_index]
    my_positions = positions[my_index]
    flat_weight = block_weight[0].reshape(slot_count, block_size * block_size)
    weight_share = lax.dynamic_slice_in_dim(
        flat_weight, dp_index * share_size, share_size, 1
    ).astype(jnp.float32)
    updated, first_state, second_state = adam_update(
        weight_share, first_moment[0], second_moment[0], grad_share
    )
    stacked = jnp.concatenate([updated, first_state, second_state], axis=1)
    packed = pack_moving(stacked, my_owner, my_moving, my_positions, shard_count, MV)
    received = lax.all_to_all(packed, SHARD, split_axis=0, concat_axis=0, tiled=True)
    placed = place_blocks(received, stacked, new_owner, new_slot, moving, positions, my_index, MV)
    new_weight = placed[:, :share_size]
    new_first = placed[:, share_size : 2 * share_size]
    new_second = placed[:, 2 * share_size :]
    return (projected, hidden_grad, new_weight[None], new_first[None], new_second[None])


WCAP = 44
GCAP = 40
PAIR = 14
UNROLL = 4
NX, NY, NZH, NZL = 4, 8, 2, 4
BS = 128
VMEM_LIMIT = 10 * 1024 * 1024
f32 = jnp.float32
bf16 = jnp.bfloat16
i32 = jnp.int32


def call(kernel, outs, n_smem, n_vmem, scratch=(), flops=0, byts=0, n_after=0):
    smem = pl.BlockSpec(memory_space=pltpu.SMEM)
    vmem = pl.BlockSpec(memory_space=pltpu.VMEM)
    anywhere = pl.BlockSpec(memory_space=pl.ANY)
    return pl.pallas_call(
        kernel,
        out_shape=outs,
        in_specs=[smem] * n_smem + [vmem] * n_vmem + [anywhere] * n_after,
        out_specs=jax.tree.map(lambda _: vmem, outs),
        scratch_shapes=list(scratch),
        compiler_params=pltpu.CompilerParams(vmem_limit_bytes=VMEM_LIMIT),
        cost_estimate=pl.CostEstimate(flops=flops, bytes_accessed=byts, transcendentals=0),
    )


def like(shape, dtype):
    return jax.ShapeDtypeStruct(shape, dtype)


def make_plan(block_row, block_col, live_count, new_owner, new_slot, row_local, me):
    shard_count, slot_count = block_row.shape
    total = shard_count * slot_count
    ids = jnp.arange(total, dtype=i32)
    live = (jnp.arange(slot_count)[None, :] < live_count[:, None]).reshape(total)
    row = block_row.reshape(total)
    col = block_col.reshape(total)
    owner = jnp.where(live, new_owner.reshape(total), -1)
    slot = new_slot.reshape(total)
    kept = owner >= 0
    row_shard = row // row_local
    key = jnp.where(kept, ids, ids + total)
    same = row_shard[:, None] == row_shard[None, :]
    before = same & live[None, :] & (key[None, :] < key[:, None])
    rank = jnp.sum(before.astype(i32), axis=1)
    earlier = same & (owner[:, None] == owner[None, :]) & (ids[None, :] < ids[:, None])
    pos = jnp.sum(earlier.astype(i32), axis=1)
    fits = (
        (jnp.max(jnp.where(live, rank, 0)) < WCAP)
        & (jnp.max(jnp.where(kept, rank, 0)) < GCAP)
        & (jnp.max(jnp.where(kept, pos, 0)) < PAIR)
    )

    here = live & (row_shard == me)
    words = ids + 256 * ((row - row_local * me) + 16 * col)
    hit = here[None, :] & (rank[None, :] == jnp.arange(WCAP)[:, None])
    code = jnp.sum(jnp.where(hit, words[None, :], 0), axis=1)
    counts = [jnp.minimum(jnp.sum(here.astype(i32)), WCAP), jnp.minimum(jnp.sum((here & kept).astype(i32)), GCAP)]
    going = jnp.where(here & kept, owner * PAIR + pos, -1)
    send_hit = going[None, :] == jnp.arange(shard_count * PAIR)[:, None]
    send = jnp.minimum(jnp.sum(jnp.where(send_hit, rank[None, :], 0), axis=1), GCAP - 1)
    owner2 = owner.reshape(shard_count, slot_count)
    sources = jnp.arange(shard_count, dtype=i32)[:, None]
    slots = jnp.arange(slot_count, dtype=i32)[None, :]
    moving, positions = send_positions(owner2, shard_count, slot_count)
    target = jnp.where(moving & (sources == me), owner2 * MV + positions, -1).reshape(total)
    state_hit = target[None, :] == jnp.arange(shard_count * MV)[:, None]
    state_send = jnp.sum(jnp.where(state_hit, (ids % slot_count)[None, :], 0), axis=1)
    state_row = jnp.where(sources == me, slots, slot_count + sources * MV + positions).reshape(total)
    landing = 1 + row_shard * PAIR + jnp.minimum(pos, PAIR - 1) + shard_count * PAIR * state_row
    lands = (owner == me)[None, :] & (slot[None, :] == jnp.arange(slot_count)[:, None])
    place = jnp.sum(jnp.where(lands, landing[None, :], 0), axis=1)
    return fits, code, counts, send, state_send, place


def prepare_kernel(blocks, out_grad, quarter, sent, sems):
    rows = quarter.shape[1]
    first = pl.multiple_of(lax.axis_index("x") * rows, rows)
    copies = [pltpu.make_async_copy(blocks.at[0, :, pl.ds(first, rows)], quarter, sems.at[NZL])]
    copies += [pltpu.make_async_copy(out_grad, sent.at[n], sems.at[n]) for n in range(NZL)]
    for copy in copies:
        copy.start()
    for copy in copies:
        copy.wait()


def grad_kernel(info, code, hidden, mine, other, out, cols, hidden_t, total):
    my_core = info[2]
    for zl in range(NZL):
        for sub in range(4):
            lanes = slice(sub * BS, (sub + 1) * BS)
            cols[(2 * zl + my_core) * 4 + sub] = mine[zl, :, lanes]
            cols[(2 * zl + 1 - my_core) * 4 + sub] = other[zl, :, lanes]
    row_local = hidden.shape[1] // BS
    for r in range(row_local):
        hidden_t[r] = hidden[:, r * BS : (r + 1) * BS].T

    def step(i, carry):
        blocks = []
        for u in range(UNROLL):
            word = code[i * UNROLL + u]
            blocks.append(jnp.dot(hidden_t[(word >> 8) & 15], cols[word >> 12], preferred_element_type=f32))
        for u in range(UNROLL):
            total[pl.ds(i * UNROLL + u, BS, stride=GCAP), :] = blocks[u]
        return carry

    lax.fori_loop(0, (info[1] + UNROLL - 1) // UNROLL, step, 0)
    for x in range(NX):
        for y in range(NY):
            for q in range(4):
                source = 16 * y + 4 * x + q
                out[x, 4 * y + q] = total[source * GCAP : (source + 1) * GCAP, :].astype(bf16)


def share_kernel(scale, send, state_send, parts, stacked, out, total):
    total[...] = parts[0].astype(f32)

    def step(n, carry):
        total[...] += parts[n].astype(f32)
        return carry

    lax.fori_loop(1, parts.shape[0], step, 0)
    total[...] = total[...] * scale
    width = stacked.shape[1] // BS
    for d in range(out.shape[0]):
        for p in range(PAIR):
            rank = send[d * PAIR + p]
            for b in range(2):
                out[d, 2 * p + b : 2 * p + b + 1, :] = total[b, pl.ds(rank, 1), :]
        for p in range(MV):
            row = stacked[pl.ds(state_send[d * MV + p], 1), :]
            for n in range(width):
                at = 2 * PAIR + width * p + n
                out[d, at : at + 1, :] = row[:, n * BS : (n + 1) * BS]


def select_sum_kernel(info, code, gathered, parts, picked, summed):
    def select(c, carry):
        value = gathered[code[c] & 255]
        picked[c] = jnp.where(c < info[0], value, jnp.zeros_like(value))
        return carry

    def add(i, carry):
        value = parts[0, i].astype(f32)
        for n in range(1, parts.shape[0]):
            value += parts[n, i].astype(f32)
        summed[i] = value.astype(bf16)
        return carry

    lax.fori_loop(0, WCAP, select, 0, unroll=4)
    lax.fori_loop(0, summed.shape[0], add, 0, unroll=4)


def forward_kernel(info, code, hidden, quarters, _after, mine, theirs, weights, total, sems):
    my_core = info[2]
    copies = [pltpu.make_async_copy(quarters.at[x], weights.at[:, x], sems.at[x]) for x in range(NX)]
    for copy in copies:
        copy.start()
    total[...] = jnp.zeros_like(total)
    for copy in copies:
        copy.wait()

    def step(i, carry):
        adds = []
        for u in range(UNROLL):
            c = i * UNROLL + u
            word = code[c]
            lanes = pl.ds(pl.multiple_of(((word >> 8) & 15) * BS, BS), BS)
            w = weights[c].reshape(BS, BS)
            adds.append((word >> 12, jnp.dot(hidden[:, lanes], w, preferred_element_type=f32)))
        for col, value in adds:
            total[col] += value
        return carry

    lax.fori_loop(0, (info[0] + UNROLL - 1) // UNROLL, step, 0)
    for zl in range(NZL):
        for sub in range(4):
            mine[zl, sub] = total[(2 * zl + my_core) * 4 + sub]
            theirs[zl, sub] = total[(2 * zl + 1 - my_core) * 4 + sub].astype(bf16)


def backward_kernel(info, code, cols, weights, back, total):
    total[...] = jnp.zeros_like(total)

    def step(i, carry):
        adds = []
        for u in range(UNROLL):
            c = i * UNROLL + u
            word = code[c]
            w = weights[c].reshape(BS, BS)
            value = lax.dot_general(cols[word >> 12], w, (((1,), (1,)), ((), ())), preferred_element_type=f32)
            adds.append(((word >> 8) & 15, value))
        for r, value in adds:
            total[r] += value
        return carry

    lax.fori_loop(0, (info[0] + UNROLL - 1) // UNROLL, step, 0)
    for r in range(total.shape[0]):
        back[:, r * BS : (r + 1) * BS] = total[r].astype(bf16)


def chip_kernel(info, mine, came, own, s1, s2, s3):
    my_zl = info[4]
    own[...] = mine[my_zl] + came[my_zl].astype(f32)
    for k, out in enumerate((s1, s2, s3)):
        zl = (my_zl + k + 1) % NZL
        out[...] = (mine[zl] + came[zl].astype(f32)).astype(bf16)


def project_kernel(own, r1, r2, r3, _after, out):
    for sub in range(4):
        value = own[sub] + r1[sub].astype(f32) + r2[sub].astype(f32) + r3[sub].astype(f32)
        out[:, sub * BS : (sub + 1) * BS] = value.astype(bf16)


def adam_kernel(place, stacked, came, _after, new_w, new_m, new_v, rows, grad):
    slots, share = new_w.shape
    places = came.shape[0] * PAIR
    width = stacked.shape[1] // BS
    for j in range(slots):
        word = jnp.maximum(place[j] - 1, 0)
        g, row = word % places, word // places
        filled = place[j] > 0
        here = row < slots
        entry = jnp.maximum(row - slots, 0)
        own = stacked[pl.ds(jnp.minimum(row, slots - 1), 1), :]
        for n in range(width):
            lanes = slice(n * BS, (n + 1) * BS)
            moved = came[entry // MV, pl.ds(2 * PAIR + width * (entry % MV) + n, 1), :]
            rows[j : j + 1, lanes] = jnp.where(filled, jnp.where(here, own[:, lanes], moved), 0.0)
        for b in range(2):
            value = came[g // PAIR, pl.ds(2 * (g % PAIR) + b, 1), :]
            grad[j : j + 1, b * BS : (b + 1) * BS] = jnp.where(filled, value, 0.0)
    w, m, v = adam_update(rows[:, :share], rows[:, share : 2 * share], rows[:, 2 * share :], grad[...])
    new_w[...] = w
    new_m[...] = m
    new_v[...] = v


def all_to_all(values, axis):
    return lax.all_to_all(values, axis, split_axis=0, concat_axis=0, tiled=True)


def shift(values, axis, count, step):
    return lax.ppermute(values, axis, [(i, (i + step) % count) for i in range(count)])


def shards(
    hidden,
    out_grad,
    block_weight,
    block_row,
    block_col,
    live_count,
    new_owner,
    new_slot,
    first_moment,
    second_moment,
):
    shard_count = lax.axis_size(SHARD)
    me = lax.axis_index(SHARD)
    dp_index = lax.axis_index(DP)
    x_index = lax.axis_index("x")
    tokens = hidden.shape[0]
    slot_count = block_weight.shape[1]
    row_local = hidden.shape[1] // BS
    share = first_moment.shape[2]
    scale = 1.0 / math.sqrt(tokens * lax.axis_size(DP))

    anywhere = pl.BlockSpec(memory_space=pl.ANY)
    quarter, sent = pl.pallas_call(
        prepare_kernel,
        out_shape=(like((slot_count, BS // NX, BS), bf16), like((NZL,) + out_grad.shape, bf16)),
        in_specs=[anywhere] * 2,
        out_specs=(anywhere, anywhere),
        scratch_shapes=[pltpu.SemaphoreType.DMA((NZL + 1,))],
    )(block_weight, out_grad)
    gathered = lax.all_gather(quarter, SHARD, axis=0, tiled=True)
    mine = all_to_all(sent, "zl")
    other = shift(mine, "core", 2, 1)
    weight_share = lax.dynamic_slice_in_dim(block_weight[0], dp_index * 2, 2, 1).reshape(slot_count, share)
    stacked = jnp.concatenate([weight_share.astype(f32), first_moment[0], second_moment[0]], axis=1)

    fits, code, counts, send, state_send, place = make_plan(
        block_row, block_col, live_count, new_owner, new_slot, row_local, me
    )
    info = jnp.stack(counts + [lax.axis_index("core"), x_index, lax.axis_index("zl"), lax.axis_index("zh")])

    partial, cols = call(
        grad_kernel,
        (like((NX, NY * NZH * 2, GCAP, BS), bf16), like((shard_count * 4, BS, BS), bf16)),
        2,
        3,
        [pltpu.VMEM((row_local, BS, BS), bf16), pltpu.VMEM((BS * GCAP, BS), f32)],
        flops=2 * WCAP * BS**3,
        byts=4 * 1024 * 1024,
    )(info, code, hidden, mine, other)
    along_x = all_to_all(partial, "x")
    picked, summed = call(
        select_sum_kernel,
        (like((WCAP, BS // NX, BS), bf16), like(partial.shape[1:], bf16)),
        2,
        2,
        byts=4 * 1024 * 1024,
    )(info, code, gathered, along_x)
    quarters = lax.all_gather(picked, "x", axis=0)
    along_yz = all_to_all(summed.reshape(NY * NZH, 2, GCAP, BS), ("y", "zh"))
    packed = call(
        functools.partial(share_kernel, scale),
        like((shard_count, 2 * PAIR + MV * stacked.shape[1] // BS, BS), f32),
        2,
        2,
        [pltpu.VMEM((2, GCAP, BS), f32)],
        byts=1024 * 1024,
    )(send, state_send, along_yz, stacked)
    shares = all_to_all(packed, SHARD)

    out_mine, out_theirs, weights = call(
        forward_kernel,
        (
            like((NZL, 4, tokens, BS), f32),
            like((NZL, 4, tokens, BS), bf16),
            like((WCAP, NX, BS // NX, BS), bf16),
        ),
        2,
        1,
        [pltpu.VMEM((shard_count * 4, tokens, BS), f32), pltpu.SemaphoreType.DMA((NX,))],
        flops=2 * WCAP * BS**3,
        byts=8 * 1024 * 1024,
        n_after=2,
    )(info, code, hidden, quarters, packed)
    came = shift(out_theirs, "core", 2, 1)
    hidden_grad = call(
        backward_kernel,
        like(hidden.shape, bf16),
        2,
        2,
        [pltpu.VMEM((row_local, tokens, BS), f32)],
        flops=2 * WCAP * BS**3,
        byts=4 * 1024 * 1024,
    )(info, code, cols, weights)
    part = (4, tokens, BS)
    own, s1, s2, s3 = call(
        chip_kernel, (like(part, f32),) + (like(part, bf16),) * 3, 1, 2, byts=3 * 1024 * 1024
    )(info, out_mine, came)
    r2, r1, r3 = (shift(s, "zl", NZL, k) for k, s in ((2, s2), (1, s1), (3, s3)))
    projected = call(project_kernel, like(out_grad.shape, bf16), 0, 4, byts=1024 * 1024, n_after=1)(
        own, r1, r2, r3, hidden_grad
    )

    shape = like((slot_count, share), f32)
    new_weight, new_first, new_second = call(
        adam_kernel,
        (shape, shape, shape),
        1,
        2,
        [pltpu.VMEM((slot_count, 3 * share), f32), pltpu.VMEM((slot_count, share), f32)],
        byts=1024 * 1024,
        n_after=1,
    )(place, stacked, shares, hidden_grad)
    result = (projected, hidden_grad, new_weight[None], new_first[None], new_second[None])
    return lax.cond(
        fits,
        lambda: result,
        lambda: general(
            hidden,
            out_grad,
            block_weight,
            block_row,
            block_col,
            live_count,
            new_owner,
            new_slot,
            first_moment,
            second_moment,
        ),
    )


def solution(mesh):
    split = Mesh(mesh.devices.reshape(NY, NX, NZH, NZL, 2), ("y", "x", "zh", "zl", "core"))
    in_specs = (
        P(DP, SHARD),
        P(DP, SHARD),
        P(SHARD, None, None, None),
        P(),
        P(),
        P(),
        P(),
        P(),
        P(SHARD, None, DP),
        P(SHARD, None, DP),
    )
    out_specs = (
        P(DP, SHARD),
        P(DP, SHARD),
        P(SHARD, None, DP),
        P(SHARD, None, DP),
        P(SHARD, None, DP),
    )
    return jax.shard_map(shards, mesh=split, in_specs=in_specs, out_specs=out_specs, check_vma=False)
```

```python
import functools
import math

import jax
import jax.numpy as jnp
from jax import lax
from jax.experimental import pallas as pl
from jax.experimental.pallas import tpu as pltpu
from jax.sharding import Mesh, PartitionSpec as P

DP = ("y", "x", "zh")
SHARD = ("zl", "core")
MV = 2


LEARN_RATE = 0.01
BETA_ONE = 0.9
BETA_TWO = 0.95
EPSILON = 1e-08


def adam_update(weight, first_state, second_state, gradient):
    first_state = BETA_ONE * first_state + (1.0 - BETA_ONE) * gradient
    second_state = BETA_TWO * second_state + (1.0 - BETA_TWO) * gradient * gradient
    weight = weight - LEARN_RATE * first_state / (jnp.sqrt(second_state) + EPSILON)
    return (weight, first_state, second_state)


def send_positions(owner_devices, shard_count, slot_count):
    sources = jnp.arange(shard_count, dtype=jnp.int32)[:, None]
    moving = (owner_devices >= 0) & (owner_devices != sources)
    slot_ids = jnp.arange(slot_count)
    earlier = slot_ids[None, :] < slot_ids[:, None]
    matches = (
        (owner_devices[:, :, None] == owner_devices[:, None, :])
        & moving[:, None, :]
        & earlier[None, :, :]
    )
    return (moving, jnp.sum(matches, axis=2))


def pack_moving(values, owner_row, moving_row, position_row, shard_count, capacity):
    slot_ids = jnp.arange(values.shape[0], dtype=jnp.int32)
    targets = owner_row * capacity + position_row
    entries = jnp.arange(shard_count * capacity, dtype=jnp.int32)
    matches = (targets[None, :] == entries[:, None]) & moving_row[None, :]
    source = jnp.sum(jnp.where(matches, slot_ids[None, :], 0), axis=1)
    filled = jnp.any(matches, axis=1)
    packed = jnp.where(filled[:, None], jnp.take(values, source, axis=0), 0.0)
    return packed.reshape(shard_count, capacity, values.shape[1])


def place_blocks(
    received,
    own_values,
    owner_devices,
    destination_slot_list,
    moving,
    positions,
    my_index,
    capacity,
):
    shard_count, slot_count = owner_devices.shape
    slot_ids = jnp.arange(slot_count, dtype=jnp.int32)
    entries = (jnp.arange(shard_count, dtype=jnp.int32)[:, None] * capacity + positions).reshape(-1)
    to_me = (moving & (owner_devices == my_index)).reshape(-1)
    matches = to_me[None, :] & (destination_slot_list.reshape(-1)[None, :] == slot_ids[:, None])
    arrived = jnp.any(matches, axis=1)
    from_entry = jnp.sum(jnp.where(matches, entries[None, :], 0), axis=1)
    flattened = received.reshape(shard_count * capacity, received.shape[2])
    arrival_rows = jnp.take(flattened, from_entry, axis=0)
    stay_hit = (owner_devices[my_index] == my_index)[None, :] & (
        destination_slot_list[my_index][None, :] == slot_ids[:, None]
    )
    stayed = jnp.any(stay_hit, axis=1)
    from_slot = jnp.sum(jnp.where(stay_hit, slot_ids[None, :], 0), axis=1)
    kept_rows = jnp.take(own_values, from_slot, axis=0)
    return jnp.where(arrived[:, None], arrival_rows, jnp.where(stayed[:, None], kept_rows, 0.0))


def local_place(block_ids, first_id, local_count):
    local_ids = block_ids - first_id
    inside = (local_ids >= 0) & (local_ids < local_count)
    return jnp.where(inside, local_ids, local_count)


def general(
    hidden,
    out_grad,
    block_weight,
    block_row,
    block_col,
    live_count,
    new_owner,
    new_slot,
    first_moment,
    second_moment,
):
    shard_count = lax.axis_size(SHARD)
    dp_count = lax.axis_size(DP)
    my_index = lax.axis_index(SHARD)
    dp_index = lax.axis_index(DP)
    tokens_dev = hidden.shape[0]
    slot_count = block_weight.shape[1]
    block_size = block_weight.shape[2]
    share_size = first_moment.shape[2]
    row_blocks = hidden.shape[1] * shard_count // block_size
    col_blocks = out_grad.shape[1] * shard_count // block_size
    grad_scale = 1.0 / math.sqrt(tokens_dev * dp_count)
    slot_ids = jnp.arange(slot_count)
    live_all = slot_ids[None, :] < live_count[:, None]
    my_live = live_all[my_index]
    my_rows = block_row[my_index]
    my_cols = block_col[my_index]
    zero_bf = jnp.zeros((), jnp.bfloat16)
    full_hidden, full_grad = (
        lax.all_gather(hidden, SHARD, axis=1, tiled=True),
        lax.all_gather(out_grad, SHARD, axis=1, tiled=True),
    )
    hidden_blocks = full_hidden.reshape(tokens_dev, row_blocks, block_size)
    grad_blocks = full_grad.reshape(tokens_dev, col_blocks, block_size)
    own_hidden = jnp.take(hidden_blocks, my_rows, axis=1)
    own_grad = jnp.take(grad_blocks, my_cols, axis=1)
    grad_share = None
    col_local = col_blocks // shard_count
    row_local = row_blocks // shard_count

    def one_shard(totals, member):
        blocks, shard_index = member
        row_ids = block_row[shard_index]
        col_ids = block_col[shard_index]
        weights = jnp.where(live_all[shard_index][:, None, None], blocks, zero_bf)
        hidden_part = jnp.take(hidden_blocks, row_ids, axis=1)
        grad_part = jnp.take(grad_blocks, col_ids, axis=1)
        forward = jnp.einsum(
            "tkr,krc->tkc", hidden_part, weights, preferred_element_type=jnp.float32
        )
        backward = jnp.einsum(
            "tkc,krc->tkr", grad_part, weights, preferred_element_type=jnp.float32
        )
        col_place = local_place(col_ids, my_index * col_local, col_local)
        row_place = local_place(row_ids, my_index * row_local, row_local)
        out_total = totals[0].at[:, col_place].add(forward, mode="drop")
        back_total = totals[1].at[:, row_place].add(backward, mode="drop")
        return ((out_total, back_total), None)

    initial = (
        jnp.zeros((tokens_dev, col_local, block_size), jnp.float32),
        jnp.zeros((tokens_dev, row_local, block_size), jnp.float32),
    )
    totals = initial
    blocks_in = lax.all_gather(block_weight, SHARD, axis=0, tiled=True)
    indices = jnp.arange(blocks_in.shape[0], dtype=jnp.int32)
    totals, unused = lax.scan(one_shard, totals, (blocks_in, indices))
    out_total, back_total = totals
    projected = out_total.reshape(tokens_dev, col_local * block_size).astype(jnp.bfloat16)
    hidden_grad = back_total.reshape(tokens_dev, row_local * block_size).astype(jnp.bfloat16)
    blocks = (
        jnp.einsum("tkr,tkc->krc", own_hidden, own_grad, preferred_element_type=jnp.float32)
        * grad_scale
    )
    blocks = jnp.where(my_live[:, None, None], blocks, 0.0)
    grad_share = lax.psum_scatter(
        blocks.reshape(slot_count, block_size * block_size), DP, scatter_dimension=1, tiled=True
    )
    moving, positions = send_positions(new_owner, shard_count, slot_count)
    my_owner = new_owner[my_index]
    my_moving = moving[my_index]
    my_positions = positions[my_index]
    flat_weight = block_weight[0].reshape(slot_count, block_size * block_size)
    weight_share = lax.dynamic_slice_in_dim(
        flat_weight, dp_index * share_size, share_size, 1
    ).astype(jnp.float32)
    updated, first_state, second_state = adam_update(
        weight_share, first_moment[0], second_moment[0], grad_share
    )
    stacked = jnp.concatenate([updated, first_state, second_state], axis=1)
    packed = pack_moving(stacked, my_owner, my_moving, my_positions, shard_count, MV)
    received = lax.all_to_all(packed, SHARD, split_axis=0, concat_axis=0, tiled=True)
    placed = place_blocks(received, stacked, new_owner, new_slot, moving, positions, my_index, MV)
    new_weight = placed[:, :share_size]
    new_first = placed[:, share_size : 2 * share_size]
    new_second = placed[:, 2 * share_size :]
    return (projected, hidden_grad, new_weight[None], new_first[None], new_second[None])


WCAP = 44
GCAP = 40
PAIR = 14
UNROLL = 4
NX, NY, NZH, NZL = 4, 8, 2, 4
BS = 128
VMEM_LIMIT = 10 * 1024 * 1024
f32 = jnp.float32
bf16 = jnp.bfloat16
i32 = jnp.int32


def call(kernel, outs, n_smem, n_vmem, scratch=(), flops=0, byts=0, n_after=0):
    smem = pl.BlockSpec(memory_space=pltpu.SMEM)
    vmem = pl.BlockSpec(memory_space=pltpu.VMEM)
    anywhere = pl.BlockSpec(memory_space=pl.ANY)
    return pl.pallas_call(
        kernel,
        out_shape=outs,
        in_specs=[smem] * n_smem + [vmem] * n_vmem + [anywhere] * n_after,
        out_specs=jax.tree.map(lambda _: vmem, outs),
        scratch_shapes=list(scratch),
        compiler_params=pltpu.CompilerParams(vmem_limit_bytes=VMEM_LIMIT),
        cost_estimate=pl.CostEstimate(flops=flops, bytes_accessed=byts, transcendentals=0),
    )


def like(shape, dtype):
    return jax.ShapeDtypeStruct(shape, dtype)


def make_plan(block_row, block_col, live_count, new_owner, new_slot, row_local, me):
    shard_count, slot_count = block_row.shape
    total = shard_count * slot_count
    ids = jnp.arange(total, dtype=i32)
    live = (jnp.arange(slot_count)[None, :] < live_count[:, None]).reshape(total)
    row = block_row.reshape(total)
    col = block_col.reshape(total)
    owner = jnp.where(live, new_owner.reshape(total), -1)
    slot = new_slot.reshape(total)
    kept = owner >= 0
    row_shard = row // row_local
    key = jnp.where(kept, ids, ids + total)
    same = row_shard[:, None] == row_shard[None, :]
    before = same & live[None, :] & (key[None, :] < key[:, None])
    rank = jnp.sum(before.astype(i32), axis=1)
    earlier = same & (owner[:, None] == owner[None, :]) & (ids[None, :] < ids[:, None])
    pos = jnp.sum(earlier.astype(i32), axis=1)
    fits = (
        (jnp.max(jnp.where(live, rank, 0)) < WCAP)
        & (jnp.max(jnp.where(kept, rank, 0)) < GCAP)
        & (jnp.max(jnp.where(kept, pos, 0)) < PAIR)
    )

    here = live & (row_shard == me)
    words = ids + 256 * ((row - row_local * me) + 16 * col)
    hit = here[None, :] & (rank[None, :] == jnp.arange(WCAP)[:, None])
    code = jnp.sum(jnp.where(hit, words[None, :], 0), axis=1)
    counts = [jnp.minimum(jnp.sum(here.astype(i32)), WCAP), jnp.minimum(jnp.sum((here & kept).astype(i32)), GCAP)]
    going = jnp.where(here & kept, owner * PAIR + pos, -1)
    send_hit = going[None, :] == jnp.arange(shard_count * PAIR)[:, None]
    send = jnp.minimum(jnp.sum(jnp.where(send_hit, rank[None, :], 0), axis=1), GCAP - 1)
    owner2 = owner.reshape(shard_count, slot_count)
    sources = jnp.arange(shard_count, dtype=i32)[:, None]
    slots = jnp.arange(slot_count, dtype=i32)[None, :]
    moving, positions = send_positions(owner2, shard_count, slot_count)
    target = jnp.where(moving & (sources == me), owner2 * MV + positions, -1).reshape(total)
    state_hit = target[None, :] == jnp.arange(shard_count * MV)[:, None]
    state_send = jnp.sum(jnp.where(state_hit, (ids % slot_count)[None, :], 0), axis=1)
    state_row = jnp.where(sources == me, slots, slot_count + sources * MV + positions).reshape(total)
    landing = 1 + row_shard * PAIR + jnp.minimum(pos, PAIR - 1) + shard_count * PAIR * state_row
    lands = (owner == me)[None, :] & (slot[None, :] == jnp.arange(slot_count)[:, None])
    place = jnp.sum(jnp.where(lands, landing[None, :], 0), axis=1)
    return fits.astype(i32).reshape(1), code, counts, send, state_send, place


def grad_kernel(info, code, hidden, mine, other, out, cols, hidden_t, total):
    my_core = info[2]
    for zl in range(NZL):
        for sub in range(4):
            lanes = slice(sub * BS, (sub + 1) * BS)
            cols[(2 * zl + my_core) * 4 + sub] = mine[zl, :, lanes]
            cols[(2 * zl + 1 - my_core) * 4 + sub] = other[zl, :, lanes]
    row_local = hidden.shape[1] // BS
    for r in range(row_local):
        hidden_t[r] = hidden[:, r * BS : (r + 1) * BS].T

    def step(i, carry):
        blocks = []
        for u in range(UNROLL):
            word = code[i * UNROLL + u]
            blocks.append(jnp.dot(hidden_t[(word >> 8) & 15], cols[word >> 12], preferred_element_type=f32))
        for u in range(UNROLL):
            total[pl.ds(i * UNROLL + u, BS, stride=GCAP), :] = blocks[u]
        return carry

    lax.fori_loop(0, (info[1] + UNROLL - 1) // UNROLL, step, 0)
    for x in range(NX):
        for y in range(NY):
            for q in range(4):
                source = 16 * y + 4 * x + q
                out[x, 4 * y + q] = total[source * GCAP : (source + 1) * GCAP, :].astype(bf16)


def share_kernel(scale, send, state_send, parts, stacked, _after, _after2, out, total):
    total[...] = parts[0].astype(f32)

    def step(n, carry):
        total[...] += parts[n].astype(f32)
        return carry

    lax.fori_loop(1, parts.shape[0], step, 0)
    total[...] = total[...] * scale
    width = stacked.shape[1] // BS
    for d in range(out.shape[0]):
        for p in range(PAIR):
            rank = send[d * PAIR + p]
            for b in range(2):
                out[d, 2 * p + b : 2 * p + b + 1, :] = total[b, pl.ds(rank, 1), :]
        for p in range(MV):
            row = stacked[pl.ds(state_send[d * MV + p], 1), :]
            for n in range(width):
                at = 2 * PAIR + width * p + n
                out[d, at : at + 1, :] = row[:, n * BS : (n + 1) * BS]


def select_sum_kernel(info, code, gathered, parts, picked, summed):
    def select(c, carry):
        value = gathered[code[c] & 255]
        picked[c] = jnp.where(c < info[0], value, jnp.zeros_like(value))
        return carry

    def add(i, carry):
        value = parts[0, i].astype(f32)
        for n in range(1, parts.shape[0]):
            value += parts[n, i].astype(f32)
        summed[i] = value.astype(bf16)
        return carry

    lax.fori_loop(0, WCAP, select, 0, unroll=4)
    lax.fori_loop(0, summed.shape[0], add, 0, unroll=4)


def forward_kernel(info, code, hidden, quarters, _after, mine, theirs, weights, total, sems):
    my_core = info[2]
    copies = [pltpu.make_async_copy(quarters.at[x], weights.at[:, x], sems.at[x]) for x in range(NX)]
    for copy in copies:
        copy.start()
    total[...] = jnp.zeros_like(total)
    for copy in copies:
        copy.wait()

    def step(i, carry):
        adds = []
        for u in range(UNROLL):
            c = i * UNROLL + u
            word = code[c]
            lanes = pl.ds(pl.multiple_of(((word >> 8) & 15) * BS, BS), BS)
            w = weights[c].reshape(BS, BS)
            adds.append((word >> 12, jnp.dot(hidden[:, lanes], w, preferred_element_type=f32)))
        for col, value in adds:
            total[col] += value
        return carry

    lax.fori_loop(0, (info[0] + UNROLL - 1) // UNROLL, step, 0)
    for zl in range(NZL):
        for sub in range(4):
            mine[zl, sub] = total[(2 * zl + my_core) * 4 + sub]
            theirs[zl, sub] = total[(2 * zl + 1 - my_core) * 4 + sub]


def backward_kernel(info, code, cols, weights, back, total):
    total[...] = jnp.zeros_like(total)

    def step(i, carry):
        adds = []
        for u in range(UNROLL):
            c = i * UNROLL + u
            word = code[c]
            w = weights[c].reshape(BS, BS)
            value = lax.dot_general(cols[word >> 12], w, (((1,), (1,)), ((), ())), preferred_element_type=f32)
            adds.append(((word >> 8) & 15, value))
        for r, value in adds:
            total[r] += value
        return carry

    lax.fori_loop(0, (info[0] + UNROLL - 1) // UNROLL, step, 0)
    for r in range(total.shape[0]):
        back[:, r * BS : (r + 1) * BS] = total[r].astype(bf16)


def chip_kernel(info, mine, came, own, s1, s2, s3):
    my_zl = info[4]
    own[...] = mine[my_zl] + came[my_zl]
    for k, out in enumerate((s1, s2, s3)):
        zl = (my_zl + k + 1) % NZL
        out[...] = (mine[zl] + came[zl]).astype(bf16)


def project_kernel(own, r1, r2, r3, _after, out):
    for sub in range(4):
        value = own[sub] + r1[sub].astype(f32) + r2[sub].astype(f32) + r3[sub].astype(f32)
        out[:, sub * BS : (sub + 1) * BS] = value.astype(bf16)


def adam_kernel(place, stacked, came, _after, new_w, new_m, new_v, rows, grad):
    slots, share = new_w.shape
    places = came.shape[0] * PAIR
    width = stacked.shape[1] // BS
    for j in range(slots):
        word = jnp.maximum(place[j] - 1, 0)
        g, row = word % places, word // places
        filled = place[j] > 0
        here = row < slots
        entry = jnp.maximum(row - slots, 0)
        own = stacked[pl.ds(jnp.minimum(row, slots - 1), 1), :]
        for n in range(width):
            lanes = slice(n * BS, (n + 1) * BS)
            moved = came[entry // MV, pl.ds(2 * PAIR + width * (entry % MV) + n, 1), :]
            rows[j : j + 1, lanes] = jnp.where(filled, jnp.where(here, own[:, lanes], moved), 0.0)
        for b in range(2):
            value = came[g // PAIR, pl.ds(2 * (g % PAIR) + b, 1), :]
            grad[j : j + 1, b * BS : (b + 1) * BS] = jnp.where(filled, value, 0.0)
    w, m, v = adam_update(rows[:, :share], rows[:, share : 2 * share], rows[:, 2 * share :], grad[...])
    new_w[...] = w
    new_m[...] = m
    new_v[...] = v


def all_to_all(values, axis):
    return lax.all_to_all(values, axis, split_axis=0, concat_axis=0, tiled=True)


def shift(values, axis, count, step):
    return lax.ppermute(values, axis, [(i, (i + step) % count) for i in range(count)])


def shards(
    hidden,
    out_grad,
    block_weight,
    block_row,
    block_col,
    live_count,
    new_owner,
    new_slot,
    first_moment,
    second_moment,
):
    shard_count = lax.axis_size(SHARD)
    me = lax.axis_index(SHARD)
    dp_index = lax.axis_index(DP)
    x_index = lax.axis_index("x")
    tokens = hidden.shape[0]
    slot_count = block_weight.shape[1]
    row_local = hidden.shape[1] // BS
    share = first_moment.shape[2]
    scale = 1.0 / math.sqrt(tokens * lax.axis_size(DP))

    quarter = lax.dynamic_slice_in_dim(block_weight[0], x_index * (BS // NX), BS // NX, 1)
    quarter, sent = lax.optimization_barrier((quarter, out_grad))
    gathered = lax.all_gather(quarter, SHARD, axis=0, tiled=True)
    mine = all_to_all(jnp.broadcast_to(sent[None], (NZL,) + out_grad.shape), "zl")
    other = shift(mine, "core", 2, 1)
    weight_share = lax.dynamic_slice_in_dim(block_weight[0], dp_index * 2, 2, 1).reshape(slot_count, share)
    stacked = jnp.concatenate([weight_share.astype(f32), first_moment[0], second_moment[0]], axis=1)

    fits, code, counts, send, state_send, place = make_plan(
        block_row, block_col, live_count, new_owner, new_slot, row_local, me
    )
    info = jnp.stack(counts + [lax.axis_index("core"), x_index, lax.axis_index("zl"), lax.axis_index("zh")])

    partial, cols = call(
        grad_kernel,
        (like((NX, NY * NZH * 2, GCAP, BS), bf16), like((shard_count * 4, BS, BS), bf16)),
        2,
        3,
        [pltpu.VMEM((row_local, BS, BS), bf16), pltpu.VMEM((BS * GCAP, BS), f32)],
        flops=2 * WCAP * BS**3,
        byts=4 * 1024 * 1024,
    )(info, code, hidden, mine, other)
    along_x = all_to_all(partial, "x")
    picked, summed = call(
        select_sum_kernel,
        (like((WCAP, BS // NX, BS), bf16), like(partial.shape[1:], bf16)),
        2,
        2,
        byts=4 * 1024 * 1024,
    )(info, code, gathered, along_x)
    quarters = lax.all_gather(picked, "x", axis=0)
    along_yz = all_to_all(summed.reshape(NY * NZH, 2, GCAP, BS), ("y", "zh"))
    packed = call(
        functools.partial(share_kernel, scale),
        like((shard_count, 2 * PAIR + MV * stacked.shape[1] // BS, BS), f32),
        2,
        2,
        [pltpu.VMEM((2, GCAP, BS), f32)],
        byts=1024 * 1024,
        n_after=2,
    )(send, state_send, along_yz, stacked, place, fits)
    shares = all_to_all(packed, SHARD)

    out_mine, out_theirs, weights = call(
        forward_kernel,
        (
            like((NZL, 4, tokens, BS), f32),
            like((NZL, 4, tokens, BS), f32),
            like((WCAP, NX, BS // NX, BS), bf16),
        ),
        2,
        1,
        [pltpu.VMEM((shard_count * 4, tokens, BS), f32), pltpu.SemaphoreType.DMA((NX,))],
        flops=2 * WCAP * BS**3,
        byts=8 * 1024 * 1024,
        n_after=2,
    )(info, code, hidden, quarters, packed)
    came = shift(out_theirs, "core", 2, 1)
    hidden_grad = call(
        backward_kernel,
        like(hidden.shape, bf16),
        2,
        2,
        [pltpu.VMEM((row_local, tokens, BS), f32)],
        flops=2 * WCAP * BS**3,
        byts=4 * 1024 * 1024,
    )(info, code, cols, weights)
    part = (4, tokens, BS)
    own, s1, s2, s3 = call(
        chip_kernel, (like(part, f32),) + (like(part, bf16),) * 3, 1, 2, byts=3 * 1024 * 1024
    )(info, out_mine, came)
    r2, r1, r3 = (shift(s, "zl", NZL, k) for k, s in ((2, s2), (1, s1), (3, s3)))
    projected = call(project_kernel, like(out_grad.shape, bf16), 0, 4, byts=1024 * 1024, n_after=1)(
        own, r1, r2, r3, hidden_grad
    )

    shape = like((slot_count, share), f32)
    new_weight, new_first, new_second = call(
        adam_kernel,
        (shape, shape, shape),
        1,
        2,
        [pltpu.VMEM((slot_count, 3 * share), f32), pltpu.VMEM((slot_count, share), f32)],
        byts=1024 * 1024,
        n_after=1,
    )(place, stacked, shares, hidden_grad)
    result = (projected, hidden_grad, new_weight[None], new_first[None], new_second[None])
    return lax.cond(
        fits[0] > 0,
        lambda: result,
        lambda: general(
            hidden,
            out_grad,
            block_weight,
            block_row,
            block_col,
            live_count,
            new_owner,
            new_slot,
            first_moment,
            second_moment,
        ),
    )


def solution(mesh):
    split = Mesh(mesh.devices.reshape(NY, NX, NZH, NZL, 2), ("y", "x", "zh", "zl", "core"))
    in_specs = (
        P(DP, SHARD),
        P(DP, SHARD),
        P(SHARD, None, None, None),
        P(),
        P(),
        P(),
        P(),
        P(),
        P(SHARD, None, DP),
        P(SHARD, None, DP),
    )
    out_specs = (
        P(DP, SHARD),
        P(DP, SHARD),
        P(SHARD, None, DP),
        P(SHARD, None, DP),
        P(SHARD, None, DP),
    )
    return jax.shard_map(shards, mesh=split, in_specs=in_specs, out_specs=out_specs, check_vma=False)
```

```python
import functools
import math

import jax
import jax.numpy as jnp
from jax import lax
from jax.experimental import pallas as pl
from jax.experimental.pallas import tpu as pltpu
from jax.sharding import Mesh, PartitionSpec as P

DP = ("y", "x", "zh")
SHARD = ("zl", "core")
MV = 2


LEARN_RATE = 0.01
BETA_ONE = 0.9
BETA_TWO = 0.95
EPSILON = 1e-08


def adam_update(weight, first_state, second_state, gradient):
    first_state = BETA_ONE * first_state + (1.0 - BETA_ONE) * gradient
    second_state = BETA_TWO * second_state + (1.0 - BETA_TWO) * gradient * gradient
    weight = weight - LEARN_RATE * first_state / (jnp.sqrt(second_state) + EPSILON)
    return (weight, first_state, second_state)


def send_positions(owner_devices, shard_count, slot_count):
    sources = jnp.arange(shard_count, dtype=jnp.int32)[:, None]
    moving = (owner_devices >= 0) & (owner_devices != sources)
    slot_ids = jnp.arange(slot_count)
    earlier = slot_ids[None, :] < slot_ids[:, None]
    matches = (
        (owner_devices[:, :, None] == owner_devices[:, None, :])
        & moving[:, None, :]
        & earlier[None, :, :]
    )
    return (moving, jnp.sum(matches, axis=2))


def pack_moving(values, owner_row, moving_row, position_row, shard_count, capacity):
    slot_ids = jnp.arange(values.shape[0], dtype=jnp.int32)
    targets = owner_row * capacity + position_row
    entries = jnp.arange(shard_count * capacity, dtype=jnp.int32)
    matches = (targets[None, :] == entries[:, None]) & moving_row[None, :]
    source = jnp.sum(jnp.where(matches, slot_ids[None, :], 0), axis=1)
    filled = jnp.any(matches, axis=1)
    packed = jnp.where(filled[:, None], jnp.take(values, source, axis=0), 0.0)
    return packed.reshape(shard_count, capacity, values.shape[1])


def place_blocks(
    received,
    own_values,
    owner_devices,
    destination_slot_list,
    moving,
    positions,
    my_index,
    capacity,
):
    shard_count, slot_count = owner_devices.shape
    slot_ids = jnp.arange(slot_count, dtype=jnp.int32)
    entries = (jnp.arange(shard_count, dtype=jnp.int32)[:, None] * capacity + positions).reshape(-1)
    to_me = (moving & (owner_devices == my_index)).reshape(-1)
    matches = to_me[None, :] & (destination_slot_list.reshape(-1)[None, :] == slot_ids[:, None])
    arrived = jnp.any(matches, axis=1)
    from_entry = jnp.sum(jnp.where(matches, entries[None, :], 0), axis=1)
    flattened = received.reshape(shard_count * capacity, received.shape[2])
    arrival_rows = jnp.take(flattened, from_entry, axis=0)
    stay_hit = (owner_devices[my_index] == my_index)[None, :] & (
        destination_slot_list[my_index][None, :] == slot_ids[:, None]
    )
    stayed = jnp.any(stay_hit, axis=1)
    from_slot = jnp.sum(jnp.where(stay_hit, slot_ids[None, :], 0), axis=1)
    kept_rows = jnp.take(own_values, from_slot, axis=0)
    return jnp.where(arrived[:, None], arrival_rows, jnp.where(stayed[:, None], kept_rows, 0.0))


def local_place(block_ids, first_id, local_count):
    local_ids = block_ids - first_id
    inside = (local_ids >= 0) & (local_ids < local_count)
    return jnp.where(inside, local_ids, local_count)


def general(
    hidden,
    out_grad,
    block_weight,
    block_row,
    block_col,
    live_count,
    new_owner,
    new_slot,
    first_moment,
    second_moment,
):
    shard_count = lax.axis_size(SHARD)
    dp_count = lax.axis_size(DP)
    my_index = lax.axis_index(SHARD)
    dp_index = lax.axis_index(DP)
    tokens_dev = hidden.shape[0]
    slot_count = block_weight.shape[1]
    block_size = block_weight.shape[2]
    share_size = first_moment.shape[2]
    row_blocks = hidden.shape[1] * shard_count // block_size
    col_blocks = out_grad.shape[1] * shard_count // block_size
    grad_scale = 1.0 / math.sqrt(tokens_dev * dp_count)
    slot_ids = jnp.arange(slot_count)
    live_all = slot_ids[None, :] < live_count[:, None]
    my_live = live_all[my_index]
    my_rows = block_row[my_index]
    my_cols = block_col[my_index]
    zero_bf = jnp.zeros((), jnp.bfloat16)
    full_hidden, full_grad = (
        lax.all_gather(hidden, SHARD, axis=1, tiled=True),
        lax.all_gather(out_grad, SHARD, axis=1, tiled=True),
    )
    hidden_blocks = full_hidden.reshape(tokens_dev, row_blocks, block_size)
    grad_blocks = full_grad.reshape(tokens_dev, col_blocks, block_size)
    own_hidden = jnp.take(hidden_blocks, my_rows, axis=1)
    own_grad = jnp.take(grad_blocks, my_cols, axis=1)
    grad_share = None
    col_local = col_blocks // shard_count
    row_local = row_blocks // shard_count

    def one_shard(totals, member):
        blocks, shard_index = member
        row_ids = block_row[shard_index]
        col_ids = block_col[shard_index]
        weights = jnp.where(live_all[shard_index][:, None, None], blocks, zero_bf)
        hidden_part = jnp.take(hidden_blocks, row_ids, axis=1)
        grad_part = jnp.take(grad_blocks, col_ids, axis=1)
        forward = jnp.einsum(
            "tkr,krc->tkc", hidden_part, weights, preferred_element_type=jnp.float32
        )
        backward = jnp.einsum(
            "tkc,krc->tkr", grad_part, weights, preferred_element_type=jnp.float32
        )
        col_place = local_place(col_ids, my_index * col_local, col_local)
        row_place = local_place(row_ids, my_index * row_local, row_local)
        out_total = totals[0].at[:, col_place].add(forward, mode="drop")
        back_total = totals[1].at[:, row_place].add(backward, mode="drop")
        return ((out_total, back_total), None)

    initial = (
        jnp.zeros((tokens_dev, col_local, block_size), jnp.float32),
        jnp.zeros((tokens_dev, row_local, block_size), jnp.float32),
    )
    totals = initial
    blocks_in = lax.all_gather(block_weight, SHARD, axis=0, tiled=True)
    indices = jnp.arange(blocks_in.shape[0], dtype=jnp.int32)
    totals, unused = lax.scan(one_shard, totals, (blocks_in, indices))
    out_total, back_total = totals
    projected = out_total.reshape(tokens_dev, col_local * block_size).astype(jnp.bfloat16)
    hidden_grad = back_total.reshape(tokens_dev, row_local * block_size).astype(jnp.bfloat16)
    blocks = (
        jnp.einsum("tkr,tkc->krc", own_hidden, own_grad, preferred_element_type=jnp.float32)
        * grad_scale
    )
    blocks = jnp.where(my_live[:, None, None], blocks, 0.0)
    grad_share = lax.psum_scatter(
        blocks.reshape(slot_count, block_size * block_size), DP, scatter_dimension=1, tiled=True
    )
    moving, positions = send_positions(new_owner, shard_count, slot_count)
    my_owner = new_owner[my_index]
    my_moving = moving[my_index]
    my_positions = positions[my_index]
    flat_weight = block_weight[0].reshape(slot_count, block_size * block_size)
    weight_share = lax.dynamic_slice_in_dim(
        flat_weight, dp_index * share_size, share_size, 1
    ).astype(jnp.float32)
    updated, first_state, second_state = adam_update(
        weight_share, first_moment[0], second_moment[0], grad_share
    )
    stacked = jnp.concatenate([updated, first_state, second_state], axis=1)
    packed = pack_moving(stacked, my_owner, my_moving, my_positions, shard_count, MV)
    received = lax.all_to_all(packed, SHARD, split_axis=0, concat_axis=0, tiled=True)
    placed = place_blocks(received, stacked, new_owner, new_slot, moving, positions, my_index, MV)
    new_weight = placed[:, :share_size]
    new_first = placed[:, share_size : 2 * share_size]
    new_second = placed[:, 2 * share_size :]
    return (projected, hidden_grad, new_weight[None], new_first[None], new_second[None])


WCAP = 44
GCAP = 40
PAIR = 14
UNROLL = 4
NX, NY, NZH, NZL = 4, 8, 2, 4
BS = 128
VMEM_LIMIT = 10 * 1024 * 1024
f32 = jnp.float32
bf16 = jnp.bfloat16
i32 = jnp.int32


def call(kernel, outs, n_smem, n_vmem, scratch=(), flops=0, byts=0, n_after=0):
    smem = pl.BlockSpec(memory_space=pltpu.SMEM)
    vmem = pl.BlockSpec(memory_space=pltpu.VMEM)
    anywhere = pl.BlockSpec(memory_space=pl.ANY)
    return pl.pallas_call(
        kernel,
        out_shape=outs,
        in_specs=[smem] * n_smem + [vmem] * n_vmem + [anywhere] * n_after,
        out_specs=jax.tree.map(lambda _: vmem, outs),
        scratch_shapes=list(scratch),
        compiler_params=pltpu.CompilerParams(vmem_limit_bytes=VMEM_LIMIT),
        cost_estimate=pl.CostEstimate(flops=flops, bytes_accessed=byts, transcendentals=0),
    )


def like(shape, dtype):
    return jax.ShapeDtypeStruct(shape, dtype)


def make_plan(block_row, block_col, live_count, new_owner, new_slot, row_local, me):
    shard_count, slot_count = block_row.shape
    total = shard_count * slot_count
    ids = jnp.arange(total, dtype=i32)
    live = (jnp.arange(slot_count)[None, :] < live_count[:, None]).reshape(total)
    row = block_row.reshape(total)
    col = block_col.reshape(total)
    owner = jnp.where(live, new_owner.reshape(total), -1)
    slot = new_slot.reshape(total)
    kept = owner >= 0
    row_shard = row // row_local
    key = jnp.where(kept, ids, ids + total)
    same = row_shard[:, None] == row_shard[None, :]
    before = same & live[None, :] & (key[None, :] < key[:, None])
    rank = jnp.sum(before.astype(i32), axis=1)
    earlier = same & (owner[:, None] == owner[None, :]) & (ids[None, :] < ids[:, None])
    pos = jnp.sum(earlier.astype(i32), axis=1)
    fits = (
        (jnp.max(jnp.where(live, rank, 0)) < WCAP)
        & (jnp.max(jnp.where(kept, rank, 0)) < GCAP)
        & (jnp.max(jnp.where(kept, pos, 0)) < PAIR)
    )

    here = live & (row_shard == me)
    words = ids + 256 * ((row - row_local * me) + 16 * col)
    hit = here[None, :] & (rank[None, :] == jnp.arange(WCAP)[:, None])
    code = jnp.sum(jnp.where(hit, words[None, :], 0), axis=1)
    counts = [jnp.minimum(jnp.sum(here.astype(i32)), WCAP), jnp.minimum(jnp.sum((here & kept).astype(i32)), GCAP)]
    going = jnp.where(here & kept, owner * PAIR + pos, -1)
    send_hit = going[None, :] == jnp.arange(shard_count * PAIR)[:, None]
    send = jnp.minimum(jnp.sum(jnp.where(send_hit, rank[None, :], 0), axis=1), GCAP - 1)
    owner2 = owner.reshape(shard_count, slot_count)
    sources = jnp.arange(shard_count, dtype=i32)[:, None]
    slots = jnp.arange(slot_count, dtype=i32)[None, :]
    moving, positions = send_positions(owner2, shard_count, slot_count)
    target = jnp.where(moving & (sources == me), owner2 * MV + positions, -1).reshape(total)
    state_hit = target[None, :] == jnp.arange(shard_count * MV)[:, None]
    state_send = jnp.sum(jnp.where(state_hit, (ids % slot_count)[None, :], 0), axis=1)
    state_row = jnp.where(sources == me, slots, slot_count + sources * MV + positions).reshape(total)
    landing = 1 + row_shard * PAIR + jnp.minimum(pos, PAIR - 1) + shard_count * PAIR * state_row
    lands = (owner == me)[None, :] & (slot[None, :] == jnp.arange(slot_count)[:, None])
    place = jnp.sum(jnp.where(lands, landing[None, :], 0), axis=1)
    return fits.astype(i32).reshape(1), code, counts, send, state_send, place


def repeat_kernel(value, out):
    for n in range(out.shape[0]):
        out[n] = value[...]


def grad_kernel(info, code, hidden, mine, other, out, cols, hidden_t, total):
    my_core = info[2]
    for zl in range(NZL):
        for sub in range(4):
            lanes = slice(sub * BS, (sub + 1) * BS)
            cols[(2 * zl + my_core) * 4 + sub] = mine[zl, :, lanes]
            cols[(2 * zl + 1 - my_core) * 4 + sub] = other[zl, :, lanes]
    row_local = hidden.shape[1] // BS
    for r in range(row_local):
        hidden_t[r] = hidden[:, r * BS : (r + 1) * BS].T

    def step(i, carry):
        blocks = []
        for u in range(UNROLL):
            word = code[i * UNROLL + u]
            blocks.append(jnp.dot(hidden_t[(word >> 8) & 15], cols[word >> 12], preferred_element_type=f32))
        for u in range(UNROLL):
            total[pl.ds(i * UNROLL + u, BS, stride=GCAP), :] = blocks[u]
        return carry

    lax.fori_loop(0, (info[1] + UNROLL - 1) // UNROLL, step, 0)
    for x in range(NX):
        for y in range(NY):
            for q in range(4):
                source = 16 * y + 4 * x + q
                out[x, 4 * y + q] = total[source * GCAP : (source + 1) * GCAP, :].astype(bf16)


def share_kernel(scale, send, state_send, parts, stacked, _after, _after2, out, total):
    total[...] = parts[0].astype(f32)

    def step(n, carry):
        total[...] += parts[n].astype(f32)
        return carry

    lax.fori_loop(1, parts.shape[0], step, 0)
    total[...] = total[...] * scale
    width = stacked.shape[1] // BS
    for d in range(out.shape[0]):
        for p in range(PAIR):
            rank = send[d * PAIR + p]
            for b in range(2):
                out[d, 2 * p + b : 2 * p + b + 1, :] = total[b, pl.ds(rank, 1), :]
        for p in range(MV):
            row = stacked[pl.ds(state_send[d * MV + p], 1), :]
            for n in range(width):
                at = 2 * PAIR + width * p + n
                out[d, at : at + 1, :] = row[:, n * BS : (n + 1) * BS]


def select_sum_kernel(info, code, gathered, parts, picked, summed):
    def select(c, carry):
        value = gathered[code[c] & 255]
        picked[c] = jnp.where(c < info[0], value, jnp.zeros_like(value))
        return carry

    def add(i, carry):
        value = parts[0, i].astype(f32)
        for n in range(1, parts.shape[0]):
            value += parts[n, i].astype(f32)
        summed[i] = value.astype(bf16)
        return carry

    lax.fori_loop(0, WCAP, select, 0, unroll=4)
    lax.fori_loop(0, summed.shape[0], add, 0, unroll=4)


def whole_block(quarters, c):
    return jnp.concatenate([quarters[x, c] for x in range(NX)], axis=0)


def forward_kernel(info, code, hidden, quarters, _after, mine, theirs, total):
    my_core = info[2]
    total[...] = jnp.zeros_like(total)

    def step(i, carry):
        adds = []
        for u in range(UNROLL):
            c = i * UNROLL + u
            word = code[c]
            lanes = pl.ds(pl.multiple_of(((word >> 8) & 15) * BS, BS), BS)
            w = whole_block(quarters, c)
            adds.append((word >> 12, jnp.dot(hidden[:, lanes], w, preferred_element_type=f32)))
        for col, value in adds:
            total[col] += value
        return carry

    lax.fori_loop(0, (info[0] + UNROLL - 1) // UNROLL, step, 0)
    for zl in range(NZL):
        for sub in range(4):
            mine[zl, sub] = total[(2 * zl + my_core) * 4 + sub]
            theirs[zl, sub] = total[(2 * zl + 1 - my_core) * 4 + sub]


def backward_kernel(info, code, cols, quarters, back, total):
    total[...] = jnp.zeros_like(total)

    def step(i, carry):
        adds = []
        for u in range(UNROLL):
            c = i * UNROLL + u
            word = code[c]
            w = whole_block(quarters, c)
            value = lax.dot_general(cols[word >> 12], w, (((1,), (1,)), ((), ())), preferred_element_type=f32)
            adds.append(((word >> 8) & 15, value))
        for r, value in adds:
            total[r] += value
        return carry

    lax.fori_loop(0, (info[0] + UNROLL - 1) // UNROLL, step, 0)
    for r in range(total.shape[0]):
        back[:, r * BS : (r + 1) * BS] = total[r].astype(bf16)


def chip_kernel(info, mine, came, own, s1, s2, s3):
    my_zl = info[4]
    own[...] = mine[my_zl] + came[my_zl]
    for k, out in enumerate((s1, s2, s3)):
        zl = (my_zl + k + 1) % NZL
        out[...] = (mine[zl] + came[zl]).astype(bf16)


def project_kernel(own, r1, r2, r3, _after, out):
    for sub in range(4):
        value = own[sub] + r1[sub].astype(f32) + r2[sub].astype(f32) + r3[sub].astype(f32)
        out[:, sub * BS : (sub + 1) * BS] = value.astype(bf16)


def adam_kernel(place, stacked, came, _after, new_w, new_m, new_v, rows, grad):
    slots, share = new_w.shape
    places = came.shape[0] * PAIR
    width = stacked.shape[1] // BS
    for j in range(slots):
        word = jnp.maximum(place[j] - 1, 0)
        g, row = word % places, word // places
        filled = place[j] > 0
        here = row < slots
        entry = jnp.maximum(row - slots, 0)
        own = stacked[pl.ds(jnp.minimum(row, slots - 1), 1), :]
        for n in range(width):
            lanes = slice(n * BS, (n + 1) * BS)
            moved = came[entry // MV, pl.ds(2 * PAIR + width * (entry % MV) + n, 1), :]
            rows[j : j + 1, lanes] = jnp.where(filled, jnp.where(here, own[:, lanes], moved), 0.0)
        for b in range(2):
            value = came[g // PAIR, pl.ds(2 * (g % PAIR) + b, 1), :]
            grad[j : j + 1, b * BS : (b + 1) * BS] = jnp.where(filled, value, 0.0)
    w, m, v = adam_update(rows[:, :share], rows[:, share : 2 * share], rows[:, 2 * share :], grad[...])
    new_w[...] = w
    new_m[...] = m
    new_v[...] = v


def all_to_all(values, axis):
    return lax.all_to_all(values, axis, split_axis=0, concat_axis=0, tiled=True)


def shift(values, axis, count, step):
    return lax.ppermute(values, axis, [(i, (i + step) % count) for i in range(count)])


def shards(
    hidden,
    out_grad,
    block_weight,
    block_row,
    block_col,
    live_count,
    new_owner,
    new_slot,
    first_moment,
    second_moment,
):
    shard_count = lax.axis_size(SHARD)
    me = lax.axis_index(SHARD)
    dp_index = lax.axis_index(DP)
    x_index = lax.axis_index("x")
    tokens = hidden.shape[0]
    slot_count = block_weight.shape[1]
    row_local = hidden.shape[1] // BS
    share = first_moment.shape[2]
    scale = 1.0 / math.sqrt(tokens * lax.axis_size(DP))

    quarter = lax.dynamic_slice_in_dim(block_weight[0], x_index * (BS // NX), BS // NX, 1)
    quarter, sent = lax.optimization_barrier((quarter, out_grad))
    gathered = lax.all_gather(quarter, SHARD, axis=0, tiled=True)
    mine = all_to_all(call(repeat_kernel, like((NZL,) + out_grad.shape, bf16), 0, 1, byts=1024 * 1024)(sent), "zl")
    other = shift(mine, "core", 2, 1)
    weight_share = lax.dynamic_slice_in_dim(block_weight[0], dp_index * 2, 2, 1).reshape(slot_count, share)
    stacked = jnp.concatenate([weight_share.astype(f32), first_moment[0], second_moment[0]], axis=1)

    fits, code, counts, send, state_send, place = make_plan(
        block_row, block_col, live_count, new_owner, new_slot, row_local, me
    )
    info = jnp.stack(counts + [lax.axis_index("core"), x_index, lax.axis_index("zl"), lax.axis_index("zh")])

    partial, cols = call(
        grad_kernel,
        (like((NX, NY * NZH * 2, GCAP, BS), bf16), like((shard_count * 4, BS, BS), bf16)),
        2,
        3,
        [pltpu.VMEM((row_local, BS, BS), bf16), pltpu.VMEM((BS * GCAP, BS), f32)],
        flops=2 * WCAP * BS**3,
        byts=4 * 1024 * 1024,
    )(info, code, hidden, mine, other)
    along_x = all_to_all(partial, "x")
    picked, summed = call(
        select_sum_kernel,
        (like((WCAP, BS // NX, BS), bf16), like(partial.shape[1:], bf16)),
        2,
        2,
        byts=4 * 1024 * 1024,
    )(info, code, gathered, along_x)
    quarters = lax.all_gather(picked, "x", axis=0)
    along_yz = all_to_all(summed.reshape(NY * NZH, 2, GCAP, BS), ("y", "zh"))
    packed = call(
        functools.partial(share_kernel, scale),
        like((shard_count, 2 * PAIR + MV * stacked.shape[1] // BS, BS), f32),
        2,
        2,
        [pltpu.VMEM((2, GCAP, BS), f32)],
        byts=1024 * 1024,
        n_after=2,
    )(send, state_send, along_yz, stacked, place, fits)
    shares = all_to_all(packed, SHARD)

    out_mine, out_theirs = call(
        forward_kernel,
        (
            like((NZL, 4, tokens, BS), f32),
            like((NZL, 4, tokens, BS), f32),
        ),
        2,
        2,
        [pltpu.VMEM((shard_count * 4, tokens, BS), f32)],
        flops=2 * WCAP * BS**3,
        byts=8 * 1024 * 1024,
        n_after=1,
    )(info, code, hidden, quarters, packed)
    came = shift(out_theirs, "core", 2, 1)
    hidden_grad = call(
        backward_kernel,
        like(hidden.shape, bf16),
        2,
        2,
        [pltpu.VMEM((row_local, tokens, BS), f32)],
        flops=2 * WCAP * BS**3,
        byts=4 * 1024 * 1024,
    )(info, code, cols, quarters)
    part = (4, tokens, BS)
    own, s1, s2, s3 = call(
        chip_kernel, (like(part, f32),) + (like(part, bf16),) * 3, 1, 2, byts=3 * 1024 * 1024
    )(info, out_mine, came)
    r2, r1, r3 = (shift(s, "zl", NZL, k) for k, s in ((2, s2), (1, s1), (3, s3)))
    projected = call(project_kernel, like(out_grad.shape, bf16), 0, 4, byts=1024 * 1024, n_after=1)(
        own, r1, r2, r3, hidden_grad
    )

    shape = like((slot_count, share), f32)
    new_weight, new_first, new_second = call(
        adam_kernel,
        (shape, shape, shape),
        1,
        2,
        [pltpu.VMEM((slot_count, 3 * share), f32), pltpu.VMEM((slot_count, share), f32)],
        byts=1024 * 1024,
        n_after=1,
    )(place, stacked, shares, projected)
    result = (projected, hidden_grad, new_weight[None], new_first[None], new_second[None])
    return lax.cond(
        fits[0] > 0,
        lambda: result,
        lambda: general(
            hidden,
            out_grad,
            block_weight,
            block_row,
            block_col,
            live_count,
            new_owner,
            new_slot,
            first_moment,
            second_moment,
        ),
    )


def solution(mesh):
    split = Mesh(mesh.devices.reshape(NY, NX, NZH, NZL, 2), ("y", "x", "zh", "zl", "core"))
    in_specs = (
        P(DP, SHARD),
        P(DP, SHARD),
        P(SHARD, None, None, None),
        P(),
        P(),
        P(),
        P(),
        P(),
        P(SHARD, None, DP),
        P(SHARD, None, DP),
    )
    out_specs = (
        P(DP, SHARD),
        P(DP, SHARD),
        P(SHARD, None, DP),
        P(SHARD, None, DP),
        P(SHARD, None, DP),
    )
    return jax.shard_map(shards, mesh=split, in_specs=in_specs, out_specs=out_specs, check_vma=False)
```

```python
import functools
import math

import jax
import jax.numpy as jnp
from jax import lax
from jax.experimental import pallas as pl
from jax.experimental.pallas import tpu as pltpu
from jax.sharding import Mesh, PartitionSpec as P

DP = ("y", "x", "zh")
SHARD = ("zl", "core")
MV = 2


LEARN_RATE = 0.01
BETA_ONE = 0.9
BETA_TWO = 0.95
EPSILON = 1e-08


def adam_update(weight, first_state, second_state, gradient):
    first_state = BETA_ONE * first_state + (1.0 - BETA_ONE) * gradient
    second_state = BETA_TWO * second_state + (1.0 - BETA_TWO) * gradient * gradient
    weight = weight - LEARN_RATE * first_state / (jnp.sqrt(second_state) + EPSILON)
    return (weight, first_state, second_state)


def send_positions(owner_devices, shard_count, slot_count):
    sources = jnp.arange(shard_count, dtype=jnp.int32)[:, None]
    moving = (owner_devices >= 0) & (owner_devices != sources)
    slot_ids = jnp.arange(slot_count)
    earlier = slot_ids[None, :] < slot_ids[:, None]
    matches = (
        (owner_devices[:, :, None] == owner_devices[:, None, :])
        & moving[:, None, :]
        & earlier[None, :, :]
    )
    return (moving, jnp.sum(matches, axis=2))


def pack_moving(values, owner_row, moving_row, position_row, shard_count, capacity):
    slot_ids = jnp.arange(values.shape[0], dtype=jnp.int32)
    targets = owner_row * capacity + position_row
    entries = jnp.arange(shard_count * capacity, dtype=jnp.int32)
    matches = (targets[None, :] == entries[:, None]) & moving_row[None, :]
    source = jnp.sum(jnp.where(matches, slot_ids[None, :], 0), axis=1)
    filled = jnp.any(matches, axis=1)
    packed = jnp.where(filled[:, None], jnp.take(values, source, axis=0), 0.0)
    return packed.reshape(shard_count, capacity, values.shape[1])


def place_blocks(
    received,
    own_values,
    owner_devices,
    destination_slot_list,
    moving,
    positions,
    my_index,
    capacity,
):
    shard_count, slot_count = owner_devices.shape
    slot_ids = jnp.arange(slot_count, dtype=jnp.int32)
    entries = (jnp.arange(shard_count, dtype=jnp.int32)[:, None] * capacity + positions).reshape(-1)
    to_me = (moving & (owner_devices == my_index)).reshape(-1)
    matches = to_me[None, :] & (destination_slot_list.reshape(-1)[None, :] == slot_ids[:, None])
    arrived = jnp.any(matches, axis=1)
    from_entry = jnp.sum(jnp.where(matches, entries[None, :], 0), axis=1)
    flattened = received.reshape(shard_count * capacity, received.shape[2])
    arrival_rows = jnp.take(flattened, from_entry, axis=0)
    stay_hit = (owner_devices[my_index] == my_index)[None, :] & (
        destination_slot_list[my_index][None, :] == slot_ids[:, None]
    )
    stayed = jnp.any(stay_hit, axis=1)
    from_slot = jnp.sum(jnp.where(stay_hit, slot_ids[None, :], 0), axis=1)
    kept_rows = jnp.take(own_values, from_slot, axis=0)
    return jnp.where(arrived[:, None], arrival_rows, jnp.where(stayed[:, None], kept_rows, 0.0))


def local_place(block_ids, first_id, local_count):
    local_ids = block_ids - first_id
    inside = (local_ids >= 0) & (local_ids < local_count)
    return jnp.where(inside, local_ids, local_count)


def general(
    hidden,
    out_grad,
    block_weight,
    block_row,
    block_col,
    live_count,
    new_owner,
    new_slot,
    first_moment,
    second_moment,
):
    shard_count = lax.axis_size(SHARD)
    dp_count = lax.axis_size(DP)
    my_index = lax.axis_index(SHARD)
    dp_index = lax.axis_index(DP)
    tokens_dev = hidden.shape[0]
    slot_count = block_weight.shape[1]
    block_size = block_weight.shape[2]
    share_size = first_moment.shape[2]
    row_blocks = hidden.shape[1] * shard_count // block_size
    col_blocks = out_grad.shape[1] * shard_count // block_size
    grad_scale = 1.0 / math.sqrt(tokens_dev * dp_count)
    slot_ids = jnp.arange(slot_count)
    live_all = slot_ids[None, :] < live_count[:, None]
    my_live = live_all[my_index]
    my_rows = block_row[my_index]
    my_cols = block_col[my_index]
    zero_bf = jnp.zeros((), jnp.bfloat16)
    full_hidden, full_grad = (
        lax.all_gather(hidden, SHARD, axis=1, tiled=True),
        lax.all_gather(out_grad, SHARD, axis=1, tiled=True),
    )
    hidden_blocks = full_hidden.reshape(tokens_dev, row_blocks, block_size)
    grad_blocks = full_grad.reshape(tokens_dev, col_blocks, block_size)
    own_hidden = jnp.take(hidden_blocks, my_rows, axis=1)
    own_grad = jnp.take(grad_blocks, my_cols, axis=1)
    grad_share = None
    col_local = col_blocks // shard_count
    row_local = row_blocks // shard_count

    def one_shard(totals, member):
        blocks, shard_index = member
        row_ids = block_row[shard_index]
        col_ids = block_col[shard_index]
        weights = jnp.where(live_all[shard_index][:, None, None], blocks, zero_bf)
        hidden_part = jnp.take(hidden_blocks, row_ids, axis=1)
        grad_part = jnp.take(grad_blocks, col_ids, axis=1)
        forward = jnp.einsum(
            "tkr,krc->tkc", hidden_part, weights, preferred_element_type=jnp.float32
        )
        backward = jnp.einsum(
            "tkc,krc->tkr", grad_part, weights, preferred_element_type=jnp.float32
        )
        col_place = local_place(col_ids, my_index * col_local, col_local)
        row_place = local_place(row_ids, my_index * row_local, row_local)
        out_total = totals[0].at[:, col_place].add(forward, mode="drop")
        back_total = totals[1].at[:, row_place].add(backward, mode="drop")
        return ((out_total, back_total), None)

    initial = (
        jnp.zeros((tokens_dev, col_local, block_size), jnp.float32),
        jnp.zeros((tokens_dev, row_local, block_size), jnp.float32),
    )
    totals = initial
    blocks_in = lax.all_gather(block_weight, SHARD, axis=0, tiled=True)
    indices = jnp.arange(blocks_in.shape[0], dtype=jnp.int32)
    totals, unused = lax.scan(one_shard, totals, (blocks_in, indices))
    out_total, back_total = totals
    projected = out_total.reshape(tokens_dev, col_local * block_size).astype(jnp.bfloat16)
    hidden_grad = back_total.reshape(tokens_dev, row_local * block_size).astype(jnp.bfloat16)
    blocks = (
        jnp.einsum("tkr,tkc->krc", own_hidden, own_grad, preferred_element_type=jnp.float32)
        * grad_scale
    )
    blocks = jnp.where(my_live[:, None, None], blocks, 0.0)
    grad_share = lax.psum_scatter(
        blocks.reshape(slot_count, block_size * block_size), DP, scatter_dimension=1, tiled=True
    )
    moving, positions = send_positions(new_owner, shard_count, slot_count)
    my_owner = new_owner[my_index]
    my_moving = moving[my_index]
    my_positions = positions[my_index]
    flat_weight = block_weight[0].reshape(slot_count, block_size * block_size)
    weight_share = lax.dynamic_slice_in_dim(
        flat_weight, dp_index * share_size, share_size, 1
    ).astype(jnp.float32)
    updated, first_state, second_state = adam_update(
        weight_share, first_moment[0], second_moment[0], grad_share
    )
    stacked = jnp.concatenate([updated, first_state, second_state], axis=1)
    packed = pack_moving(stacked, my_owner, my_moving, my_positions, shard_count, MV)
    received = lax.all_to_all(packed, SHARD, split_axis=0, concat_axis=0, tiled=True)
    placed = place_blocks(received, stacked, new_owner, new_slot, moving, positions, my_index, MV)
    new_weight = placed[:, :share_size]
    new_first = placed[:, share_size : 2 * share_size]
    new_second = placed[:, 2 * share_size :]
    return (projected, hidden_grad, new_weight[None], new_first[None], new_second[None])


WCAP = 44
GCAP = 40
PAIR = 14
UNROLL = 4
NX, NY, NZH, NZL = 4, 8, 2, 4
BS = 128
VMEM_LIMIT = 10 * 1024 * 1024
f32 = jnp.float32
bf16 = jnp.bfloat16
i32 = jnp.int32


def call(kernel, outs, n_smem, n_vmem, scratch=(), flops=0, byts=0, n_after=0):
    smem = pl.BlockSpec(memory_space=pltpu.SMEM)
    vmem = pl.BlockSpec(memory_space=pltpu.VMEM)
    anywhere = pl.BlockSpec(memory_space=pl.ANY)
    return pl.pallas_call(
        kernel,
        out_shape=outs,
        in_specs=[smem] * n_smem + [vmem] * n_vmem + [anywhere] * n_after,
        out_specs=jax.tree.map(lambda _: vmem, outs),
        scratch_shapes=list(scratch),
        compiler_params=pltpu.CompilerParams(vmem_limit_bytes=VMEM_LIMIT),
        cost_estimate=pl.CostEstimate(flops=flops, bytes_accessed=byts, transcendentals=0),
    )


def like(shape, dtype):
    return jax.ShapeDtypeStruct(shape, dtype)


def make_plan(block_row, block_col, live_count, new_owner, new_slot, row_local, me):
    shard_count, slot_count = block_row.shape
    total = shard_count * slot_count
    ids = jnp.arange(total, dtype=i32)
    live = (jnp.arange(slot_count)[None, :] < live_count[:, None]).reshape(total)
    row = block_row.reshape(total)
    col = block_col.reshape(total)
    owner = jnp.where(live, new_owner.reshape(total), -1)
    slot = new_slot.reshape(total)
    kept = owner >= 0
    row_shard = row // row_local
    key = jnp.where(kept, ids, ids + total)
    same = row_shard[:, None] == row_shard[None, :]
    before = same & live[None, :] & (key[None, :] < key[:, None])
    rank = jnp.sum(before.astype(i32), axis=1)
    earlier = same & (owner[:, None] == owner[None, :]) & (ids[None, :] < ids[:, None])
    pos = jnp.sum(earlier.astype(i32), axis=1)
    fits = (
        (jnp.max(jnp.where(live, rank, 0)) < WCAP)
        & (jnp.max(jnp.where(kept, rank, 0)) < GCAP)
        & (jnp.max(jnp.where(kept, pos, 0)) < PAIR)
    )

    here = live & (row_shard == me)
    words = ids + 256 * ((row - row_local * me) + 16 * col)
    hit = here[None, :] & (rank[None, :] == jnp.arange(WCAP)[:, None])
    code = jnp.sum(jnp.where(hit, words[None, :], 0), axis=1)
    counts = [jnp.minimum(jnp.sum(here.astype(i32)), WCAP), jnp.minimum(jnp.sum((here & kept).astype(i32)), GCAP)]
    going = jnp.where(here & kept, owner * PAIR + pos, -1)
    send_hit = going[None, :] == jnp.arange(shard_count * PAIR)[:, None]
    send = jnp.minimum(jnp.sum(jnp.where(send_hit, rank[None, :], 0), axis=1), GCAP - 1)
    owner2 = owner.reshape(shard_count, slot_count)
    sources = jnp.arange(shard_count, dtype=i32)[:, None]
    slots = jnp.arange(slot_count, dtype=i32)[None, :]
    moving, positions = send_positions(owner2, shard_count, slot_count)
    target = jnp.where(moving & (sources == me), owner2 * MV + positions, -1).reshape(total)
    state_hit = target[None, :] == jnp.arange(shard_count * MV)[:, None]
    state_send = jnp.sum(jnp.where(state_hit, (ids % slot_count)[None, :], 0), axis=1)
    state_row = jnp.where(sources == me, slots, slot_count + sources * MV + positions).reshape(total)
    landing = 1 + row_shard * PAIR + jnp.minimum(pos, PAIR - 1) + shard_count * PAIR * state_row
    lands = (owner == me)[None, :] & (slot[None, :] == jnp.arange(slot_count)[:, None])
    place = jnp.sum(jnp.where(lands, landing[None, :], 0), axis=1)
    return fits.astype(i32).reshape(1), code, counts, send, state_send, place


def repeat_kernel(value, out):
    for n in range(out.shape[0]):
        out[n] = value[...]


def grad_kernel(info, code, hidden, mine, other, out, cols, hidden_t, total):
    my_core = info[2]
    for zl in range(NZL):
        for sub in range(4):
            lanes = slice(sub * BS, (sub + 1) * BS)
            cols[(2 * zl + my_core) * 4 + sub] = mine[zl, :, lanes]
            cols[(2 * zl + 1 - my_core) * 4 + sub] = other[zl, :, lanes]
    row_local = hidden.shape[1] // BS
    for r in range(row_local):
        hidden_t[r] = hidden[:, r * BS : (r + 1) * BS].T

    def step(i, carry):
        blocks = []
        for u in range(UNROLL):
            word = code[i * UNROLL + u]
            blocks.append(jnp.dot(hidden_t[(word >> 8) & 15], cols[word >> 12], preferred_element_type=f32))
        for u in range(UNROLL):
            total[pl.ds(i * UNROLL + u, BS, stride=GCAP), :] = blocks[u]
        return carry

    lax.fori_loop(0, (info[1] + UNROLL - 1) // UNROLL, step, 0)
    for x in range(NX):
        for y in range(NY):
            for q in range(4):
                source = 16 * y + 4 * x + q
                out[x, 4 * y + q] = total[source * GCAP : (source + 1) * GCAP, :].astype(bf16)


def share_kernel(scale, send, state_send, keep, came, stacked, _after, _after2, out, total):
    total[...] = (keep[...] + came[...]) * scale
    width = stacked.shape[1] // BS
    for d in range(out.shape[0]):
        for p in range(PAIR):
            rank = send[d * PAIR + p]
            for b in range(2):
                out[d, 2 * p + b : 2 * p + b + 1, :] = total[b, pl.ds(rank, 1), :]
        for p in range(MV):
            row = stacked[pl.ds(state_send[d * MV + p], 1), :]
            for n in range(width):
                at = 2 * PAIR + width * p + n
                out[d, at : at + 1, :] = row[:, n * BS : (n + 1) * BS]


def select_kernel(info, code, gathered, _after, picked):
    def select(c, carry):
        value = gathered[code[c] & 255]
        picked[c] = jnp.where(c < info[0], value, jnp.zeros_like(value))
        return carry

    lax.fori_loop(0, WCAP, select, 0, unroll=4)


def sum_kernel(parts, out):
    def step(i, carry):
        value = parts[0, i].astype(f32)
        for n in range(1, parts.shape[0]):
            value += parts[n, i].astype(f32)
        out[i] = value.astype(bf16)
        return carry

    lax.fori_loop(0, out.shape[0], step, 0, unroll=4)


def pair_kernel(info, parts, keep, send):
    my_zh = info[5]
    for out, zh in ((keep, my_zh), (send, 1 - my_zh)):
        for b in range(2):
            value = parts[0, 2 * zh + b].astype(f32)
            for n in range(1, parts.shape[0]):
                value += parts[n, 2 * zh + b].astype(f32)
            out[b] = value


def forward_kernel(info, code, hidden, w0, w1, w2, w3, _after, mine, theirs, weights, total, sems):
    my_core, my_x = info[2], info[3]
    copies = [
        pltpu.make_async_copy(part, weights.at[:, (my_x + NX - k) % NX], sems.at[k])
        for k, part in enumerate((w0, w1, w2, w3))
    ]
    for copy in copies:
        copy.start()
    total[...] = jnp.zeros_like(total)
    for copy in copies:
        copy.wait()

    def step(i, carry):
        adds = []
        for u in range(UNROLL):
            c = i * UNROLL + u
            word = code[c]
            lanes = pl.ds(pl.multiple_of(((word >> 8) & 15) * BS, BS), BS)
            w = weights[c].reshape(BS, BS)
            adds.append((word >> 12, jnp.dot(hidden[:, lanes], w, preferred_element_type=f32)))
        for col, value in adds:
            total[col] += value
        return carry

    lax.fori_loop(0, (info[0] + UNROLL - 1) // UNROLL, step, 0)
    for zl in range(NZL):
        for sub in range(4):
            mine[zl, sub] = total[(2 * zl + my_core) * 4 + sub]
            theirs[zl, sub] = total[(2 * zl + 1 - my_core) * 4 + sub]


def backward_kernel(info, code, cols, weights, back, total):
    total[...] = jnp.zeros_like(total)

    def step(i, carry):
        adds = []
        for u in range(UNROLL):
            c = i * UNROLL + u
            word = code[c]
            w = weights[c].reshape(BS, BS)
            value = lax.dot_general(cols[word >> 12], w, (((1,), (1,)), ((), ())), preferred_element_type=f32)
            adds.append(((word >> 8) & 15, value))
        for r, value in adds:
            total[r] += value
        return carry

    lax.fori_loop(0, (info[0] + UNROLL - 1) // UNROLL, step, 0)
    for r in range(total.shape[0]):
        back[:, r * BS : (r + 1) * BS] = total[r].astype(bf16)


def chip_kernel(info, mine, came, own, s1, s2, s3):
    my_zl = info[4]
    own[...] = mine[my_zl] + came[my_zl]
    for k, out in enumerate((s1, s2, s3)):
        zl = (my_zl + k + 1) % NZL
        out[...] = (mine[zl] + came[zl]).astype(bf16)


def project_kernel(own, r1, r2, r3, _after, out):
    for sub in range(4):
        value = own[sub] + r1[sub].astype(f32) + r2[sub].astype(f32) + r3[sub].astype(f32)
        out[:, sub * BS : (sub + 1) * BS] = value.astype(bf16)


def adam_kernel(place, stacked, came, _after, new_w, new_m, new_v, rows, grad):
    slots, share = new_w.shape
    places = came.shape[0] * PAIR
    width = stacked.shape[1] // BS
    for j in range(slots):
        word = jnp.maximum(place[j] - 1, 0)
        g, row = word % places, word // places
        filled = place[j] > 0
        here = row < slots
        entry = jnp.maximum(row - slots, 0)
        own = stacked[pl.ds(jnp.minimum(row, slots - 1), 1), :]
        for n in range(width):
            lanes = slice(n * BS, (n + 1) * BS)
            moved = came[entry // MV, pl.ds(2 * PAIR + width * (entry % MV) + n, 1), :]
            rows[j : j + 1, lanes] = jnp.where(filled, jnp.where(here, own[:, lanes], moved), 0.0)
        for b in range(2):
            value = came[g // PAIR, pl.ds(2 * (g % PAIR) + b, 1), :]
            grad[j : j + 1, b * BS : (b + 1) * BS] = jnp.where(filled, value, 0.0)
    w, m, v = adam_update(rows[:, :share], rows[:, share : 2 * share], rows[:, 2 * share :], grad[...])
    new_w[...] = w
    new_m[...] = m
    new_v[...] = v


def all_to_all(values, axis):
    return lax.all_to_all(values, axis, split_axis=0, concat_axis=0, tiled=True)


def shift(values, axis, count, step):
    return lax.ppermute(values, axis, [(i, (i + step) % count) for i in range(count)])


def shards(
    hidden,
    out_grad,
    block_weight,
    block_row,
    block_col,
    live_count,
    new_owner,
    new_slot,
    first_moment,
    second_moment,
):
    shard_count = lax.axis_size(SHARD)
    me = lax.axis_index(SHARD)
    dp_index = lax.axis_index(DP)
    x_index = lax.axis_index("x")
    tokens = hidden.shape[0]
    slot_count = block_weight.shape[1]
    row_local = hidden.shape[1] // BS
    share = first_moment.shape[2]
    scale = 1.0 / math.sqrt(tokens * lax.axis_size(DP))

    quarter = lax.dynamic_slice_in_dim(block_weight[0], x_index * (BS // NX), BS // NX, 1)
    quarter, sent = lax.optimization_barrier((quarter, out_grad))
    gathered = lax.all_gather(quarter, SHARD, axis=0, tiled=True)
    mine = all_to_all(call(repeat_kernel, like((NZL,) + out_grad.shape, bf16), 0, 1, byts=1024 * 1024)(sent), "zl")
    other = shift(mine, "core", 2, 1)
    weight_share = lax.dynamic_slice_in_dim(block_weight[0], dp_index * 2, 2, 1).reshape(slot_count, share)
    stacked = jnp.concatenate([weight_share.astype(f32), first_moment[0], second_moment[0]], axis=1)

    fits, code, counts, send, state_send, place = make_plan(
        block_row, block_col, live_count, new_owner, new_slot, row_local, me
    )
    info = jnp.stack(counts + [lax.axis_index("core"), x_index, lax.axis_index("zl"), lax.axis_index("zh")])

    partial, cols = call(
        grad_kernel,
        (like((NX, NY * NZH * 2, GCAP, BS), bf16), like((shard_count * 4, BS, BS), bf16)),
        2,
        3,
        [pltpu.VMEM((row_local, BS, BS), bf16), pltpu.VMEM((BS * GCAP, BS), f32)],
        flops=2 * WCAP * BS**3,
        byts=4 * 1024 * 1024,
    )(info, code, hidden, mine, other)
    along_x = all_to_all(partial, "x")
    summed = call(sum_kernel, like(partial.shape[1:], bf16), 0, 1, byts=2 * 1024 * 1024)(along_x)
    along_y = all_to_all(summed.reshape(NY, 2 * NZH, GCAP, BS), "y")
    half = like((2, GCAP, BS), f32)
    keep, send_zh = call(pair_kernel, (half, half), 1, 1, byts=1024 * 1024)(info, along_y)
    came_zh = shift(send_zh, "zh", NZH, 1)

    picked = call(select_kernel, like((WCAP, BS // NX, BS), bf16), 2, 1, byts=1024 * 1024, n_after=1)(
        info, code, gathered, summed
    )
    w2, w1, w3 = (shift(picked, "x", NX, k) for k in (2, 1, 3))
    packed = call(
        functools.partial(share_kernel, scale),
        like((shard_count, 2 * PAIR + MV * stacked.shape[1] // BS, BS), f32),
        2,
        3,
        [pltpu.VMEM((2, GCAP, BS), f32)],
        byts=1024 * 1024,
        n_after=2,
    )(send, state_send, keep, came_zh, stacked, place, fits)
    shares = all_to_all(packed, SHARD)

    out_mine, out_theirs, weights = call(
        forward_kernel,
        (
            like((NZL, 4, tokens, BS), f32),
            like((NZL, 4, tokens, BS), f32),
            like((WCAP, NX, BS // NX, BS), bf16),
        ),
        2,
        1,
        [pltpu.VMEM((shard_count * 4, tokens, BS), f32), pltpu.SemaphoreType.DMA((NX,))],
        flops=2 * WCAP * BS**3,
        byts=8 * 1024 * 1024,
        n_after=5,
    )(info, code, hidden, picked, w1, w2, w3, packed)
    came = shift(out_theirs, "core", 2, 1)
    hidden_grad = call(
        backward_kernel,
        like(hidden.shape, bf16),
        2,
        2,
        [pltpu.VMEM((row_local, tokens, BS), f32)],
        flops=2 * WCAP * BS**3,
        byts=4 * 1024 * 1024,
    )(info, code, cols, weights)
    part = (4, tokens, BS)
    own, s1, s2, s3 = call(
        chip_kernel, (like(part, f32),) + (like(part, bf16),) * 3, 1, 2, byts=3 * 1024 * 1024
    )(info, out_mine, came)
    r2, r1, r3 = (shift(s, "zl", NZL, k) for k, s in ((2, s2), (1, s1), (3, s3)))
    projected = call(project_kernel, like(out_grad.shape, bf16), 0, 4, byts=1024 * 1024, n_after=1)(
        own, r1, r2, r3, hidden_grad
    )

    shape = like((slot_count, share), f32)
    new_weight, new_first, new_second = call(
        adam_kernel,
        (shape, shape, shape),
        1,
        2,
        [pltpu.VMEM((slot_count, 3 * share), f32), pltpu.VMEM((slot_count, share), f32)],
        byts=1024 * 1024,
        n_after=1,
    )(place, stacked, shares, hidden_grad)
    result = (projected, hidden_grad, new_weight[None], new_first[None], new_second[None])
    return lax.cond(
        fits[0] > 0,
        lambda: result,
        lambda: general(
            hidden,
            out_grad,
            block_weight,
            block_row,
            block_col,
            live_count,
            new_owner,
            new_slot,
            first_moment,
            second_moment,
        ),
    )


def solution(mesh):
    split = Mesh(mesh.devices.reshape(NY, NX, NZH, NZL, 2), ("y", "x", "zh", "zl", "core"))
    in_specs = (
        P(DP, SHARD),
        P(DP, SHARD),
        P(SHARD, None, None, None),
        P(),
        P(),
        P(),
        P(),
        P(),
        P(SHARD, None, DP),
        P(SHARD, None, DP),
    )
    out_specs = (
        P(DP, SHARD),
        P(DP, SHARD),
        P(SHARD, None, DP),
        P(SHARD, None, DP),
        P(SHARD, None, DP),
    )
    return jax.shard_map(shards, mesh=split, in_specs=in_specs, out_specs=out_specs, check_vma=False)
```

```python
import functools
import math

import jax
import jax.numpy as jnp
from jax import lax
from jax.experimental import pallas as pl
from jax.experimental.pallas import tpu as pltpu
from jax.sharding import Mesh, PartitionSpec as P

DP = ("y", "x", "zh")
SHARD = ("zl", "core")
MV = 2


LEARN_RATE = 0.01
BETA_ONE = 0.9
BETA_TWO = 0.95
EPSILON = 1e-08


def adam_update(weight, first_state, second_state, gradient):
    first_state = BETA_ONE * first_state + (1.0 - BETA_ONE) * gradient
    second_state = BETA_TWO * second_state + (1.0 - BETA_TWO) * gradient * gradient
    weight = weight - LEARN_RATE * first_state / (jnp.sqrt(second_state) + EPSILON)
    return (weight, first_state, second_state)


def send_positions(owner_devices, shard_count, slot_count):
    sources = jnp.arange(shard_count, dtype=jnp.int32)[:, None]
    moving = (owner_devices >= 0) & (owner_devices != sources)
    slot_ids = jnp.arange(slot_count)
    earlier = slot_ids[None, :] < slot_ids[:, None]
    matches = (
        (owner_devices[:, :, None] == owner_devices[:, None, :])
        & moving[:, None, :]
        & earlier[None, :, :]
    )
    return (moving, jnp.sum(matches, axis=2))


def pack_moving(values, owner_row, moving_row, position_row, shard_count, capacity):
    slot_ids = jnp.arange(values.shape[0], dtype=jnp.int32)
    targets = owner_row * capacity + position_row
    entries = jnp.arange(shard_count * capacity, dtype=jnp.int32)
    matches = (targets[None, :] == entries[:, None]) & moving_row[None, :]
    source = jnp.sum(jnp.where(matches, slot_ids[None, :], 0), axis=1)
    filled = jnp.any(matches, axis=1)
    packed = jnp.where(filled[:, None], jnp.take(values, source, axis=0), 0.0)
    return packed.reshape(shard_count, capacity, values.shape[1])


def place_blocks(
    received,
    own_values,
    owner_devices,
    destination_slot_list,
    moving,
    positions,
    my_index,
    capacity,
):
    shard_count, slot_count = owner_devices.shape
    slot_ids = jnp.arange(slot_count, dtype=jnp.int32)
    entries = (jnp.arange(shard_count, dtype=jnp.int32)[:, None] * capacity + positions).reshape(-1)
    to_me = (moving & (owner_devices == my_index)).reshape(-1)
    matches = to_me[None, :] & (destination_slot_list.reshape(-1)[None, :] == slot_ids[:, None])
    arrived = jnp.any(matches, axis=1)
    from_entry = jnp.sum(jnp.where(matches, entries[None, :], 0), axis=1)
    flattened = received.reshape(shard_count * capacity, received.shape[2])
    arrival_rows = jnp.take(flattened, from_entry, axis=0)
    stay_hit = (owner_devices[my_index] == my_index)[None, :] & (
        destination_slot_list[my_index][None, :] == slot_ids[:, None]
    )
    stayed = jnp.any(stay_hit, axis=1)
    from_slot = jnp.sum(jnp.where(stay_hit, slot_ids[None, :], 0), axis=1)
    kept_rows = jnp.take(own_values, from_slot, axis=0)
    return jnp.where(arrived[:, None], arrival_rows, jnp.where(stayed[:, None], kept_rows, 0.0))


def local_place(block_ids, first_id, local_count):
    local_ids = block_ids - first_id
    inside = (local_ids >= 0) & (local_ids < local_count)
    return jnp.where(inside, local_ids, local_count)


def general(
    hidden,
    out_grad,
    block_weight,
    block_row,
    block_col,
    live_count,
    new_owner,
    new_slot,
    first_moment,
    second_moment,
):
    shard_count = lax.axis_size(SHARD)
    dp_count = lax.axis_size(DP)
    my_index = lax.axis_index(SHARD)
    dp_index = lax.axis_index(DP)
    tokens_dev = hidden.shape[0]
    slot_count = block_weight.shape[1]
    block_size = block_weight.shape[2]
    share_size = first_moment.shape[2]
    row_blocks = hidden.shape[1] * shard_count // block_size
    col_blocks = out_grad.shape[1] * shard_count // block_size
    grad_scale = 1.0 / math.sqrt(tokens_dev * dp_count)
    slot_ids = jnp.arange(slot_count)
    live_all = slot_ids[None, :] < live_count[:, None]
    my_live = live_all[my_index]
    my_rows = block_row[my_index]
    my_cols = block_col[my_index]
    zero_bf = jnp.zeros((), jnp.bfloat16)
    full_hidden, full_grad = (
        lax.all_gather(hidden, SHARD, axis=1, tiled=True),
        lax.all_gather(out_grad, SHARD, axis=1, tiled=True),
    )
    hidden_blocks = full_hidden.reshape(tokens_dev, row_blocks, block_size)
    grad_blocks = full_grad.reshape(tokens_dev, col_blocks, block_size)
    own_hidden = jnp.take(hidden_blocks, my_rows, axis=1)
    own_grad = jnp.take(grad_blocks, my_cols, axis=1)
    grad_share = None
    col_local = col_blocks // shard_count
    row_local = row_blocks // shard_count

    def one_shard(totals, member):
        blocks, shard_index = member
        row_ids = block_row[shard_index]
        col_ids = block_col[shard_index]
        weights = jnp.where(live_all[shard_index][:, None, None], blocks, zero_bf)
        hidden_part = jnp.take(hidden_blocks, row_ids, axis=1)
        grad_part = jnp.take(grad_blocks, col_ids, axis=1)
        forward = jnp.einsum(
            "tkr,krc->tkc", hidden_part, weights, preferred_element_type=jnp.float32
        )
        backward = jnp.einsum(
            "tkc,krc->tkr", grad_part, weights, preferred_element_type=jnp.float32
        )
        col_place = local_place(col_ids, my_index * col_local, col_local)
        row_place = local_place(row_ids, my_index * row_local, row_local)
        out_total = totals[0].at[:, col_place].add(forward, mode="drop")
        back_total = totals[1].at[:, row_place].add(backward, mode="drop")
        return ((out_total, back_total), None)

    initial = (
        jnp.zeros((tokens_dev, col_local, block_size), jnp.float32),
        jnp.zeros((tokens_dev, row_local, block_size), jnp.float32),
    )
    totals = initial
    blocks_in = lax.all_gather(block_weight, SHARD, axis=0, tiled=True)
    indices = jnp.arange(blocks_in.shape[0], dtype=jnp.int32)
    totals, unused = lax.scan(one_shard, totals, (blocks_in, indices))
    out_total, back_total = totals
    projected = out_total.reshape(tokens_dev, col_local * block_size).astype(jnp.bfloat16)
    hidden_grad = back_total.reshape(tokens_dev, row_local * block_size).astype(jnp.bfloat16)
    blocks = (
        jnp.einsum("tkr,tkc->krc", own_hidden, own_grad, preferred_element_type=jnp.float32)
        * grad_scale
    )
    blocks = jnp.where(my_live[:, None, None], blocks, 0.0)
    grad_share = lax.psum_scatter(
        blocks.reshape(slot_count, block_size * block_size), DP, scatter_dimension=1, tiled=True
    )
    moving, positions = send_positions(new_owner, shard_count, slot_count)
    my_owner = new_owner[my_index]
    my_moving = moving[my_index]
    my_positions = positions[my_index]
    flat_weight = block_weight[0].reshape(slot_count, block_size * block_size)
    weight_share = lax.dynamic_slice_in_dim(
        flat_weight, dp_index * share_size, share_size, 1
    ).astype(jnp.float32)
    updated, first_state, second_state = adam_update(
        weight_share, first_moment[0], second_moment[0], grad_share
    )
    stacked = jnp.concatenate([updated, first_state, second_state], axis=1)
    packed = pack_moving(stacked, my_owner, my_moving, my_positions, shard_count, MV)
    received = lax.all_to_all(packed, SHARD, split_axis=0, concat_axis=0, tiled=True)
    placed = place_blocks(received, stacked, new_owner, new_slot, moving, positions, my_index, MV)
    new_weight = placed[:, :share_size]
    new_first = placed[:, share_size : 2 * share_size]
    new_second = placed[:, 2 * share_size :]
    return (projected, hidden_grad, new_weight[None], new_first[None], new_second[None])


WCAP = 44
GCAP = 40
PAIR = 14
UNROLL = 4
NX, NY, NZH, NZL = 4, 8, 2, 4
BS = 128
VMEM_LIMIT = 8 * 1024 * 1024
SMALL = 3 * 1024 * 1024
f32 = jnp.float32
bf16 = jnp.bfloat16
i32 = jnp.int32


def call(kernel, outs, n_smem, n_vmem, scratch=(), flops=0, byts=0, n_after=0, limit=VMEM_LIMIT):
    smem = pl.BlockSpec(memory_space=pltpu.SMEM)
    vmem = pl.BlockSpec(memory_space=pltpu.VMEM)
    anywhere = pl.BlockSpec(memory_space=pl.ANY)
    return pl.pallas_call(
        kernel,
        out_shape=outs,
        in_specs=[smem] * n_smem + [vmem] * n_vmem + [anywhere] * n_after,
        out_specs=jax.tree.map(lambda _: vmem, outs),
        scratch_shapes=list(scratch),
        compiler_params=pltpu.CompilerParams(vmem_limit_bytes=limit),
        cost_estimate=pl.CostEstimate(flops=flops, bytes_accessed=byts, transcendentals=0),
    )


def like(shape, dtype):
    return jax.ShapeDtypeStruct(shape, dtype)


def make_plan(block_row, block_col, live_count, new_owner, new_slot, row_local, me):
    shard_count, slot_count = block_row.shape
    total = shard_count * slot_count
    ids = jnp.arange(total, dtype=i32)
    live = (jnp.arange(slot_count)[None, :] < live_count[:, None]).reshape(total)
    row = block_row.reshape(total)
    col = block_col.reshape(total)
    owner = jnp.where(live, new_owner.reshape(total), -1)
    slot = new_slot.reshape(total)
    kept = owner >= 0
    row_shard = row // row_local
    key = jnp.where(kept, ids, ids + total)
    same = row_shard[:, None] == row_shard[None, :]
    before = same & live[None, :] & (key[None, :] < key[:, None])
    rank = jnp.sum(before.astype(i32), axis=1)
    earlier = same & (owner[:, None] == owner[None, :]) & (ids[None, :] < ids[:, None])
    pos = jnp.sum(earlier.astype(i32), axis=1)
    fits = (
        (jnp.max(jnp.where(live, rank, 0)) < WCAP)
        & (jnp.max(jnp.where(kept, rank, 0)) < GCAP)
        & (jnp.max(jnp.where(kept, pos, 0)) < PAIR)
    )

    here = live & (row_shard == me)
    words = ids + 256 * ((row - row_local * me) + 16 * col)
    hit = here[None, :] & (rank[None, :] == jnp.arange(WCAP)[:, None])
    code = jnp.sum(jnp.where(hit, words[None, :], 0), axis=1)
    counts = [jnp.minimum(jnp.sum(here.astype(i32)), WCAP), jnp.minimum(jnp.sum((here & kept).astype(i32)), GCAP)]
    going = jnp.where(here & kept, owner * PAIR + pos, -1)
    send_hit = going[None, :] == jnp.arange(shard_count * PAIR)[:, None]
    send = jnp.minimum(jnp.sum(jnp.where(send_hit, rank[None, :], 0), axis=1), GCAP - 1)
    owner2 = owner.reshape(shard_count, slot_count)
    sources = jnp.arange(shard_count, dtype=i32)[:, None]
    slots = jnp.arange(slot_count, dtype=i32)[None, :]
    moving, positions = send_positions(owner2, shard_count, slot_count)
    target = jnp.where(moving & (sources == me), owner2 * MV + positions, -1).reshape(total)
    state_hit = target[None, :] == jnp.arange(shard_count * MV)[:, None]
    state_send = jnp.sum(jnp.where(state_hit, (ids % slot_count)[None, :], 0), axis=1)
    state_row = jnp.where(sources == me, slots, slot_count + sources * MV + positions).reshape(total)
    landing = 1 + row_shard * PAIR + jnp.minimum(pos, PAIR - 1) + shard_count * PAIR * state_row
    lands = (owner == me)[None, :] & (slot[None, :] == jnp.arange(slot_count)[:, None])
    place = jnp.sum(jnp.where(lands, landing[None, :], 0), axis=1)
    return fits.astype(i32).reshape(1), code, counts, send, state_send, place


def repeat_kernel(value, out):
    for n in range(out.shape[0]):
        out[n] = value[...]


def grad_kernel(info, code, hidden, mine, other, out, cols, hidden_t, total):
    my_core = info[2]
    for zl in range(NZL):
        for sub in range(4):
            lanes = slice(sub * BS, (sub + 1) * BS)
            cols[(2 * zl + my_core) * 4 + sub] = mine[zl, :, lanes]
            cols[(2 * zl + 1 - my_core) * 4 + sub] = other[zl, :, lanes]
    row_local = hidden.shape[1] // BS
    for r in range(row_local):
        hidden_t[r] = hidden[:, r * BS : (r + 1) * BS].T

    def step(i, carry):
        blocks = []
        for u in range(UNROLL):
            word = code[i * UNROLL + u]
            blocks.append(jnp.dot(hidden_t[(word >> 8) & 15], cols[word >> 12], preferred_element_type=f32))
        for u in range(UNROLL):
            total[pl.ds(i * UNROLL + u, BS, stride=GCAP), :] = blocks[u]
        return carry

    lax.fori_loop(0, (info[1] + UNROLL - 1) // UNROLL, step, 0)
    for x in range(NX):
        for y in range(NY):
            for q in range(4):
                source = 16 * y + 4 * x + q
                out[x, 4 * y + q] = total[source * GCAP : (source + 1) * GCAP, :].astype(bf16)


def share_kernel(scale, send, state_send, keep, came, stacked, _after, _after2, out, total):
    total[...] = (keep[...] + came[...]) * scale
    width = stacked.shape[1] // BS
    for d in range(out.shape[0]):
        for p in range(PAIR):
            rank = send[d * PAIR + p]
            for b in range(2):
                out[d, 2 * p + b : 2 * p + b + 1, :] = total[b, pl.ds(rank, 1), :]
        for p in range(MV):
            row = stacked[pl.ds(state_send[d * MV + p], 1), :]
            for n in range(width):
                at = 2 * PAIR + width * p + n
                out[d, at : at + 1, :] = row[:, n * BS : (n + 1) * BS]


def select_kernel(info, code, gathered, _after, picked):
    def select(c, carry):
        value = gathered[code[c] & 255]
        picked[c] = jnp.where(c < info[0], value, jnp.zeros_like(value))
        return carry

    lax.fori_loop(0, WCAP, select, 0, unroll=4)


def sum_kernel(parts, _after, out):
    def step(i, carry):
        value = parts[0, i].astype(f32)
        for n in range(1, parts.shape[0]):
            value += parts[n, i].astype(f32)
        out[i] = value.astype(bf16)
        return carry

    lax.fori_loop(0, out.shape[0], step, 0, unroll=4)


def pair_kernel(info, parts, keep, send):
    my_zh = info[5]
    for out, zh in ((keep, my_zh), (send, 1 - my_zh)):
        for b in range(2):
            value = parts[0, 2 * zh + b].astype(f32)
            for n in range(1, parts.shape[0]):
                value += parts[n, 2 * zh + b].astype(f32)
            out[b] = value


def forward_kernel(info, code, hidden, w0, w1, w2, w3, _after, mine, theirs, weights, total, sems):
    my_core, my_x = info[2], info[3]
    copies = [
        pltpu.make_async_copy(part, weights.at[:, (my_x + NX - k) % NX], sems.at[k])
        for k, part in enumerate((w0, w1, w2, w3))
    ]
    for copy in copies:
        copy.start()
    total[...] = jnp.zeros_like(total)
    for copy in copies:
        copy.wait()

    def step(i, carry):
        adds = []
        for u in range(UNROLL):
            c = i * UNROLL + u
            word = code[c]
            lanes = pl.ds(pl.multiple_of(((word >> 8) & 15) * BS, BS), BS)
            w = weights[c].reshape(BS, BS)
            adds.append((word >> 12, jnp.dot(hidden[:, lanes], w, preferred_element_type=f32)))
        for col, value in adds:
            total[col] += value
        return carry

    lax.fori_loop(0, (info[0] + UNROLL - 1) // UNROLL, step, 0)
    for zl in range(NZL):
        for sub in range(4):
            mine[zl, sub] = total[(2 * zl + my_core) * 4 + sub]
            theirs[zl, sub] = total[(2 * zl + 1 - my_core) * 4 + sub]


def backward_kernel(info, code, cols, weights, back, total):
    total[...] = jnp.zeros_like(total)

    def step(i, carry):
        adds = []
        for u in range(UNROLL):
            c = i * UNROLL + u
            word = code[c]
            w = weights[c].reshape(BS, BS)
            value = lax.dot_general(cols[word >> 12], w, (((1,), (1,)), ((), ())), preferred_element_type=f32)
            adds.append(((word >> 8) & 15, value))
        for r, value in adds:
            total[r] += value
        return carry

    lax.fori_loop(0, (info[0] + UNROLL - 1) // UNROLL, step, 0)
    for r in range(total.shape[0]):
        back[:, r * BS : (r + 1) * BS] = total[r].astype(bf16)


def chip_kernel(info, mine, came, own, s1, s2, s3):
    my_zl = info[4]
    own[...] = mine[my_zl] + came[my_zl]
    for k, out in enumerate((s1, s2, s3)):
        zl = (my_zl + k + 1) % NZL
        out[...] = (mine[zl] + came[zl]).astype(bf16)


def project_kernel(own, r1, r2, r3, _after, out):
    for sub in range(4):
        value = own[sub] + r1[sub].astype(f32) + r2[sub].astype(f32) + r3[sub].astype(f32)
        out[:, sub * BS : (sub + 1) * BS] = value.astype(bf16)


def adam_kernel(place, stacked, came, _after, new_w, new_m, new_v, rows, grad):
    slots, share = new_w.shape
    places = came.shape[0] * PAIR
    width = stacked.shape[1] // BS
    for j in range(slots):
        word = jnp.maximum(place[j] - 1, 0)
        g, row = word % places, word // places
        filled = place[j] > 0
        here = row < slots
        entry = jnp.maximum(row - slots, 0)
        own = stacked[pl.ds(jnp.minimum(row, slots - 1), 1), :]
        for n in range(width):
            lanes = slice(n * BS, (n + 1) * BS)
            moved = came[entry // MV, pl.ds(2 * PAIR + width * (entry % MV) + n, 1), :]
            rows[j : j + 1, lanes] = jnp.where(filled, jnp.where(here, own[:, lanes], moved), 0.0)
        for b in range(2):
            value = came[g // PAIR, pl.ds(2 * (g % PAIR) + b, 1), :]
            grad[j : j + 1, b * BS : (b + 1) * BS] = jnp.where(filled, value, 0.0)
    w, m, v = adam_update(rows[:, :share], rows[:, share : 2 * share], rows[:, 2 * share :], grad[...])
    new_w[...] = w
    new_m[...] = m
    new_v[...] = v


def all_to_all(values, axis):
    return lax.all_to_all(values, axis, split_axis=0, concat_axis=0, tiled=True)


def shift(values, axis, count, step):
    return lax.ppermute(values, axis, [(i, (i + step) % count) for i in range(count)])


def shards(
    hidden,
    out_grad,
    block_weight,
    block_row,
    block_col,
    live_count,
    new_owner,
    new_slot,
    first_moment,
    second_moment,
):
    shard_count = lax.axis_size(SHARD)
    me = lax.axis_index(SHARD)
    dp_index = lax.axis_index(DP)
    x_index = lax.axis_index("x")
    tokens = hidden.shape[0]
    slot_count = block_weight.shape[1]
    row_local = hidden.shape[1] // BS
    share = first_moment.shape[2]
    scale = 1.0 / math.sqrt(tokens * lax.axis_size(DP))

    quarter = lax.dynamic_slice_in_dim(block_weight[0], x_index * (BS // NX), BS // NX, 1)
    quarter, sent = lax.optimization_barrier((quarter, out_grad))
    gathered = lax.all_gather(quarter, SHARD, axis=0, tiled=True)
    mine = all_to_all(call(repeat_kernel, like((NZL,) + out_grad.shape, bf16), 0, 1, byts=1024 * 1024)(sent), "zl")
    other = shift(mine, "core", 2, 1)
    weight_share = lax.dynamic_slice_in_dim(block_weight[0], dp_index * 2, 2, 1).reshape(slot_count, share)
    stacked = jnp.concatenate([weight_share.astype(f32), first_moment[0], second_moment[0]], axis=1)

    fits, code, counts, send, state_send, place = make_plan(
        block_row, block_col, live_count, new_owner, new_slot, row_local, me
    )
    info = jnp.stack(counts + [lax.axis_index("core"), x_index, lax.axis_index("zl"), lax.axis_index("zh")])

    partial, cols = call(
        grad_kernel,
        (like((NX, NY * NZH * 2, GCAP, BS), bf16), like((shard_count * 4, BS, BS), bf16)),
        2,
        3,
        [pltpu.VMEM((row_local, BS, BS), bf16), pltpu.VMEM((BS * GCAP, BS), f32)],
        flops=2 * WCAP * BS**3,
        byts=4 * 1024 * 1024,
    )(info, code, hidden, mine, other)
    along_x = all_to_all(partial, "x")
    summed = call(sum_kernel, like(partial.shape[1:], bf16), 0, 1, byts=2 * 1024 * 1024, n_after=1, limit=SMALL)(
        along_x, stacked
    )
    along_y = all_to_all(summed.reshape(NY, 2 * NZH, GCAP, BS), "y")
    half = like((2, GCAP, BS), f32)
    keep, send_zh = call(pair_kernel, (half, half), 1, 1, byts=1024 * 1024, limit=SMALL)(info, along_y)
    came_zh = shift(send_zh, "zh", NZH, 1)

    picked = call(select_kernel, like((WCAP, BS // NX, BS), bf16), 2, 1, byts=1024 * 1024, n_after=1)(
        info, code, gathered, summed
    )
    w2, w1, w3 = (shift(picked, "x", NX, k) for k in (2, 1, 3))
    packed = call(
        functools.partial(share_kernel, scale),
        like((shard_count, 2 * PAIR + MV * stacked.shape[1] // BS, BS), f32),
        2,
        3,
        [pltpu.VMEM((2, GCAP, BS), f32)],
        byts=1024 * 1024,
        n_after=2,
        limit=SMALL,
    )(send, state_send, keep, came_zh, stacked, place, fits)
    shares = all_to_all(packed, SHARD)

    out_mine, out_theirs, weights = call(
        forward_kernel,
        (
            like((NZL, 4, tokens, BS), f32),
            like((NZL, 4, tokens, BS), f32),
            like((WCAP, NX, BS // NX, BS), bf16),
        ),
        2,
        1,
        [pltpu.VMEM((shard_count * 4, tokens, BS), f32), pltpu.SemaphoreType.DMA((NX,))],
        flops=2 * WCAP * BS**3,
        byts=8 * 1024 * 1024,
        n_after=5,
    )(info, code, hidden, picked, w1, w2, w3, packed)
    came = shift(out_theirs, "core", 2, 1)
    hidden_grad = call(
        backward_kernel,
        like(hidden.shape, bf16),
        2,
        2,
        [pltpu.VMEM((row_local, tokens, BS), f32)],
        flops=2 * WCAP * BS**3,
        byts=4 * 1024 * 1024,
    )(info, code, cols, weights)
    part = (4, tokens, BS)
    own, s1, s2, s3 = call(
        chip_kernel, (like(part, f32),) + (like(part, bf16),) * 3, 1, 2, byts=3 * 1024 * 1024
    )(info, out_mine, came)
    r2, r1, r3 = (shift(s, "zl", NZL, k) for k, s in ((2, s2), (1, s1), (3, s3)))
    projected = call(project_kernel, like(out_grad.shape, bf16), 0, 4, byts=1024 * 1024, n_after=1)(
        own, r1, r2, r3, hidden_grad
    )

    shape = like((slot_count, share), f32)
    new_weight, new_first, new_second = call(
        adam_kernel,
        (shape, shape, shape),
        1,
        2,
        [pltpu.VMEM((slot_count, 3 * share), f32), pltpu.VMEM((slot_count, share), f32)],
        byts=1024 * 1024,
        n_after=1,
    )(place, stacked, shares, hidden_grad)
    result = (projected, hidden_grad, new_weight[None], new_first[None], new_second[None])
    return lax.cond(
        fits[0] > 0,
        lambda: result,
        lambda: general(
            hidden,
            out_grad,
            block_weight,
            block_row,
            block_col,
            live_count,
            new_owner,
            new_slot,
            first_moment,
            second_moment,
        ),
    )


def solution(mesh):
    split = Mesh(mesh.devices.reshape(NY, NX, NZH, NZL, 2), ("y", "x", "zh", "zl", "core"))
    in_specs = (
        P(DP, SHARD),
        P(DP, SHARD),
        P(SHARD, None, None, None),
        P(),
        P(),
        P(),
        P(),
        P(),
        P(SHARD, None, DP),
        P(SHARD, None, DP),
    )
    out_specs = (
        P(DP, SHARD),
        P(DP, SHARD),
        P(SHARD, None, DP),
        P(SHARD, None, DP),
        P(SHARD, None, DP),
    )
    return jax.shard_map(shards, mesh=split, in_specs=in_specs, out_specs=out_specs, check_vma=False)
```

```python
import functools
import math

import jax
import jax.numpy as jnp
from jax import lax
from jax.experimental import pallas as pl
from jax.experimental.pallas import tpu as pltpu
from jax.sharding import Mesh, PartitionSpec as P

DP = ("y", "x", "zh")
SHARD = ("zl", "core")
MV = 2


LEARN_RATE = 0.01
BETA_ONE = 0.9
BETA_TWO = 0.95
EPSILON = 1e-08


def adam_update(weight, first_state, second_state, gradient):
    first_state = BETA_ONE * first_state + (1.0 - BETA_ONE) * gradient
    second_state = BETA_TWO * second_state + (1.0 - BETA_TWO) * gradient * gradient
    weight = weight - LEARN_RATE * first_state / (jnp.sqrt(second_state) + EPSILON)
    return (weight, first_state, second_state)


def send_positions(owner_devices, shard_count, slot_count):
    sources = jnp.arange(shard_count, dtype=jnp.int32)[:, None]
    moving = (owner_devices >= 0) & (owner_devices != sources)
    slot_ids = jnp.arange(slot_count)
    earlier = slot_ids[None, :] < slot_ids[:, None]
    matches = (
        (owner_devices[:, :, None] == owner_devices[:, None, :])
        & moving[:, None, :]
        & earlier[None, :, :]
    )
    return (moving, jnp.sum(matches, axis=2))


def pack_moving(values, owner_row, moving_row, position_row, shard_count, capacity):
    slot_ids = jnp.arange(values.shape[0], dtype=jnp.int32)
    targets = owner_row * capacity + position_row
    entries = jnp.arange(shard_count * capacity, dtype=jnp.int32)
    matches = (targets[None, :] == entries[:, None]) & moving_row[None, :]
    source = jnp.sum(jnp.where(matches, slot_ids[None, :], 0), axis=1)
    filled = jnp.any(matches, axis=1)
    packed = jnp.where(filled[:, None], jnp.take(values, source, axis=0), 0.0)
    return packed.reshape(shard_count, capacity, values.shape[1])


def place_blocks(
    received,
    own_values,
    owner_devices,
    destination_slot_list,
    moving,
    positions,
    my_index,
    capacity,
):
    shard_count, slot_count = owner_devices.shape
    slot_ids = jnp.arange(slot_count, dtype=jnp.int32)
    entries = (jnp.arange(shard_count, dtype=jnp.int32)[:, None] * capacity + positions).reshape(-1)
    to_me = (moving & (owner_devices == my_index)).reshape(-1)
    matches = to_me[None, :] & (destination_slot_list.reshape(-1)[None, :] == slot_ids[:, None])
    arrived = jnp.any(matches, axis=1)
    from_entry = jnp.sum(jnp.where(matches, entries[None, :], 0), axis=1)
    flattened = received.reshape(shard_count * capacity, received.shape[2])
    arrival_rows = jnp.take(flattened, from_entry, axis=0)
    stay_hit = (owner_devices[my_index] == my_index)[None, :] & (
        destination_slot_list[my_index][None, :] == slot_ids[:, None]
    )
    stayed = jnp.any(stay_hit, axis=1)
    from_slot = jnp.sum(jnp.where(stay_hit, slot_ids[None, :], 0), axis=1)
    kept_rows = jnp.take(own_values, from_slot, axis=0)
    return jnp.where(arrived[:, None], arrival_rows, jnp.where(stayed[:, None], kept_rows, 0.0))


def local_place(block_ids, first_id, local_count):
    local_ids = block_ids - first_id
    inside = (local_ids >= 0) & (local_ids < local_count)
    return jnp.where(inside, local_ids, local_count)


def general(
    hidden,
    out_grad,
    block_weight,
    block_row,
    block_col,
    live_count,
    new_owner,
    new_slot,
    first_moment,
    second_moment,
):
    shard_count = lax.axis_size(SHARD)
    dp_count = lax.axis_size(DP)
    my_index = lax.axis_index(SHARD)
    dp_index = lax.axis_index(DP)
    tokens_dev = hidden.shape[0]
    slot_count = block_weight.shape[1]
    block_size = block_weight.shape[2]
    share_size = first_moment.shape[2]
    row_blocks = hidden.shape[1] * shard_count // block_size
    col_blocks = out_grad.shape[1] * shard_count // block_size
    grad_scale = 1.0 / math.sqrt(tokens_dev * dp_count)
    slot_ids = jnp.arange(slot_count)
    live_all = slot_ids[None, :] < live_count[:, None]
    my_live = live_all[my_index]
    my_rows = block_row[my_index]
    my_cols = block_col[my_index]
    zero_bf = jnp.zeros((), jnp.bfloat16)
    full_hidden, full_grad = (
        lax.all_gather(hidden, SHARD, axis=1, tiled=True),
        lax.all_gather(out_grad, SHARD, axis=1, tiled=True),
    )
    hidden_blocks = full_hidden.reshape(tokens_dev, row_blocks, block_size)
    grad_blocks = full_grad.reshape(tokens_dev, col_blocks, block_size)
    own_hidden = jnp.take(hidden_blocks, my_rows, axis=1)
    own_grad = jnp.take(grad_blocks, my_cols, axis=1)
    grad_share = None
    col_local = col_blocks // shard_count
    row_local = row_blocks // shard_count

    def one_shard(totals, member):
        blocks, shard_index = member
        row_ids = block_row[shard_index]
        col_ids = block_col[shard_index]
        weights = jnp.where(live_all[shard_index][:, None, None], blocks, zero_bf)
        hidden_part = jnp.take(hidden_blocks, row_ids, axis=1)
        grad_part = jnp.take(grad_blocks, col_ids, axis=1)
        forward = jnp.einsum(
            "tkr,krc->tkc", hidden_part, weights, preferred_element_type=jnp.float32
        )
        backward = jnp.einsum(
            "tkc,krc->tkr", grad_part, weights, preferred_element_type=jnp.float32
        )
        col_place = local_place(col_ids, my_index * col_local, col_local)
        row_place = local_place(row_ids, my_index * row_local, row_local)
        out_total = totals[0].at[:, col_place].add(forward, mode="drop")
        back_total = totals[1].at[:, row_place].add(backward, mode="drop")
        return ((out_total, back_total), None)

    initial = (
        jnp.zeros((tokens_dev, col_local, block_size), jnp.float32),
        jnp.zeros((tokens_dev, row_local, block_size), jnp.float32),
    )
    totals = initial
    blocks_in = lax.all_gather(block_weight, SHARD, axis=0, tiled=True)
    indices = jnp.arange(blocks_in.shape[0], dtype=jnp.int32)
    totals, unused = lax.scan(one_shard, totals, (blocks_in, indices))
    out_total, back_total = totals
    projected = out_total.reshape(tokens_dev, col_local * block_size).astype(jnp.bfloat16)
    hidden_grad = back_total.reshape(tokens_dev, row_local * block_size).astype(jnp.bfloat16)
    blocks = (
        jnp.einsum("tkr,tkc->krc", own_hidden, own_grad, preferred_element_type=jnp.float32)
        * grad_scale
    )
    blocks = jnp.where(my_live[:, None, None], blocks, 0.0)
    grad_share = lax.psum_scatter(
        blocks.reshape(slot_count, block_size * block_size), DP, scatter_dimension=1, tiled=True
    )
    moving, positions = send_positions(new_owner, shard_count, slot_count)
    my_owner = new_owner[my_index]
    my_moving = moving[my_index]
    my_positions = positions[my_index]
    flat_weight = block_weight[0].reshape(slot_count, block_size * block_size)
    weight_share = lax.dynamic_slice_in_dim(
        flat_weight, dp_index * share_size, share_size, 1
    ).astype(jnp.float32)
    updated, first_state, second_state = adam_update(
        weight_share, first_moment[0], second_moment[0], grad_share
    )
    stacked = jnp.concatenate([updated, first_state, second_state], axis=1)
    packed = pack_moving(stacked, my_owner, my_moving, my_positions, shard_count, MV)
    received = lax.all_to_all(packed, SHARD, split_axis=0, concat_axis=0, tiled=True)
    placed = place_blocks(received, stacked, new_owner, new_slot, moving, positions, my_index, MV)
    new_weight = placed[:, :share_size]
    new_first = placed[:, share_size : 2 * share_size]
    new_second = placed[:, 2 * share_size :]
    return (projected, hidden_grad, new_weight[None], new_first[None], new_second[None])


WCAP = 44
GCAP = 40
PAIR = 14
UNROLL = 4
NX, NY, NZH, NZL = 4, 8, 2, 4
BS = 128
VMEM_LIMIT = 8 * 1024 * 1024
SMALL = 3 * 1024 * 1024
f32 = jnp.float32
bf16 = jnp.bfloat16
i32 = jnp.int32


def call(kernel, outs, n_smem, n_vmem, scratch=(), flops=0, byts=0, n_after=0, limit=VMEM_LIMIT):
    smem = pl.BlockSpec(memory_space=pltpu.SMEM)
    vmem = pl.BlockSpec(memory_space=pltpu.VMEM)
    anywhere = pl.BlockSpec(memory_space=pl.ANY)
    return pl.pallas_call(
        kernel,
        out_shape=outs,
        in_specs=[smem] * n_smem + [vmem] * n_vmem + [anywhere] * n_after,
        out_specs=jax.tree.map(lambda _: vmem, outs),
        scratch_shapes=list(scratch),
        compiler_params=pltpu.CompilerParams(vmem_limit_bytes=limit),
        cost_estimate=pl.CostEstimate(flops=flops, bytes_accessed=byts, transcendentals=0),
    )


def like(shape, dtype):
    return jax.ShapeDtypeStruct(shape, dtype)


def make_plan(block_row, block_col, live_count, new_owner, new_slot, row_local, me):
    shard_count, slot_count = block_row.shape
    total = shard_count * slot_count
    ids = jnp.arange(total, dtype=i32)
    live = (jnp.arange(slot_count)[None, :] < live_count[:, None]).reshape(total)
    row = block_row.reshape(total)
    col = block_col.reshape(total)
    owner = jnp.where(live, new_owner.reshape(total), -1)
    slot = new_slot.reshape(total)
    kept = owner >= 0
    row_shard = row // row_local
    key = jnp.where(kept, ids, ids + total)
    same = row_shard[:, None] == row_shard[None, :]
    before = same & live[None, :] & (key[None, :] < key[:, None])
    rank = jnp.sum(before.astype(i32), axis=1)
    earlier = same & (owner[:, None] == owner[None, :]) & (ids[None, :] < ids[:, None])
    pos = jnp.sum(earlier.astype(i32), axis=1)
    fits = (
        (jnp.max(jnp.where(live, rank, 0)) < WCAP)
        & (jnp.max(jnp.where(kept, rank, 0)) < GCAP)
        & (jnp.max(jnp.where(kept, pos, 0)) < PAIR)
    )

    here = live & (row_shard == me)
    words = ids + 256 * ((row - row_local * me) + 16 * col)
    hit = here[None, :] & (rank[None, :] == jnp.arange(WCAP)[:, None])
    code = jnp.sum(jnp.where(hit, words[None, :], 0), axis=1)
    counts = [jnp.minimum(jnp.sum(here.astype(i32)), WCAP), jnp.minimum(jnp.sum((here & kept).astype(i32)), GCAP)]
    going = jnp.where(here & kept, owner * PAIR + pos, -1)
    send_hit = going[None, :] == jnp.arange(shard_count * PAIR)[:, None]
    send = jnp.minimum(jnp.sum(jnp.where(send_hit, rank[None, :], 0), axis=1), GCAP - 1)
    owner2 = owner.reshape(shard_count, slot_count)
    sources = jnp.arange(shard_count, dtype=i32)[:, None]
    slots = jnp.arange(slot_count, dtype=i32)[None, :]
    moving, positions = send_positions(owner2, shard_count, slot_count)
    target = jnp.where(moving & (sources == me), owner2 * MV + positions, -1).reshape(total)
    state_hit = target[None, :] == jnp.arange(shard_count * MV)[:, None]
    state_send = jnp.sum(jnp.where(state_hit, (ids % slot_count)[None, :], 0), axis=1)
    state_row = jnp.where(sources == me, slots, slot_count + sources * MV + positions).reshape(total)
    landing = 1 + row_shard * PAIR + jnp.minimum(pos, PAIR - 1) + shard_count * PAIR * state_row
    lands = (owner == me)[None, :] & (slot[None, :] == jnp.arange(slot_count)[:, None])
    place = jnp.sum(jnp.where(lands, landing[None, :], 0), axis=1)
    return fits.astype(i32).reshape(1), code, counts, send, state_send, place


def repeat_kernel(value, out):
    for n in range(out.shape[0]):
        out[n] = value[...]


def grad_kernel(info, code, hidden, mine, other, out, cols, hidden_t, total):
    my_core = info[2]
    for zl in range(NZL):
        for sub in range(4):
            lanes = slice(sub * BS, (sub + 1) * BS)
            cols[(2 * zl + my_core) * 4 + sub] = mine[zl, :, lanes]
            cols[(2 * zl + 1 - my_core) * 4 + sub] = other[zl, :, lanes]
    row_local = hidden.shape[1] // BS
    for r in range(row_local):
        hidden_t[r] = hidden[:, r * BS : (r + 1) * BS].T

    def step(i, carry):
        blocks = []
        for u in range(UNROLL):
            word = code[i * UNROLL + u]
            blocks.append(jnp.dot(hidden_t[(word >> 8) & 15], cols[word >> 12], preferred_element_type=f32))
        for u in range(UNROLL):
            total[pl.ds(i * UNROLL + u, BS, stride=GCAP), :] = blocks[u]
        return carry

    lax.fori_loop(0, (info[1] + UNROLL - 1) // UNROLL, step, 0)
    for x in range(NX):
        for y in range(NY):
            for q in range(4):
                source = 16 * y + 4 * x + q
                out[x, 4 * y + q] = total[source * GCAP : (source + 1) * GCAP, :].astype(bf16)


def share_kernel(scale, send, state_send, keep, came, stacked, _after, _after2, out, total):
    total[...] = (keep[...] + came[...]) * scale
    width = stacked.shape[1] // BS
    for d in range(out.shape[0]):
        for p in range(PAIR):
            rank = send[d * PAIR + p]
            for b in range(2):
                out[d, 2 * p + b : 2 * p + b + 1, :] = total[b, pl.ds(rank, 1), :]
        for p in range(MV):
            row = stacked[pl.ds(state_send[d * MV + p], 1), :]
            for n in range(width):
                at = 2 * PAIR + width * p + n
                out[d, at : at + 1, :] = row[:, n * BS : (n + 1) * BS]


def select_kernel(info, code, gathered, _after, picked):
    def select(c, carry):
        value = gathered[code[c] & 255]
        picked[c] = jnp.where(c < info[0], value, jnp.zeros_like(value))
        return carry

    lax.fori_loop(0, WCAP, select, 0, unroll=4)


def sum_kernel(parts, _after, _after2, out):
    def step(i, carry):
        value = parts[0, i].astype(f32)
        for n in range(1, parts.shape[0]):
            value += parts[n, i].astype(f32)
        out[i] = value.astype(bf16)
        return carry

    lax.fori_loop(0, out.shape[0], step, 0, unroll=4)


def pair_kernel(info, parts, keep, send):
    my_zh = info[5]
    for out, zh in ((keep, my_zh), (send, 1 - my_zh)):
        for b in range(2):
            value = parts[0, 2 * zh + b].astype(f32)
            for n in range(1, parts.shape[0]):
                value += parts[n, 2 * zh + b].astype(f32)
            out[b] = value


def forward_kernel(info, code, hidden, w0, w1, w2, w3, _after, mine, theirs, weights, total, sems):
    my_core, my_x = info[2], info[3]
    copies = [
        pltpu.make_async_copy(part, weights.at[:, (my_x + NX - k) % NX], sems.at[k])
        for k, part in enumerate((w0, w1, w2, w3))
    ]
    for copy in copies:
        copy.start()
    total[...] = jnp.zeros_like(total)
    for copy in copies:
        copy.wait()

    def step(i, carry):
        adds = []
        for u in range(UNROLL):
            c = i * UNROLL + u
            word = code[c]
            lanes = pl.ds(pl.multiple_of(((word >> 8) & 15) * BS, BS), BS)
            w = weights[c].reshape(BS, BS)
            adds.append((word >> 12, jnp.dot(hidden[:, lanes], w, preferred_element_type=f32)))
        for col, value in adds:
            total[col] += value
        return carry

    lax.fori_loop(0, (info[0] + UNROLL - 1) // UNROLL, step, 0)
    for zl in range(NZL):
        for sub in range(4):
            mine[zl, sub] = total[(2 * zl + my_core) * 4 + sub]
            theirs[zl, sub] = total[(2 * zl + 1 - my_core) * 4 + sub]


def backward_kernel(info, code, cols, weights, back, total):
    total[...] = jnp.zeros_like(total)

    def step(i, carry):
        adds = []
        for u in range(UNROLL):
            c = i * UNROLL + u
            word = code[c]
            w = weights[c].reshape(BS, BS)
            value = lax.dot_general(cols[word >> 12], w, (((1,), (1,)), ((), ())), preferred_element_type=f32)
            adds.append(((word >> 8) & 15, value))
        for r, value in adds:
            total[r] += value
        return carry

    lax.fori_loop(0, (info[0] + UNROLL - 1) // UNROLL, step, 0)
    for r in range(total.shape[0]):
        back[:, r * BS : (r + 1) * BS] = total[r].astype(bf16)


def chip_kernel(info, mine, came, own, s1, s2, s3):
    my_zl = info[4]
    own[...] = mine[my_zl] + came[my_zl]
    for k, out in enumerate((s1, s2, s3)):
        zl = (my_zl + k + 1) % NZL
        out[...] = (mine[zl] + came[zl]).astype(bf16)


def project_kernel(own, r1, r2, r3, _after, out):
    for sub in range(4):
        value = own[sub] + r1[sub].astype(f32) + r2[sub].astype(f32) + r3[sub].astype(f32)
        out[:, sub * BS : (sub + 1) * BS] = value.astype(bf16)


def adam_kernel(place, stacked, came, _after, new_w, new_m, new_v, rows, grad):
    slots, share = new_w.shape
    places = came.shape[0] * PAIR
    width = stacked.shape[1] // BS
    for j in range(slots):
        word = jnp.maximum(place[j] - 1, 0)
        g, row = word % places, word // places
        filled = place[j] > 0
        here = row < slots
        entry = jnp.maximum(row - slots, 0)
        own = stacked[pl.ds(jnp.minimum(row, slots - 1), 1), :]
        for n in range(width):
            lanes = slice(n * BS, (n + 1) * BS)
            moved = came[entry // MV, pl.ds(2 * PAIR + width * (entry % MV) + n, 1), :]
            rows[j : j + 1, lanes] = jnp.where(filled, jnp.where(here, own[:, lanes], moved), 0.0)
        for b in range(2):
            value = came[g // PAIR, pl.ds(2 * (g % PAIR) + b, 1), :]
            grad[j : j + 1, b * BS : (b + 1) * BS] = jnp.where(filled, value, 0.0)
    w, m, v = adam_update(rows[:, :share], rows[:, share : 2 * share], rows[:, 2 * share :], grad[...])
    new_w[...] = w
    new_m[...] = m
    new_v[...] = v


def all_to_all(values, axis):
    return lax.all_to_all(values, axis, split_axis=0, concat_axis=0, tiled=True)


def shift(values, axis, count, step):
    return lax.ppermute(values, axis, [(i, (i + step) % count) for i in range(count)])


def shards(
    hidden,
    out_grad,
    block_weight,
    block_row,
    block_col,
    live_count,
    new_owner,
    new_slot,
    first_moment,
    second_moment,
):
    shard_count = lax.axis_size(SHARD)
    me = lax.axis_index(SHARD)
    dp_index = lax.axis_index(DP)
    x_index = lax.axis_index("x")
    tokens = hidden.shape[0]
    slot_count = block_weight.shape[1]
    row_local = hidden.shape[1] // BS
    share = first_moment.shape[2]
    scale = 1.0 / math.sqrt(tokens * lax.axis_size(DP))

    quarter = lax.dynamic_slice_in_dim(block_weight[0], x_index * (BS // NX), BS // NX, 1)
    quarter, sent = lax.optimization_barrier((quarter, out_grad))
    gathered = lax.all_gather(quarter, SHARD, axis=0, tiled=True)
    mine = all_to_all(call(repeat_kernel, like((NZL,) + out_grad.shape, bf16), 0, 1, byts=1024 * 1024)(sent), "zl")
    other = shift(mine, "core", 2, 1)
    weight_share = lax.dynamic_slice_in_dim(block_weight[0], dp_index * 2, 2, 1).reshape(slot_count, share)
    stacked = jnp.concatenate([weight_share.astype(f32), first_moment[0], second_moment[0]], axis=1)

    fits, code, counts, send, state_send, place = make_plan(
        block_row, block_col, live_count, new_owner, new_slot, row_local, me
    )
    info = jnp.stack(counts + [lax.axis_index("core"), x_index, lax.axis_index("zl"), lax.axis_index("zh")])

    partial, cols = call(
        grad_kernel,
        (like((NX, NY * NZH * 2, GCAP, BS), bf16), like((shard_count * 4, BS, BS), bf16)),
        2,
        3,
        [pltpu.VMEM((row_local, BS, BS), bf16), pltpu.VMEM((BS * GCAP, BS), f32)],
        flops=2 * WCAP * BS**3,
        byts=4 * 1024 * 1024,
    )(info, code, hidden, mine, other)
    along_x = all_to_all(partial, "x")
    picked = call(select_kernel, like((WCAP, BS // NX, BS), bf16), 2, 1, byts=1024 * 1024, n_after=1)(
        info, code, gathered, partial
    )
    summed = call(sum_kernel, like(partial.shape[1:], bf16), 0, 1, byts=2 * 1024 * 1024, n_after=2, limit=SMALL)(
        along_x, stacked, picked
    )
    along_y = all_to_all(summed.reshape(NY, 2 * NZH, GCAP, BS), "y")
    half = like((2, GCAP, BS), f32)
    keep, send_zh = call(pair_kernel, (half, half), 1, 1, byts=1024 * 1024, limit=SMALL)(info, along_y)
    came_zh = shift(send_zh, "zh", NZH, 1)

    ready, _ = lax.optimization_barrier((picked, summed))
    w2, w1, w3 = (shift(ready, "x", NX, k) for k in (2, 1, 3))
    packed = call(
        functools.partial(share_kernel, scale),
        like((shard_count, 2 * PAIR + MV * stacked.shape[1] // BS, BS), f32),
        2,
        3,
        [pltpu.VMEM((2, GCAP, BS), f32)],
        byts=1024 * 1024,
        n_after=2,
        limit=SMALL,
    )(send, state_send, keep, came_zh, stacked, place, fits)
    shares = all_to_all(packed, SHARD)

    out_mine, out_theirs, weights = call(
        forward_kernel,
        (
            like((NZL, 4, tokens, BS), f32),
            like((NZL, 4, tokens, BS), f32),
            like((WCAP, NX, BS // NX, BS), bf16),
        ),
        2,
        1,
        [pltpu.VMEM((shard_count * 4, tokens, BS), f32), pltpu.SemaphoreType.DMA((NX,))],
        flops=2 * WCAP * BS**3,
        byts=8 * 1024 * 1024,
        n_after=5,
    )(info, code, hidden, picked, w1, w2, w3, packed)
    came = shift(out_theirs, "core", 2, 1)
    hidden_grad = call(
        backward_kernel,
        like(hidden.shape, bf16),
        2,
        2,
        [pltpu.VMEM((row_local, tokens, BS), f32)],
        flops=2 * WCAP * BS**3,
        byts=4 * 1024 * 1024,
    )(info, code, cols, weights)
    part = (4, tokens, BS)
    own, s1, s2, s3 = call(
        chip_kernel, (like(part, f32),) + (like(part, bf16),) * 3, 1, 2, byts=3 * 1024 * 1024
    )(info, out_mine, came)
    r2, r1, r3 = (shift(s, "zl", NZL, k) for k, s in ((2, s2), (1, s1), (3, s3)))
    projected = call(project_kernel, like(out_grad.shape, bf16), 0, 4, byts=1024 * 1024, n_after=1)(
        own, r1, r2, r3, hidden_grad
    )

    shape = like((slot_count, share), f32)
    new_weight, new_first, new_second = call(
        adam_kernel,
        (shape, shape, shape),
        1,
        2,
        [pltpu.VMEM((slot_count, 3 * share), f32), pltpu.VMEM((slot_count, share), f32)],
        byts=1024 * 1024,
        n_after=1,
    )(place, stacked, shares, hidden_grad)
    result = (projected, hidden_grad, new_weight[None], new_first[None], new_second[None])
    return lax.cond(
        fits[0] > 0,
        lambda: result,
        lambda: general(
            hidden,
            out_grad,
            block_weight,
            block_row,
            block_col,
            live_count,
            new_owner,
            new_slot,
            first_moment,
            second_moment,
        ),
    )


def solution(mesh):
    split = Mesh(mesh.devices.reshape(NY, NX, NZH, NZL, 2), ("y", "x", "zh", "zl", "core"))
    in_specs = (
        P(DP, SHARD),
        P(DP, SHARD),
        P(SHARD, None, None, None),
        P(),
        P(),
        P(),
        P(),
        P(),
        P(SHARD, None, DP),
        P(SHARD, None, DP),
    )
    out_specs = (
        P(DP, SHARD),
        P(DP, SHARD),
        P(SHARD, None, DP),
        P(SHARD, None, DP),
        P(SHARD, None, DP),
    )
    return jax.shard_map(shards, mesh=split, in_specs=in_specs, out_specs=out_specs, check_vma=False)
```
